32 devices in a mesh: dp: 4 (over z), tensor: 4 (over y, core), section: 2 (over x).
Axes of the slice: x: 2, y: 2, z: 4, core: 2. Of those that a mesh axis runs over, the one named last changes fastest.
Arguments:
- section_inputs: bfloat16 [2, 8, 256, 1152], P('section', 'dp', 'tensor'), may hold values from -6 to 6
- condition: float32 [8, 1152], P('dp'), may hold values from -6 to 6
- timesteps: int32 [8], P('dp'), may hold values from 0 to 999
- ada_weight: bfloat16 [2, 1152, 6912], P('section', 'dp', 'tensor'), may hold values from -0.1875 to 0.1875
- ada_bias: bfloat16 [2, 6912], P('section', 'tensor'), may hold values from -3 to 3
- in_weight: bfloat16 [2, 4, 1152, 1152], P('section', None, 'dp', 'tensor'), may hold values from -0.1875 to 0.1875
- gate_weight: bfloat16 [2, 1152, 16], P('section', 'dp', 'tensor'), may hold values from -0.1875 to 0.1875
- gate_bias: bfloat16 [2, 16], P('section', 'tensor'), may hold values from -6 to 1
- conv_taps: bfloat16 [2, 9, 1152], P('section', None, 'tensor'), may hold values from -1.5 to 1.5
- out_weight: bfloat16 [2, 1152, 1152], P('section', 'tensor', 'dp'), may hold values from -0.1875 to 0.1875
- up_weight: bfloat16 [2, 1152, 4608], P('section', 'dp', 'tensor'), may hold values from -0.1875 to 0.1875
- up_bias: bfloat16 [2, 4608], P('section', 'tensor'), may hold values from -3 to 3
- down_weight: bfloat16 [2, 4608, 1152], P('section', 'tensor', 'dp'), may hold values from -0.09375 to 0.09375
Outputs:
- section_ends: bfloat16 [2, 8, 256, 1152], P('section', 'dp', 'tensor')
- cond_grad: float32 [8, 1152], P('dp')
- grad_ada_weight: float32 [2, 1152, 6912], P('section', 'dp', 'tensor')
- grad_ada_bias: float32 [2, 6912], P('section', 'tensor')
- grad_in_weight: float32 [2, 4, 1152, 1152], P('section', None, 'dp', 'tensor')
- grad_gate_weight: float32 [2, 1152, 16], P('section', 'dp', 'tensor')
- grad_gate_bias: float32 [2, 16], P('section', 'tensor')
- grad_conv_taps: float32 [2, 9, 1152], P('section', None, 'tensor')
- grad_out_weight: float32 [2, 1152, 1152], P('section', 'tensor', 'dp')
- grad_up_weight: float32 [2, 1152, 4608], P('section', 'dp', 'tensor')
- grad_up_bias: float32 [2, 4608], P('section', 'tensor')
- grad_down_weight: float32 [2, 4608, 1152], P('section', 'tensor', 'dp')
The draws below stay inside these ranges and needn't reach their ends.
All inputs are finite; a program needn't handle non-finite values.
Results may differ from the reference program's by a relative error of at most 0.03.
Values may be sent and summed in bfloat16 or wider, within the bound.
No kernel may reach another device: no remote copies, remote signals or barrier semaphores. Data moves between devices by JAX's collectives and lax.ppermute only.
A program may use at most 128 MiB of HBM per device.

```python
import math
import jax
import jax.numpy as jnp
from jax import lax

D = 1152
H = 16
FF = 4608
SIDE = 16
STEPS_T = 1000
PATCHES = 256
IMAGES = 8


def touch_ends(values, own_key, least, largest):
    longest = values.shape.index(max(values.shape))
    spots = []
    for shift in (0, 1):
        where = [jax.random.randint(jax.random.fold_in(own_key, axis), (), 0, length) for axis, length in enumerate(values.shape)]
        where[longest] = (where[longest] + shift) % values.shape[longest]
        spots.append(tuple(where))
    return values.at[spots[0]].set(least).at[spots[1]].set(largest)


def block_levels(own_key, dims, cuts, smallest, high):
    level, own = 1.0, jax.random.fold_in(own_key, 6)
    for axis_at, blocks in cuts:
        draws = jnp.exp(jax.random.uniform(jax.random.fold_in(own, axis_at), (blocks,), jnp.float32, smallest / len(cuts), high / len(cuts)))
        level = level * jnp.repeat(draws, dims[axis_at] // blocks).reshape([-1 if axis == axis_at else 1 for axis in range(len(dims))])
    return level


def scatter_about(own_key, dims, scale, bound, cuts=(), kind=jnp.bfloat16):
    drawn = scale * jax.random.normal(own_key, dims, jnp.float32)
    if cuts:
        drawn = drawn * block_levels(own_key, dims, cuts, -0.22, 0.18)
    return jnp.clip(drawn, -bound, bound).astype(kind)


def setup_inputs(seed: int = 0) -> dict:
    streams_of = jax.random.split(jax.random.key(seed), 14)
    section_inputs = scatter_about(streams_of[0], (2, IMAGES, PATCHES, D), 1.0, 6.0, ((0, 2), (1, 4), (2, 4)))
    condition = scatter_about(streams_of[1], (IMAGES, D), 1.0, 6.0, ((0, 4),), jnp.float32)
    timesteps = touch_ends(jax.random.randint(streams_of[2], (IMAGES,), 0, STEPS_T), jax.random.fold_in(streams_of[2], 1), 0, STEPS_T - 1).astype(jnp.int32)
    ada_weight = scatter_about(streams_of[3], (2, D, 6 * D), D ** -0.5, 0.1875, ((0, 2), (1, 4), (2, 4)))
    ada_bias = scatter_about(streams_of[4], (2, 6 * D), 0.5, 3.0, ((0, 2), (1, 4)))
    in_weight = scatter_about(streams_of[5], (2, 4, D, D), D ** -0.5, 0.1875, ((0, 2), (2, 4), (3, 4)))
    gate_weight = scatter_about(streams_of[6], (2, D, H), D ** -0.5, 0.1875, ((0, 2), (1, 4), (2, 4)))
    gate_bias = jnp.clip(-6.0 + 7.0 * jax.random.uniform(streams_of[7], (2, H), jnp.float32) ** block_levels(streams_of[7], (2, H), ((0, 2), (1, 4)), -0.2, 0.2), -6.0, 1.0).astype(jnp.bfloat16)
    conv_taps = scatter_about(streams_of[8], (2, 9, D), 0.3, 1.5, ((0, 2), (2, 4)))
    out_weight = scatter_about(streams_of[9], (2, D, D), D ** -0.5, 0.1875, ((0, 2), (1, 4), (2, 4)))
    up_weight = scatter_about(streams_of[10], (2, D, FF), D ** -0.5, 0.1875, ((0, 2), (1, 4), (2, 4)))
    up_bias = scatter_about(streams_of[11], (2, FF), 0.5, 3.0, ((0, 2), (1, 4)))
    down_weight = scatter_about(streams_of[12], (2, FF, D), FF ** -0.5, 0.09375, ((0, 2), (1, 4), (2, 4)))
    return dict(section_inputs=section_inputs, condition=condition, timesteps=timesteps, ada_weight=ada_weight, ada_bias=ada_bias, in_weight=in_weight, gate_weight=gate_weight, gate_bias=gate_bias, conv_taps=conv_taps, out_weight=out_weight, up_weight=up_weight, up_bias=up_bias, down_weight=down_weight)


@jax.custom_vjp
def low(v):
    return lax.optimization_barrier(v.astype(jnp.bfloat16)).astype(jnp.float32)

@jax.custom_vjp
def low_back(v):
    return v

def low_keep(v):
    return (low(v), None)

def low_pass(kept, grad):
    return (grad,)

def back_keep(v):
    return (v, None)

def back_low(kept, grad):
    return (low(grad),)
low.defvjp(low_keep, low_pass)
low_back.defvjp(back_keep, back_low)
HIGHEST = lax.Precision.HIGHEST

def sinusoid(time_steps, channels):
    half_width = channels // 2
    frequency = jnp.exp(jnp.arange(half_width, dtype=jnp.float32) * (-math.log(10000.0) / half_width))
    angles = time_steps.astype(jnp.float32)[:, None] * frequency[None, :]
    return jnp.concatenate([jnp.cos(angles), jnp.sin(angles)], axis=1)

def layer_norm(values):
    row_mean = lax.optimization_barrier(jnp.mean(values, axis=-1, keepdims=True))
    centered = values - row_mean
    variance = lax.optimization_barrier(jnp.mean(centered * centered, axis=-1, keepdims=True))
    return centered * lax.rsqrt(variance + 1e-06)

def reorient(values, flip, side):
    lead_shape = values.shape[:-2]
    channels = values.shape[-1]
    grid_view = values.reshape(lead_shape + (side, side, channels))
    turned = jnp.swapaxes(grid_view, -3, -2).reshape(values.shape)
    return jnp.where(flip, turned, values)

def middle(projected, logits, taps, flip, side):
    length = projected.shape[1]
    channels = projected.shape[2]
    head_count = logits.shape[1]
    head_width = channels // head_count
    scan_proj = reorient(projected[:3], flip, side)
    scan_logit = reorient(logits, flip, side)
    split_parts = scan_proj.reshape(3, length, head_count, head_width).transpose(0, 2, 1, 3)
    queries = split_parts[0] * head_width ** (-0.5)
    key_rows = split_parts[1]
    value_rows = split_parts[2]
    decay_rates = -jax.nn.softplus(scan_logit)
    totals = jnp.cumsum(decay_rates, axis=0).T
    positions = jnp.arange(length)
    causal = positions[:, None] >= positions[None, :]
    log_spans = jnp.where(causal[None], totals[:, :, None] - totals[:, None, :], -1e+30)
    decays = jnp.exp(log_spans)
    scores = jnp.einsum('htc,hsc->hts', queries, key_rows, precision=HIGHEST) * decays
    mixed_out = jnp.einsum('hts,hsc->htc', scores, value_rows, precision=HIGHEST)
    decay_mass = lax.optimization_barrier(jnp.sum(decays, axis=2))
    normed = mixed_out * lax.rsqrt(decay_mass)[:, :, None]
    flat_out = reorient(normed.transpose(1, 0, 2).reshape(length, channels), flip, side)
    grid_out = flat_out.reshape(side, side, channels)
    padded = jnp.pad(grid_out, ((1, 1), (1, 1), (0, 0)))
    spread = grid_out
    for tap_row in range(3):
        for tap_col in range(3):
            spread = spread + padded[tap_row:tap_row + side, tap_col:tap_col + side] * taps[3 * tap_row + tap_col]
    return spread.reshape(length, channels) * jax.nn.silu(projected[3])

def block(block_in, cond_row, params, flip):
    ada_weight, ada_bias, in_weight, gate_weight, gate_bias, conv_taps, out_weight, up_weight, up_bias, down_weight = params
    activated = low(jax.nn.silu(cond_row))
    modulation = low_back(jnp.dot(activated, ada_weight, precision=HIGHEST) + ada_bias)
    pieces = jnp.split(modulation, 6)
    normed_one = low(layer_norm(block_in) * (1.0 + pieces[1]) + pieces[0])
    projected = low(low_back(jnp.einsum('ld,jde->jle', normed_one, in_weight, precision=HIGHEST)))
    logits = low_back(jnp.dot(normed_one, gate_weight, precision=HIGHEST) + gate_bias)
    mixed_rows = low(middle(projected, logits, conv_taps, flip, SIDE))
    attended = low_back(jnp.dot(mixed_rows, out_weight, precision=HIGHEST))
    after_attn = block_in + pieces[2] * attended
    normed_two = low(layer_norm(after_attn) * (1.0 + pieces[4]) + pieces[3])
    pre_act = low_back(jnp.dot(normed_two, up_weight, precision=HIGHEST) + up_bias)
    hidden = low(jax.nn.gelu(pre_act))
    mlp_out = low_back(jnp.dot(hidden, down_weight, precision=HIGHEST))
    return after_attn + pieces[5] * mlp_out

def reference(section_inputs, condition, timesteps, ada_weight, ada_bias, in_weight, gate_weight, gate_bias, conv_taps, out_weight, up_weight, up_bias, down_weight):
    params = tuple((weight_arg.astype(jnp.float32) for weight_arg in (ada_weight, ada_bias, in_weight, gate_weight, gate_bias, conv_taps, out_weight, up_weight, up_bias, down_weight)))
    inputs = section_inputs[0].astype(jnp.float32)
    cotangent = section_inputs[1].astype(jnp.float32)
    cond_vec = condition + sinusoid(timesteps, D)

    def forward(image_inputs, cond_rows, weights):

        def per_image(image_rows, image_cond):
            first_out = block(image_rows, image_cond, tuple((stacked[0] for stacked in weights)), False)
            middle_rows = low_back(low(first_out))
            return block(middle_rows, image_cond, tuple((stacked[1] for stacked in weights)), True)
        return jax.vmap(per_image)(image_inputs, cond_rows)
    result, pull_back = jax.vjp(forward, inputs, cond_vec, params)
    grad_inputs, cond_grad, grads = pull_back(cotangent)
    section_ends = jnp.stack([grad_inputs.astype(jnp.bfloat16), result.astype(jnp.bfloat16)])
    return (section_ends, cond_grad, grads[0], grads[1], grads[2], grads[3], grads[4], grads[5], grads[6], grads[7], grads[8], grads[9])
```

```python
import functools
import math

import jax
import jax.numpy as jnp
from jax import lax
from jax.experimental import pallas as pl
from jax.experimental.pallas import tpu as pltpu
from jax.sharding import PartitionSpec as P

SIDE = 16
PATCHES = SIDE * SIDE
LANES = 128
F32 = jnp.float32
BF16 = jnp.bfloat16
HIGHEST = lax.Precision.HIGHEST
PLANE = ("tensor", "section")


def call(body, outs, *args, scalars=0, flops=0, scratch=(), after=(), saved=()):
    count, waits, many = len(args), len(after), len(outs)

    def kernel(*refs):
        ins, out_refs = refs[:count], list(refs[count + waits : count + waits + many])
        own = refs[count + waits + many : count + waits + many + len(scratch)]
        held = refs[count + waits + many + len(scratch) :]
        copies = []
        for i, at in enumerate(saved):
            copies.append(pltpu.make_async_copy(held[i], out_refs[at], held[-1].at[i]))
            out_refs[at] = held[i]
        started = []

        def flush(*places):
            for at in places:
                copies[saved.index(at)].start()
                started.append(at)

        if saved:
            body(flush, *ins, *out_refs, *own)
        else:
            body(*ins, *out_refs, *own)
        flush(*[at for at in saved if at not in started])
        for copy in copies:
            copy.wait()

    moved = sum(a.size * a.dtype.itemsize for a in args)
    moved += sum(math.prod(o.shape) * o.dtype.itemsize for o in outs)
    specs = [pl.BlockSpec(memory_space=pltpu.SMEM)] * scalars
    specs += [pl.BlockSpec(memory_space=pltpu.VMEM)] * (count - scalars)
    specs += [pl.BlockSpec(memory_space=pl.ANY)] * waits
    spaces = [pltpu.HBM if i in saved else pltpu.VMEM for i in range(many)]
    hold = [pltpu.VMEM(outs[i].shape, outs[i].dtype) for i in saved]
    if saved:
        hold.append(pltpu.SemaphoreType.DMA((len(saved),)))
    return pl.pallas_call(
        kernel,
        out_shape=tuple(outs),
        in_specs=specs,
        out_specs=tuple(pl.BlockSpec(memory_space=space) for space in spaces),
        scratch_shapes=[*scratch, *hold],
        compiler_params=pltpu.CompilerParams(vmem_limit_bytes=6 * 2**20 + moved * 3 // 2),
        cost_estimate=pl.CostEstimate(flops=flops, bytes_accessed=moved, transcendentals=0),
    )(*args, *after)


def out(shape, dtype):
    return jax.ShapeDtypeStruct(shape, dtype)


def mm(a, b):
    return lax.dot_general(a, b, (((1,), (0,)), ((), ())), preferred_element_type=F32)


def mm_nt(a, b):
    return lax.dot_general(a, b, (((1,), (1,)), ((), ())), preferred_element_type=F32)


def mm_tn(a, b):
    return lax.dot_general(a, b, (((0,), (0,)), ((), ())), preferred_element_type=F32)


def normalize(v):
    centered = v - jnp.mean(v, axis=-1, keepdims=True)
    scale = lax.rsqrt(jnp.mean(centered * centered, axis=-1, keepdims=True) + 1e-06)
    return centered * scale, scale


def norm_grad(hat, rstd, grad):
    inner = jnp.mean(grad * hat, axis=-1, keepdims=True)
    return rstd * (grad - jnp.mean(grad, axis=-1, keepdims=True) - hat * inner)


def gather_total(pieces):
    total = pieces[0][...].astype(F32)
    for piece in pieces[1:]:
        total = total + piece[...].astype(F32)
    return total


def rows_sum(v):
    return jnp.sum(v, axis=0, keepdims=True)


def gelu_terms(x):
    k = math.sqrt(2.0 / math.pi)
    th = jnp.tanh(k * (x + 0.044715 * x * x * x))
    value = 0.5 * x * (1.0 + th)
    slope = 0.5 * (1.0 + th) + 0.5 * x * (1.0 - th * th) * k * (1.0 + 3 * 0.044715 * x * x)
    return value, slope


def start_kernel(x_ref, mod_ref, n_ref):
    for m in range(x_ref.shape[0]):
        hat, _ = normalize(x_ref[m].astype(F32))
        n_ref[m] = (hat * (1.0 + mod_ref[m, 1:2]) + mod_ref[m, 0:1]).astype(BF16)


def scale_rows_kernel(g_ref, mod_ref, o_ref):
    for m in range(g_ref.shape[0]):
        o_ref[m] = (mod_ref[m, 5:6] * g_ref[m].astype(F32)).astype(BF16)


def after_attn_kernel(flush, p0, p1, p2, p3, x_ref, mod_ref, att_ref, aft_ref, n_ref):
    for m in range(x_ref.shape[0]):
        att = gather_total([p.at[m] for p in (p0, p1, p2, p3)])
        aft = x_ref[m].astype(F32) + mod_ref[m, 2:3] * att
        hat, _ = normalize(aft)
        att_ref[m] = att
        aft_ref[m] = aft
        n_ref[m] = (hat * (1.0 + mod_ref[m, 4:5]) + mod_ref[m, 3:4]).astype(BF16)


def between_kernel(p0, p1, p2, p3, aft_ref, mod_ref, next_ref, mlp_ref, x_ref, n_ref):
    for m in range(aft_ref.shape[0]):
        mlp = gather_total([p.at[m] for p in (p0, p1, p2, p3)])
        x = (aft_ref[m] + mod_ref[m, 5:6] * mlp).astype(BF16)
        hat, _ = normalize(x.astype(F32))
        mlp_ref[m] = mlp
        x_ref[m] = x
        n_ref[m] = (hat * (1.0 + next_ref[m, 1:2]) + next_ref[m, 0:1]).astype(BF16)


def end_kernel(p0, p1, p2, p3, aft_ref, mod_ref, g_ref, x_ref, gate_ref):
    for m in range(aft_ref.shape[0]):
        mlp = gather_total([p.at[m] for p in (p0, p1, p2, p3)])
        x_ref[m] = (aft_ref[m] + mod_ref[m, 5:6] * mlp).astype(BF16)
        gate_ref[m] = rows_sum(g_ref[m].astype(F32) * mlp)


def back_mlp_rows_kernel(p0, p1, p2, p3, g_ref, aft_ref, att_ref, mod_ref, ga_ref, gt_ref, gm_ref):
    for m in range(aft_ref.shape[0]):
        gn = gather_total([p.at[m] for p in (p0, p1, p2, p3)])
        hat, rstd = normalize(aft_ref[m])
        grad = g_ref[m].astype(F32) + norm_grad(hat, rstd, gn * (1.0 + mod_ref[m, 4:5]))
        ga_ref[m] = grad
        gt_ref[m] = (mod_ref[m, 2:3] * grad).astype(BF16)
        gm_ref[m, 0:1] = rows_sum(grad * att_ref[m])
        gm_ref[m, 1:2] = rows_sum(gn)
        gm_ref[m, 2:3] = rows_sum(gn * hat)


def back_attn_rows(pieces, ga_ref, x_ref, mod_ref, some_ref, gate_ref, gm_ref, m):
    gn = gather_total([p.at[m] for p in pieces])
    hat, rstd = normalize(x_ref[m].astype(F32))
    grad = ga_ref[m] + norm_grad(hat, rstd, gn * (1.0 + mod_ref[m, 1:2]))
    gm_ref[m, 0:1] = rows_sum(gn)
    gm_ref[m, 1:2] = rows_sum(gn * hat)
    gm_ref[m, 2:5] = some_ref[m]
    gm_ref[m, 5:6] = gate_ref[m]
    return grad.astype(BF16)


def back_between_kernel(
    p0, p1, p2, p3, ga_ref, x_ref, mod_ref, some_ref, gate_ref, prev_ref, mlp_ref, g_ref, gmlp_ref, gm_ref, next_ref
):
    for m in range(x_ref.shape[0]):
        grad = back_attn_rows((p0, p1, p2, p3), ga_ref, x_ref, mod_ref, some_ref, gate_ref, gm_ref, m)
        g_ref[m] = grad
        wide = grad.astype(F32)
        gmlp_ref[m] = (prev_ref[m, 5:6] * wide).astype(BF16)
        next_ref[m] = rows_sum(wide * mlp_ref[m])


def back_end_kernel(p0, p1, p2, p3, ga_ref, x_ref, mod_ref, some_ref, gate_ref, g_ref, gm_ref):
    for m in range(x_ref.shape[0]):
        g_ref[m] = back_attn_rows((p0, p1, p2, p3), ga_ref, x_ref, mod_ref, some_ref, gate_ref, gm_ref, m)


def scan_mask(columns_first):
    def place(number):
        if columns_first:
            return (number % SIDE) * SIDE + number // SIDE
        return number

    shape = (PATCHES, PATCHES)
    later = place(lax.broadcasted_iota(jnp.int32, shape, 0))
    return later >= place(lax.broadcasted_iota(jnp.int32, shape, 1))


def grid_column():
    return lax.broadcasted_iota(jnp.int32, (PATCHES, 1), 0) % SIDE


def side_shifts(a, column):
    left = jnp.where(column == 0, 0.0, pltpu.roll(a, 1, 0))
    right = jnp.where(column == SIDE - 1, 0.0, pltpu.roll(a, PATCHES - 1, 0))
    return left, a, right


def convolve(shifted, tap):
    sums = []
    for row in range(3):
        terms = [shifted[col] * tap(3 * row + col) for col in range(3)]
        sums.append(terms[0] + terms[1] + terms[2])
    zeros = jnp.zeros((SIDE, sums[0].shape[1]), F32)
    above = jnp.concatenate([zeros, sums[0][:-SIDE]], axis=0)
    below = jnp.concatenate([sums[2][SIDE:], zeros], axis=0)
    return shifted[1] + sums[1] + above + below


def tap_grads(shifted, grad):
    found = []
    for row in range(3):
        for col in range(3):
            if row == 0:
                product = shifted[col][:-SIDE] * grad[SIDE:]
            elif row == 1:
                product = shifted[col] * grad
            else:
                product = shifted[col][SIDE:] * grad[:-SIDE]
            found.append(rows_sum(product))
    return found


def lane_sets(width, first, head_width, heads):
    lane = lax.broadcasted_iota(jnp.int32, (1, width), 1)
    return [
        (lane >= first + h * head_width) & (lane < first + (h + 1) * head_width)
        for h in range(heads)
    ]


def decay_parts(logits, mask, gate_lane, heads):
    rates = -(jnp.maximum(logits, 0.0) + jnp.log1p(jnp.exp(-jnp.abs(logits))))
    ones = jnp.where(mask, 1.0, 0.0)
    totals = lax.dot_general(
        ones, rates, (((1,), (0,)), ((), ())), precision=HIGHEST, preferred_element_type=F32
    )
    turned = totals.T
    decays = []
    for h in range(heads):
        at = gate_lane + h
        spans = jnp.where(mask, totals[:, at : at + 1] - turned[at : at + 1, :], -1e30)
        w = jnp.exp(spans)
        decays.append((w, jnp.sum(w, axis=1, keepdims=True)))
    return decays, ones


def send_order(k):
    return (0, 1, None, None, 2, 3, None, None)[k], (None, None, 0, 1, None, None, 2, 3)[k]


def write_pieces(me, total_ref, other_ref, own_refs):
    rows = total_ref.shape[1] // 8
    for k in range(8):
        spot = pl.ds(pl.multiple_of(jnp.bitwise_xor(me, k) * rows, rows), rows)
        own, other = send_order(k)
        if own is None:
            other_ref[other] = total_ref[:, spot, :]
        else:
            own_refs[own][...] = total_ref[:, spot, :]


def each_shard(refs):
    own, core, three, crossed = refs
    return (own, three.at[0], core, crossed.at[0], three.at[1], three.at[2], crossed.at[1], crossed.at[2])


def gather_pieces(me, shard_refs, full_ref):
    rows = full_ref.shape[1] // 8
    for k, shard in enumerate(each_shard(shard_refs)):
        spot = pl.ds(pl.multiple_of(jnp.bitwise_xor(me, k) * rows, rows), rows)
        full_ref[:, spot, :] = shard[...]


def tail_spots(heads):
    return (0, 32, 48, 64, 80)


def join_tail(packed, piece, tails, lane):
    tile = packed[:, piece * LANES : (piece + 1) * LANES]
    return jnp.concatenate([tile, pltpu.roll(tails, (LANES - lane) % LANES, 1)], axis=1)


def lanes():
    return lax.broadcasted_iota(jnp.int32, (1, LANES), 1)


def half_tiles(tiles, at):
    if at == 0:
        return tiles[0], tiles[1]
    shift = 2 * LANES - at
    first = jnp.where(lanes() < shift, pltpu.roll(tiles[1], shift, 1), pltpu.roll(tiles[2], shift, 1))
    return first, pltpu.roll(tiles[2], shift, 1)


def pack_attn_kernel(cfg, sec_ref, in_ref, gate_ref, out_ref, keep_ref, send_ref):
    heads, channels = cfg
    spots = tail_spots(heads)
    tail = channels - LANES
    rows = in_ref.shape[1]
    short = jnp.zeros((rows, 3 * LANES - 2 * channels), F32)
    keep_first = sec_ref[0] == 0
    lane = lanes()
    tails = [gate_ref[...], pltpu.roll(gate_ref[...], LANES - heads, 1)]
    tails = [
        jnp.where((lane >= tail) & (lane < tail + heads), pltpu.roll(v, tail, 1), 0.0) for v in tails
    ]
    for j in range(5):
        ref = out_ref if j == 4 else in_ref.at[j]
        tiles = [ref[:, :LANES].astype(F32), ref[:, LANES : 2 * LANES].astype(F32)]
        tiles.append(jnp.concatenate([ref[:, 2 * LANES :].astype(F32), short], axis=1))
        whole = []
        for h in range(2):
            tile, rest = half_tiles(tiles, h * channels)
            whole.append(tile)
            tails[h] = tails[h] + pltpu.roll(jnp.where(lane < tail, rest, 0.0), spots[j], 1)
        cols = slice(j * LANES, (j + 1) * LANES)
        keep_ref[:, cols] = jnp.where(keep_first, whole[0], whole[1]).astype(BF16)
        send_ref[:, cols] = jnp.where(keep_first, whole[1], whole[0]).astype(BF16)
    keep_ref[:, 5 * LANES :] = jnp.where(keep_first, tails[0], tails[1]).astype(BF16)
    send_ref[:, 5 * LANES :] = jnp.where(keep_first, tails[1], tails[0]).astype(BF16)


def unpack_attn_kernel(cfg, sec_ref, mine_ref, recv_ref, in_ref, gate_ref, out_ref):
    heads, channels = cfg
    spots = tail_spots(heads)
    tail = channels - LANES
    mine_first = sec_ref[0] == 0
    lane = lanes()
    shift = channels - LANES

    def both(cols):
        mine, recv = mine_ref[:, cols], recv_ref[:, cols].astype(F32)
        return jnp.where(mine_first, mine, recv), jnp.where(mine_first, recv, mine)

    low_tails, high_tails = both(slice(5 * LANES, 6 * LANES))
    for j in range(5):
        ref = out_ref if j == 4 else in_ref.at[j]
        low, high = both(slice(j * LANES, (j + 1) * LANES))
        ref[:, :LANES] = low
        high = pltpu.roll(high, shift, 1)
        low_tail = pltpu.roll(low_tails, (LANES - spots[j]) % LANES, 1)
        high_tail = pltpu.roll(high_tails, (LANES - spots[j] + shift) % LANES, 1)
        ref[:, LANES : 2 * LANES] = jnp.where(lane < tail, low_tail, high)
        last = jnp.where(lane < shift, high, high_tail)
        ref[:, 2 * LANES :] = last[:, : 2 * channels - 2 * LANES]
    low_gate = pltpu.roll(low_tails, LANES - tail, 1)
    high_gate = pltpu.roll(high_tails, LANES - tail + heads, 1)
    gate_ref[...] = jnp.where(lane < heads, low_gate, high_gate)[:, : 2 * heads]


def attn_forward_kernel(cfg, flush, me_ref, *refs):
    columns_first, heads, head_width = cfg
    shards, (w_ref, gb_ref, tap_ref) = refs[:4], refs[4:7]
    n_ref, proj_ref, log_ref, attn_ref, mix_ref, other_ref = refs[7:13]
    own_refs, total_ref = refs[13:17], refs[17]
    me = me_ref[0]
    wide = 2 * LANES
    gate_lane = heads * head_width - LANES
    spots = tail_spots(heads)
    mask = scan_mask(columns_first)
    column = grid_column()
    sets = lane_sets(wide, 0, head_width, heads)
    gather_pieces(me, shards, n_ref)
    flush(0)
    for m in range(n_ref.shape[0]):
        projected = mm(n_ref[m], w_ref[:, : 4 * LANES])
        tails = mm(n_ref[m], w_ref[:, 5 * LANES :])
        logits = tails + gb_ref[...]
        log_ref[m] = logits
        decays, _ = decay_parts(logits, mask, gate_lane, heads)
        query, key, value, gate = (join_tail(projected, j, tails, spots[j]) for j in range(4))
        in_head = sets[0]
        for own in sets[1:]:
            in_head = in_head | own
        query, key, value = (jnp.where(in_head, v, 0.0).astype(BF16) for v in (query, key, value))
        gate = gate.astype(BF16)
        for j, v in enumerate((query, key, value, gate)):
            proj_ref[m, :, j * wide : (j + 1) * wide] = v
        attn = None
        for h in range(heads):
            w, mass = decays[h]
            raw = mm_nt(jnp.where(sets[h], query, jnp.zeros_like(query)), key)
            scores = (raw * head_width ** (-0.5) * w).astype(BF16)
            normed = mm(scores, value) * lax.rsqrt(mass)
            attn = jnp.where(sets[h], normed, 0.0 if attn is None else attn)
        attn_ref[m] = attn
        spread = convolve(side_shifts(attn, column), lambda i: tap_ref[i : i + 1, :])
        gate = gate.astype(F32)
        mixed = spread * (gate * jax.nn.sigmoid(gate))
        mixed = jnp.where(in_head, mixed, 0.0)
        mixed = jnp.concatenate(
            [mixed[:, :LANES], pltpu.roll(mixed[:, LANES:], spots[4], 1)], axis=1
        ).astype(BF16)
        mix_ref[m] = mixed
        if m == n_ref.shape[0] - 1:
            flush(1, 2, 3, 4)
        total_ref[m] = mm_nt(mixed, w_ref[:, 4 * LANES :]).astype(BF16)
    write_pieces(me, total_ref, other_ref, own_refs)


def attn_backward_kernel(cfg, me_ref, *refs):
    columns_first, heads, head_width = cfg
    shards, (proj_ref, log_ref, attn_ref, w_ref, tap_ref) = refs[:4], refs[4:9]
    g_ref, gproj_ref, gtap_ref, other_ref = refs[9:13]
    own_refs, total_ref = refs[13:17], refs[17]
    me = me_ref[0]
    wide = 2 * LANES
    gate_lane = heads * head_width - LANES
    spots = tail_spots(heads)
    scale = head_width ** (-0.5)
    mask = scan_mask(columns_first)
    column = grid_column()
    sets = lane_sets(wide, 0, head_width, heads)
    gate_sets = lane_sets(LANES, gate_lane, 1, heads)
    sublane = lax.broadcasted_iota(jnp.int32, (LANES, 1), 0)
    in_head = sets[0]
    for own in sets[1:]:
        in_head = in_head | own
    gather_pieces(me, shards, g_ref)
    gtap_ref[...] = jnp.zeros(gtap_ref.shape, F32)
    for m in range(g_ref.shape[0]):
        g_packed = mm(g_ref[m], w_ref[:, 4 * LANES :])
        g_mixed = jnp.where(in_head, join_tail(g_packed, 0, g_packed[:, LANES:], spots[4]), 0.0)
        query, key, value, gate = (proj_ref[m, :, j * wide : (j + 1) * wide] for j in range(4))
        gate = gate.astype(F32)
        sig = jax.nn.sigmoid(gate)
        attn = attn_ref[m]
        shifted = side_shifts(attn, column)
        spread = convolve(shifted, lambda i: tap_ref[i : i + 1, :])
        g_spread = g_mixed * (gate * sig)
        g_gate = g_mixed * spread * (sig * (1.0 + gate * (1.0 - sig)))
        for i, grad in enumerate(tap_grads(shifted, g_spread)):
            gtap_ref[i : i + 1, :] = grad if m == 0 else gtap_ref[i : i + 1, :] + grad
        g_attn = convolve(side_shifts(g_spread, column), lambda i: tap_ref[8 - i : 9 - i, :])
        logits = log_ref[m]
        decays, ones = decay_parts(logits, mask, gate_lane, heads)
        g_query = g_key = g_value = 0.0
        across = jnp.zeros((PATCHES, LANES), F32)
        down = jnp.zeros((LANES, PATCHES), F32)
        for h in range(heads):
            w, mass = decays[h]
            own_query = jnp.where(sets[h], query, jnp.zeros_like(query))
            raw = mm_nt(own_query, key) * scale
            own_grad = jnp.where(sets[h], g_attn, 0.0)
            g_mass = -0.5 * jnp.sum(own_grad * attn, axis=1, keepdims=True) / mass
            g_out = (own_grad * lax.rsqrt(mass)).astype(BF16)
            g_value = g_value + mm_tn((raw * w).astype(BF16), g_out)
            g_scores = mm_nt(g_out, value)
            g_raw = (g_scores * w * scale).astype(BF16)
            g_query = jnp.where(sets[h], mm(g_raw, key), g_query)
            g_key = g_key + mm_tn(g_raw, own_query)
            g_span = (g_scores * raw + g_mass) * w
            across = jnp.where(gate_sets[h], jnp.sum(g_span, axis=1, keepdims=True), across)
            down = jnp.where(sublane == gate_lane + h, rows_sum(g_span), down)
        g_rates = lax.dot_general(
            ones,
            across - down.T,
            (((0,), (0,)), ((), ())),
            precision=HIGHEST,
            preferred_element_type=F32,
        )
        g_logits = (-g_rates * jax.nn.sigmoid(logits)).astype(BF16).astype(F32)
        g_bias = rows_sum(g_logits)
        gtap_ref[9:10, :LANES] = g_bias if m == 0 else gtap_ref[9:10, :LANES] + g_bias
        tails = g_logits
        for j, v in enumerate((g_query, g_key, g_value, g_gate)):
            gproj_ref[m, :, j * LANES : (j + 1) * LANES] = v[:, :LANES].astype(BF16)
            tails = tails + pltpu.roll(v[:, LANES:], spots[j], 1)
        gproj_ref[m, :, 4 * LANES :] = tails.astype(BF16)
        total = mm_nt(gproj_ref[m, :, : 4 * LANES], w_ref[:, : 4 * LANES])
        total = total + mm_nt(gproj_ref[m, :, 4 * LANES :], w_ref[:, 5 * LANES :])
        total_ref[m] = total.astype(BF16)
    write_pieces(me, total_ref, other_ref, own_refs)


def attn_weights_kernel(n_ref, gproj_ref, g_ref, mix_ref, gw_ref):
    for part in range(2):
        cols = slice(part * 2 * LANES, (part + 1) * 2 * LANES)
        total = mm_tn(n_ref[0], gproj_ref[0, :, cols])
        for m in range(1, n_ref.shape[0]):
            total = total + mm_tn(n_ref[m], gproj_ref[m, :, cols])
        gw_ref[:, cols] = total.astype(BF16)
    total = mm_tn(g_ref[0], mix_ref[0])
    tails = mm_tn(n_ref[0], gproj_ref[0, :, 4 * LANES :])
    for m in range(1, n_ref.shape[0]):
        total = total + mm_tn(g_ref[m], mix_ref[m])
        tails = tails + mm_tn(n_ref[m], gproj_ref[m, :, 4 * LANES :])
    gw_ref[:, 4 * LANES : 5 * LANES] = total[:, :LANES].astype(BF16)
    gw_ref[:, 5 * LANES :] = (total[:, LANES:] + tails).astype(BF16)


def stack_shards(shards, full_ref):
    for k, shard in enumerate(each_shard(shards)):
        images, rows, width = shard.shape
        full_ref[k * images * rows : (k + 1) * images * rows, :] = shard[...].reshape(
            images * rows, width
        )


def put_shard(k, value, shape, other_ref, own_refs):
    own, other = send_order(k)
    if own is None:
        other_ref[other] = value.astype(BF16).reshape(shape)
    else:
        own_refs[own][...] = value.astype(BF16).reshape(shape)


def put_shards(total, shape, other_ref, own_refs):
    rows = total.shape[0] // 8
    for k in range(8):
        put_shard(k, total[k * rows : (k + 1) * rows], shape, other_ref, own_refs)


def mlp_forward_kernel(left, flush, *refs):
    shards, (w_ref, ub_ref) = refs[:4], refs[4:6]
    n_ref, pre_ref, hid_ref, other_ref = refs[6:10]
    own_refs = refs[10:14]
    main = (w_ref.shape[1] - LANES) // 2
    stack_shards(shards, n_ref)
    flush(0)
    n = n_ref[...]
    pre = mm(n, w_ref[:, :main]) + ub_ref[:, :main]
    pre_ref[:, :main] = pre
    hidden = gelu_terms(pre)[0].astype(BF16)
    hid_ref[:, :main] = hidden
    last = mm(n, w_ref[:, 2 * main :]) + ub_ref[:, main:]
    pre_ref[:, main:] = last
    lane = lax.broadcasted_iota(jnp.int32, (1, LANES), 1)
    tail = jnp.where(lane < left, gelu_terms(last)[0], 0.0)
    tail = pltpu.roll(tail, LANES - left, 1).astype(BF16)
    hid_ref[:, main:] = tail
    flush(1, 2)
    total = mm_nt(hidden, w_ref[:, main : 2 * main]) + mm_nt(tail, w_ref[:, 2 * main :])
    put_shards(total, shards[0].shape, other_ref, own_refs)


def mlp_backward_kernel(left, *refs):
    shards, (pre_ref, w_ref) = refs[:4], refs[4:6]
    g_ref, gpre_ref, gub_ref, other_ref = refs[6:10]
    own_refs = refs[10:14]
    main = (w_ref.shape[1] - LANES) // 2
    stack_shards(shards, g_ref)
    g = g_ref[...]
    g_pre = mm(g, w_ref[:, main : 2 * main]) * gelu_terms(pre_ref[:, :main])[1]
    g_pre = g_pre.astype(BF16)
    gpre_ref[:, :main] = g_pre
    gub_ref[:, :main] = rows_sum(g_pre.astype(F32))
    lane = lax.broadcasted_iota(jnp.int32, (1, LANES), 1)
    last = pltpu.roll(mm(g, w_ref[:, 2 * main :]), left, 1) * gelu_terms(pre_ref[:, main:])[1]
    last = jnp.where(lane < left, last, 0.0).astype(BF16)
    gpre_ref[:, main:] = last
    gub_ref[:, main:] = rows_sum(last.astype(F32))
    total = mm_nt(g_pre, w_ref[:, :main]) + mm_nt(last, w_ref[:, 2 * main :])
    put_shards(total, shards[0].shape, other_ref, own_refs)


def mlp_weights_kernel(n_ref, gpre_ref, g_ref, hid_ref, gw_ref):
    main = gpre_ref.shape[1] - LANES
    gw_ref[:, :main] = mm_tn(n_ref[...], gpre_ref[:, :main]).astype(BF16)
    gw_ref[:, main : 2 * main] = mm_tn(g_ref[...], hid_ref[:, :main]).astype(BF16)
    last = mm_tn(n_ref[...], gpre_ref[:, main:]) + mm_tn(g_ref[...], hid_ref[:, main:])
    gw_ref[:, 2 * main :] = last.astype(BF16)


def swap(value, tensor_bits, section_bit):
    tensors, sections = lax.axis_size("tensor"), lax.axis_size("section")
    route = [
        (t * sections + s, (t ^ tensor_bits) * sections + (s ^ section_bit))
        for t in range(tensors)
        for s in range(sections)
    ]
    return lax.ppermute(value, PLANE, route)


def gather_plane(own):
    core = swap(own, 1, 0)
    xy, x, y = swap(own, 2, 1), swap(own, 0, 1), swap(own, 2, 0)
    three = jnp.stack([x, y, xy])
    return own, core, three, swap(three, 1, 0)


def scatter_plane(other, own):
    received = swap(other, 1, 0)
    sums = [(o.astype(F32) + received[j].astype(F32)).astype(BF16) for j, o in enumerate(own)]
    return (sums[0], swap(sums[3], 2, 1), swap(sums[1], 0, 1), swap(sums[2], 2, 0)), sums


def spread_over(value, axes):
    count = math.prod(lax.axis_size(a) for a in axes)
    copies = jnp.broadcast_to(value[None], (count,) + value.shape)
    return lax.all_to_all(copies, axes, split_axis=0, concat_axis=0, tiled=True)


def along(value, pairs):
    return lax.ppermute(value, "dp", pairs)


def gather_rows(own, ring=False):
    count = lax.axis_size("dp")
    if count != 4 or not ring:
        return lax.all_gather(own, "dp", axis=0, tiled=True)
    d = lax.axis_index("dp")
    rows = own.shape[0]
    r1 = along(own, [(0, 1), (1, 2), (2, 3)])
    l1 = along(own, [(3, 2), (2, 1), (1, 0)])
    r2 = along(r1, [(1, 2), (2, 3)])
    l2 = along(l1, [(2, 1), (1, 0)])
    r3 = along(r2, [(2, 3)])
    l3 = along(l2, [(1, 0)])
    full = jnp.zeros((count * rows, own.shape[1]), own.dtype)
    full = lax.dynamic_update_slice_in_dim(full, own, d * rows, 0)
    for k, (left, right) in enumerate(((r3, l1), (r2, l2), (r1, l3)), 1):
        piece = jnp.where(d + k < count, right, left)
        full = lax.dynamic_update_slice_in_dim(full, piece, (d + k) % count * rows, 0)
    return full


def scatter_rows(partial, ring=False):
    count = lax.axis_size("dp")
    if count != 4 or not ring:
        return lax.psum_scatter(partial, "dp", scatter_dimension=0, tiled=True).astype(F32)
    d = lax.axis_index("dp")
    parts = partial.reshape(count, partial.shape[0] // count, partial.shape[1])

    def part(at):
        return lax.dynamic_index_in_dim(parts, at % count, 0, keepdims=False)

    def plus(a, b):
        return (a.astype(F32) + b.astype(F32)).astype(BF16)

    l1 = along(part(d + 1), [(3, 2)])
    r1 = along(part(d + 3), [(0, 1)])
    l2 = along(plus(part(d + 2), l1), [(3, 2), (2, 1)])
    r2 = along(plus(part(d + 2), r1), [(0, 1), (1, 2)])
    l3 = along(plus(part(d + 3), l2), [(3, 2), (2, 1), (1, 0)])
    r3 = along(plus(part(d + 1), r2), [(0, 1), (1, 2), (2, 3)])
    return part(d).astype(F32) + l3.astype(F32) + r3.astype(F32)


def sinusoid(time_steps, channels):
    half_width = channels // 2
    frequency = jnp.exp(
        jnp.arange(half_width, dtype=jnp.float32) * (-math.log(10000.0) / half_width)
    )
    angles = time_steps.astype(jnp.float32)[:, None] * frequency[None, :]
    return jnp.concatenate([jnp.cos(angles), jnp.sin(angles)], axis=1)


def per_device(
    section_inputs,
    condition,
    timesteps,
    ada_weight,
    ada_bias,
    in_weight,
    gate_weight,
    gate_bias,
    conv_taps,
    out_weight,
    up_weight,
    up_bias,
    down_weight,
):
    d = lax.axis_index("dp")
    t = lax.axis_index("tensor")
    s = lax.axis_index("section")
    dps, tensors, sections = (lax.axis_size(a) for a in ("dp", "tensor", "section"))
    first = s == 0
    me = (t * sections + s).astype(jnp.int32).reshape(1)
    images = condition.shape[0]
    width = condition.shape[1]
    slab = in_weight.shape[2]
    heads = gate_weight.shape[2] // sections
    channels = in_weight.shape[3] // sections
    head_width = channels // heads
    units = up_weight.shape[2] // sections
    wide = 2 * LANES
    tail = channels - LANES
    rows = section_inputs.shape[2] // sections
    main = units // LANES * LANES
    left = units - main
    spots = tail_spots(heads)

    def cut(value, axis):
        half = value.shape[axis] // 2
        return (
            lax.slice_in_dim(value, 0, half, axis=axis),
            lax.slice_in_dim(value, half, 2 * half, axis=axis),
        )

    def swap_halves(keep, send):
        received = lax.ppermute(send, "section", [(0, 1), (1, 0)])
        return jnp.where(first, keep, received), jnp.where(first, received, keep)

    def choose(pair):
        return jnp.where(first, pair[0], pair[1]), jnp.where(first, pair[1], pair[0])

    shape_a = (slab, 6 * LANES)
    cfg = (heads, channels)
    section = s.astype(jnp.int32).reshape(1)
    def unit_halves(value):
        rest = sections * main
        return tuple(
            (value[:, h * main : (h + 1) * main], value[:, rest + h * left : rest + (h + 1) * left])
            for h in (0, 1)
        )

    def pack_b(up_half, down_half):
        return jnp.concatenate([up_half[0], down_half[0], up_half[1], down_half[1]], axis=1)

    def pack_small(gate_half, taps_half, up_half):
        return jnp.concatenate([gate_half.reshape(-1), taps_half.reshape(-1), up_half.reshape(-1)])

    def pack_halves(pack, *pairs):
        return tuple(pack(*(pair[i] for pair in pairs)) for i in (0, 1))

    x_pair = cut(section_inputs[0], 1)
    x_received = lax.ppermute(
        jnp.where(first, x_pair[1], x_pair[0]), "section", [(0, 1), (1, 0)]
    )
    x0 = jnp.where(first, x_pair[0], x_received)
    g1 = jnp.where(first, x_received, x_pair[1])
    kept_b, sent_b = choose(
        pack_halves(pack_b, unit_halves(up_weight[0]), unit_halves(down_weight[0].T))
    )
    in_own, sent_b = lax.optimization_barrier((in_weight[0], sent_b))
    packs_b = swap_halves(kept_b, sent_b)
    kept_a, sent_a = (
        call(
            functools.partial(pack_attn_kernel, cfg),
            (out(shape_a, BF16),) * 2,
            section,
            in_own,
            jnp.pad(gate_weight[0].astype(F32), ((0, 0), (0, LANES - gate_weight.shape[2]))),
            out_weight[0].T,
            scalars=1,
        )
    )

    kept_a, sent_a, condition = lax.optimization_barrier((kept_a, sent_a, condition))
    packs_a = swap_halves(kept_a, sent_a)
    taps_count = conv_taps.shape[1]
    up_row = up_bias[0].astype(F32)[None]
    small = swap_halves(
        *choose(
            pack_halves(
                pack_small,
                cut(gate_bias[0].astype(F32), 0),
                cut(conv_taps[0].astype(F32), 1),
                tuple(jnp.concatenate(v, axis=1) for v in unit_halves(up_row)),
            )
        )
    )

    def unpack_small(packed):
        gate_row = jnp.pad(packed[:heads][None], ((0, 0), (tail, LANES - heads - tail)))
        taps = packed[heads : heads + taps_count * channels].reshape(taps_count, channels)
        taps = jnp.pad(taps, ((0, 16 - taps_count), (0, wide - channels)))
        up_row = packed[heads + taps_count * channels :][None]
        return gate_row, taps, jnp.pad(up_row, ((0, 0), (0, main + LANES - units)))

    weights = [
        (gather_rows(packs_a[b], b == 0), gather_rows(packs_b[b]), *unpack_small(small[b]))
        for b in (0, 1)
    ]

    cond_vec = condition + sinusoid(timesteps, width)
    activated = jax.nn.silu(cond_vec).astype(BF16)
    slab_active = activated.reshape(images, dps, slab).transpose(1, 0, 2)
    slab_active = lax.all_to_all(slab_active, "dp", split_axis=0, concat_axis=0, tiled=True)
    slab_active = slab_active.reshape(dps * images, slab)
    mod_part = jnp.dot(slab_active, ada_weight[0], preferred_element_type=F32)
    mod_parts = lax.all_to_all(
        mod_part.reshape(dps, images, -1), "dp", split_axis=0, concat_axis=0, tiled=True
    )
    mod_share = jnp.sum(mod_parts, axis=0) + ada_bias[0].astype(F32)
    mod_all = spread_over(mod_share, ("section", "tensor"))
    mod_all = mod_all.reshape(sections, tensors, images, -1).transpose(0, 2, 1, 3)
    mod_all = mod_all.reshape(sections, images, 6, width)
    mods = (mod_all[0], mod_all[1])

    shard = out((images, rows, width), BF16)
    shard_wide = out((images, rows, width), F32)
    vector = out((images, 1, width), F32)
    pieces_out = (out((4, images, rows, width), BF16),) + (shard,) * 4
    full = out((images, PATCHES, width), BF16)
    flat = out((images * PATCHES, width), BF16)
    total_rows = images * PATCHES
    kept = pltpu.VMEM((images, PATCHES, width), BF16)
    middle_flops = 2 * total_rows * PATCHES * wide * heads * 6
    attn_flops = 2 * total_rows * width * wide * 5 + middle_flops
    mlp_flops = 4 * total_rows * width * units

    def attn_forward(b, normed):
        w, _, gate_row, taps, _ = weights[b]
        body = functools.partial(attn_forward_kernel, (b == 1, heads, head_width))
        found = call(
            body,
            (
                full,
                out((images, PATCHES, 4 * wide), BF16),
                out((images, PATCHES, LANES), F32),
                out((images, PATCHES, wide), F32),
                out((images, PATCHES, wide), BF16),
                *pieces_out,
            ),
            me,
            *gather_plane(normed),
            w,
            gate_row,
            taps,
            scalars=1,
            flops=attn_flops,
            scratch=[kept],
            saved=(0, 1, 2, 3, 4),
        )
        return found[:5], scatter_plane(found[5], found[6:])[0]

    def attn_backward(b, grad, saved):
        w, _, _, taps, _ = weights[b]
        body = functools.partial(attn_backward_kernel, (b == 1, heads, head_width))
        found = call(
            body,
            (
                full,
                out((images, PATCHES, 5 * LANES), BF16),
                out((16, wide), F32),
                *pieces_out,
            ),
            me,
            *gather_plane(grad),
            saved[1],
            saved[2],
            saved[3],
            w,
            taps,
            scalars=1,
            flops=2 * attn_flops,
            scratch=[kept],
        )
        terms, sums = scatter_plane(found[3], found[4:])
        (grads,) = call(
            attn_weights_kernel,
            (out((width, 6 * LANES), BF16),),
            saved[0],
            found[1],
            found[0],
            saved[4],
            flops=2 * total_rows * width * wide * 5,
            after=sums,
        )
        return terms, grads, found[2]

    def mlp_forward(b, normed):
        _, w, _, _, up_row = weights[b]
        found = call(
            functools.partial(mlp_forward_kernel, left),
            (
                flat,
                out((total_rows, main + LANES), F32),
                out((total_rows, main + LANES), BF16),
                *pieces_out,
            ),
            *gather_plane(normed),
            w,
            up_row,
            flops=mlp_flops,
            saved=(0, 1, 2),
        )
        return found[:3], scatter_plane(found[3], found[4:])[0]

    def mlp_backward(b, shards, saved):
        _, w, _, _, _ = weights[b]
        found = call(
            functools.partial(mlp_backward_kernel, left),
            (flat, out((total_rows, main + LANES), BF16), out((1, main + LANES), F32), *pieces_out),
            *shards,
            saved[1],
            w,
            flops=mlp_flops,
        )
        terms, sums = scatter_plane(found[3], found[4:])
        (grads,) = call(
            mlp_weights_kernel,
            (out((width, 2 * main + LANES), BF16),),
            saved[0],
            found[1],
            found[0],
            saved[2],
            flops=mlp_flops,
            after=sums,
        )
        return terms, grads, found[2]

    (normed,) = call(start_kernel, (shard,), x0, mods[0])
    attn0, terms = attn_forward(0, normed)
    att0, aft0, normed = call(
        after_attn_kernel,
        (shard_wide, shard_wide, shard),
        *terms,
        x0,
        mods[0],
        saved=(0, 1),
    )
    mlp0, terms = mlp_forward(0, normed)
    mlp_out0, x1, normed = call(
        between_kernel, (shard_wide, shard, shard), *terms, aft0, mods[0], mods[1]
    )
    attn1, terms = attn_forward(1, normed)
    att1, aft1, normed = call(
        after_attn_kernel,
        (shard_wide, shard_wide, shard),
        *terms,
        x1,
        mods[1],
        saved=(0, 1),
    )
    mlp1, end_terms = mlp_forward(1, normed)
    (g_mlp,) = call(scale_rows_kernel, (shard,), g1, mods[1])
    block_out, g_gate_two1 = call(end_kernel, (shard, vector), *end_terms, aft1, mods[1], g1)

    three, six = out((images, 3, width), F32), out((images, 6, width), F32)
    terms, mlp_grads1, g_up_bias1 = mlp_backward(1, gather_plane(g_mlp), mlp1)
    g_after, g_attn, g_some = call(
        back_mlp_rows_kernel,
        (shard_wide, shard, three),
        *terms,
        g1,
        aft1,
        att1,
        mods[1],
        after=(mlp_grads1,),
    )
    sum_b1 = scatter_rows(mlp_grads1)
    terms, attn_grads1, g_taps1 = attn_backward(1, g_attn, attn1)
    g0, g_mlp, g_mods1, g_gate_two0 = call(
        back_between_kernel,
        (shard, shard, six, vector),
        *terms,
        g_after,
        x1,
        mods[1],
        g_some,
        g_gate_two1,
        mods[0],
        mlp_out0,
        after=(attn_grads1,),
    )
    sum_a1 = scatter_rows(attn_grads1)
    terms, mlp_grads0, g_up_bias0 = mlp_backward(0, gather_plane(g_mlp), mlp0)
    g_after, g_attn, g_some = call(
        back_mlp_rows_kernel,
        (shard_wide, shard, three),
        *terms,
        g0,
        aft0,
        att0,
        mods[0],
        after=(mlp_grads0, sum_b1),
    )
    terms, attn_grads0, g_taps0 = attn_backward(0, g_attn, attn0)
    g_in, g_mods0 = call(
        back_end_kernel,
        (shard, six),
        *terms,
        g_after,
        x0,
        mods[0],
        g_some,
        g_gate_two0,
        after=(attn_grads0, sum_a1),
    )

    def finish(sum1, sum0):
        from_first = lax.ppermute(sum1.astype(BF16), "section", [(0, 1)])
        from_second = lax.ppermute(sum0.astype(BF16), "section", [(1, 0)])
        return jnp.where(first, sum0, sum1), jnp.where(first, from_second, from_first)

    mine, received = finish(sum_b1, scatter_rows(mlp_grads0))
    pair_b = choose((mine, received.astype(F32)))
    end = 2 * main + left
    grad_up = [g[:, :main] for g in pair_b] + [g[:, 2 * main : end] for g in pair_b]
    grad_up = jnp.concatenate(grad_up, axis=1)
    grad_down = [g[:, main : 2 * main].T for g in pair_b] + [g[:, end:].T for g in pair_b]
    grad_down = jnp.concatenate(grad_down, axis=0)
    grad_in, grad_gate, grad_out = call(
        functools.partial(unpack_attn_kernel, cfg),
        (
            out(in_weight.shape[1:], F32),
            out(gate_weight.shape[1:], F32),
            out((slab, out_weight.shape[1]), F32),
        ),
        section,
        *finish(sum_a1, scatter_rows(attn_grads0)),
        scalars=1,
    )
    grad_out = grad_out.T

    g_mod = jnp.stack([g_mods0.reshape(images, -1), g_mods1.reshape(images, -1)])
    g_mod = g_mod.reshape(sections, images, tensors, -1).transpose(0, 2, 1, 3)
    columns = g_mod.shape[3]
    g_mod = g_mod.reshape(sections, tensors, images * columns)
    taps_rows = taps_count + 1

    def small_grads(g_taps, g_up_bias):
        return jnp.concatenate([g_taps[:taps_rows].reshape(-1), g_up_bias.reshape(-1)])

    g_small = jnp.stack([small_grads(g_taps0, g_up_bias0), small_grads(g_taps1, g_up_bias1)])
    to_tensor = (jnp.arange(tensors) == t)[None, :, None]
    g_small = jnp.where(to_tensor, g_small[:, None], 0.0)
    g_sent = jnp.concatenate([g_mod, g_small], axis=2).reshape(sections * tensors, -1)
    g_parts = lax.all_to_all(
        g_sent, ("section", "tensor"), split_axis=0, concat_axis=0, tiled=True
    )
    g_share = jnp.sum(g_parts[:, : images * columns], axis=0)
    small_parts = g_parts[:, images * columns :].reshape(sections, tensors, -1).sum(1)
    g_all = spread_over(jnp.concatenate([g_share, small_parts.reshape(-1)]), ("dp",))
    small_own = jnp.sum(g_all[:, images * columns :], axis=0).reshape(sections, -1)
    g_all = g_all[:, : images * columns].reshape(dps * images, columns).astype(BF16)
    grad_ada_bias = jnp.sum(g_all.astype(F32), axis=0)
    grad_ada = jnp.einsum("md,me->de", slab_active, g_all, preferred_element_type=F32)
    act_part = jnp.einsum("me,de->md", g_all, ada_weight[0], preferred_element_type=F32)
    act_all = lax.all_to_all(
        act_part.reshape(dps, images, slab), "dp", split_axis=0, concat_axis=0, tiled=True
    )
    act_all = jnp.sum(spread_over(act_all, ("section", "tensor")), axis=0)
    act_grad = act_all.reshape(dps, images, slab).transpose(1, 0, 2).reshape(images, width)
    cond_grad = jax.vjp(jax.nn.silu, cond_vec)[1](act_grad)[0]

    small_taps = small_own[:, : taps_rows * wide].reshape(sections, taps_rows, wide)
    grad_gateb = small_taps[:, taps_count, tail : tail + heads].reshape(-1)
    grad_taps = small_taps[:, :taps_count, :channels].transpose(1, 0, 2)
    grad_taps = grad_taps.reshape(taps_count, sections * channels)
    up_halves = small_own[:, taps_rows * wide :]
    grad_up_bias = jnp.concatenate(
        [up_halves[:, :main].reshape(-1), up_halves[:, main : main + left].reshape(-1)]
    )

    ends_from_first = lax.ppermute(block_out, "section", [(0, 1)])
    ends_from_second = lax.ppermute(g_in, "section", [(1, 0)])
    mine = jnp.where(first, g_in, block_out)
    received = jnp.where(first, ends_from_second, ends_from_first)
    section_ends = jnp.concatenate(
        [jnp.where(first, mine, received), jnp.where(first, received, mine)], axis=1
    )
    return (
        section_ends[None],
        cond_grad,
        grad_ada[None],
        grad_ada_bias[None],
        grad_in[None],
        grad_gate[None],
        grad_gateb[None],
        grad_taps[None],
        grad_out[None],
        grad_up[None],
        grad_up_bias[None],
        grad_down[None],
    )


def solution(mesh):
    in_specs = (
        P("section", "dp", "tensor", None),
        P("dp", None),
        P("dp"),
        P("section", "dp", "tensor"),
        P("section", "tensor"),
        P("section", None, "dp", "tensor"),
        P("section", "dp", "tensor"),
        P("section", "tensor"),
        P("section", None, "tensor"),
        P("section", "tensor", "dp"),
        P("section", "dp", "tensor"),
        P("section", "tensor"),
        P("section", "tensor", "dp"),
    )
    out_specs = (
        P("section", "dp", "tensor", None),
        P("dp", None),
        P("section", "dp", "tensor"),
        P("section", "tensor"),
        P("section", None, "dp", "tensor"),
        P("section", "dp", "tensor"),
        P("section", "tensor"),
        P("section", None, "tensor"),
        P("section", "tensor", "dp"),
        P("section", "dp", "tensor"),
        P("section", "tensor"),
        P("section", "tensor", "dp"),
    )
    return jax.shard_map(
        per_device, mesh=mesh, in_specs=in_specs, out_specs=out_specs, check_vma=False
    )
```

```python
import functools
import math

import jax
import jax.numpy as jnp
from jax import lax
from jax.experimental import pallas as pl
from jax.experimental.pallas import tpu as pltpu
from jax.sharding import PartitionSpec as P

SIDE = 16
PATCHES = SIDE * SIDE
LANES = 128
F32 = jnp.float32
BF16 = jnp.bfloat16
HIGHEST = lax.Precision.HIGHEST
PLANE = ("tensor", "section")


class Traffic:
    def __init__(self, arriving, leaving):
        self.arriving, self.leaving, self.left = arriving, leaving, set()

    def wait(self, *places):
        for at in places:
            self.arriving[at].wait()

    def flush(self, *places):
        for at in places:
            self.leaving[at].start()
            self.left.add(at)


def call(body, outs, *args, scalars=0, flops=0, scratch=(), after=(), streamed=(), saved=()):
    count, waits, many = len(args), len(after), len(outs)
    moving = bool(streamed or saved)

    def kernel(*refs):
        ins, out_refs = list(refs[:count]), list(refs[count + waits : count + waits + many])
        rest = refs[count + waits + many :]
        own, held = rest[: len(scratch)], rest[len(scratch) :]
        arriving, leaving = {}, {}
        for i, at in enumerate(streamed):
            arriving[at] = pltpu.make_async_copy(ins[at], held[i], held[-1].at[i])
            ins[at] = held[i]
        for i, at in enumerate(saved, len(streamed)):
            leaving[at] = pltpu.make_async_copy(held[i], out_refs[at], held[-1].at[i])
            out_refs[at] = held[i]
        traffic = Traffic(arriving, leaving)
        for copy in arriving.values():
            copy.start()
        if moving:
            body(traffic, *ins, *out_refs, *own)
        else:
            body(*ins, *out_refs, *own)
        traffic.flush(*[at for at in saved if at not in traffic.left])
        for copy in leaving.values():
            copy.wait()

    moved = sum(a.size * a.dtype.itemsize for a in args)
    moved += sum(math.prod(o.shape) * o.dtype.itemsize for o in outs)
    specs = [pl.BlockSpec(memory_space=pltpu.SMEM)] * scalars
    specs += [
        pl.BlockSpec(memory_space=pltpu.HBM if i in streamed else pltpu.VMEM)
        for i in range(scalars, count)
    ]
    large = [a.size > 2**17 for a in after]
    specs += [pl.BlockSpec(memory_space=pltpu.HBM if v else pl.ANY) for v in large]
    after = [
        pltpu.with_memory_space_constraint(a, pltpu.HBM) if v else a for a, v in zip(after, large)
    ]
    spaces = [pltpu.HBM if i in saved else pltpu.VMEM for i in range(many)]
    shapes = [
        pltpu.HBM(o.shape, o.dtype) if i in saved else o for i, o in enumerate(outs)
    ]
    args = [
        pltpu.with_memory_space_constraint(a, pltpu.HBM) if i in streamed else a
        for i, a in enumerate(args)
    ]
    hold = [pltpu.VMEM(args[i].shape, args[i].dtype) for i in streamed]
    hold += [pltpu.VMEM(outs[i].shape, outs[i].dtype) for i in saved]
    if moving:
        hold.append(pltpu.SemaphoreType.DMA((len(hold),)))
    return pl.pallas_call(
        kernel,
        out_shape=tuple(shapes),
        in_specs=specs,
        out_specs=tuple(pl.BlockSpec(memory_space=space) for space in spaces),
        scratch_shapes=[*scratch, *hold],
        compiler_params=pltpu.CompilerParams(vmem_limit_bytes=6 * 2**20 + moved * 3 // 2),
        cost_estimate=pl.CostEstimate(flops=flops, bytes_accessed=moved, transcendentals=0),
    )(*args, *after)


def out(shape, dtype):
    return jax.ShapeDtypeStruct(shape, dtype)


def mm(a, b):
    return lax.dot_general(a, b, (((1,), (0,)), ((), ())), preferred_element_type=F32)


def mm_nt(a, b):
    return lax.dot_general(a, b, (((1,), (1,)), ((), ())), preferred_element_type=F32)


def mm_tn(a, b):
    return lax.dot_general(a, b, (((0,), (0,)), ((), ())), preferred_element_type=F32)


def normalize(v):
    centered = v - jnp.mean(v, axis=-1, keepdims=True)
    scale = lax.rsqrt(jnp.mean(centered * centered, axis=-1, keepdims=True) + 1e-06)
    return centered * scale, scale


def norm_grad(hat, rstd, grad):
    inner = jnp.mean(grad * hat, axis=-1, keepdims=True)
    return rstd * (grad - jnp.mean(grad, axis=-1, keepdims=True) - hat * inner)


def gather_total(pieces):
    total = pieces[0][...].astype(F32)
    for piece in pieces[1:]:
        total = total + piece[...].astype(F32)
    return total


def rows_sum(v):
    return jnp.sum(v, axis=0, keepdims=True)


def gelu_terms(x):
    k = math.sqrt(2.0 / math.pi)
    th = jnp.tanh(k * (x + 0.044715 * x * x * x))
    value = 0.5 * x * (1.0 + th)
    slope = 0.5 * (1.0 + th) + 0.5 * x * (1.0 - th * th) * k * (1.0 + 3 * 0.044715 * x * x)
    return value, slope


def start_kernel(x_ref, mod_ref, n_ref):
    for m in range(x_ref.shape[0]):
        hat, _ = normalize(x_ref[m].astype(F32))
        n_ref[m] = (hat * (1.0 + mod_ref[m, 1:2]) + mod_ref[m, 0:1]).astype(BF16)


def add_kernel(a, b, c, d, recv, *outs):
    for j, own in enumerate((a, b, c, d)):
        outs[j][...] = (own[...].astype(F32) + recv[j].astype(F32)).astype(BF16)


def scale_rows_kernel(g_ref, mod_ref, o_ref):
    for m in range(g_ref.shape[0]):
        o_ref[m] = (mod_ref[m, 5:6] * g_ref[m].astype(F32)).astype(BF16)


def after_attn_kernel(traffic, p0, p1, p2, p3, x_ref, mod_ref, att_ref, aft_ref, n_ref):
    for m in range(x_ref.shape[0]):
        att = gather_total([p.at[m] for p in (p0, p1, p2, p3)])
        aft = x_ref[m].astype(F32) + mod_ref[m, 2:3] * att
        hat, _ = normalize(aft)
        att_ref[m] = att
        aft_ref[m] = aft
        n_ref[m] = (hat * (1.0 + mod_ref[m, 4:5]) + mod_ref[m, 3:4]).astype(BF16)


def between_kernel(traffic, p0, p1, p2, p3, aft_ref, mod_ref, next_ref, mlp_ref, x_ref, n_ref):
    for m in range(aft_ref.shape[0]):
        mlp = gather_total([p.at[m] for p in (p0, p1, p2, p3)])
        x = (aft_ref[m] + mod_ref[m, 5:6] * mlp).astype(BF16)
        hat, _ = normalize(x.astype(F32))
        mlp_ref[m] = mlp
        x_ref[m] = x
        n_ref[m] = (hat * (1.0 + next_ref[m, 1:2]) + next_ref[m, 0:1]).astype(BF16)


def end_kernel(p0, p1, p2, p3, aft_ref, mod_ref, g_ref, more_ref, x_ref, gm_ref):
    for m in range(aft_ref.shape[0]):
        mlp = gather_total([p.at[m] for p in (p0, p1, p2, p3)])
        x_ref[m] = (aft_ref[m] + mod_ref[m, 5:6] * mlp).astype(BF16)
        gm_ref[m, 0:5] = more_ref[m]
        gm_ref[m, 5:6] = rows_sum(g_ref[m].astype(F32) * mlp)


def back_mlp_rows_kernel(traffic, p0, p1, p2, p3, g_ref, aft_ref, att_ref, mod_ref, ga_ref, gt_ref, gm_ref):
    for m in range(aft_ref.shape[0]):
        gn = gather_total([p.at[m] for p in (p0, p1, p2, p3)])
        hat, rstd = normalize(aft_ref[m])
        grad = g_ref[m].astype(F32) + norm_grad(hat, rstd, gn * (1.0 + mod_ref[m, 4:5]))
        ga_ref[m] = grad
        gt_ref[m] = (mod_ref[m, 2:3] * grad).astype(BF16)
        gm_ref[m, 0:1] = rows_sum(grad * att_ref[m])
        gm_ref[m, 1:2] = rows_sum(gn)
        gm_ref[m, 2:3] = rows_sum(gn * hat)


def back_attn_rows(pieces, ga_ref, x_ref, mod_ref, some_ref, gm_ref, m):
    gn = gather_total([p.at[m] for p in pieces])
    hat, rstd = normalize(x_ref[m].astype(F32))
    grad = ga_ref[m] + norm_grad(hat, rstd, gn * (1.0 + mod_ref[m, 1:2]))
    gm_ref[m, 0:1] = rows_sum(gn)
    gm_ref[m, 1:2] = rows_sum(gn * hat)
    gm_ref[m, 2:5] = some_ref[m]
    return grad.astype(BF16)


def back_between_kernel(
    p0, p1, p2, p3, ga_ref, x_ref, mod_ref, some_ref, prev_ref, mlp_ref, g_ref, gmlp_ref, gm_ref, gate_ref
):
    for m in range(x_ref.shape[0]):
        grad = back_attn_rows((p0, p1, p2, p3), ga_ref, x_ref, mod_ref, some_ref, gm_ref, m)
        g_ref[m] = grad
        wide = grad.astype(F32)
        gmlp_ref[m] = (prev_ref[m, 5:6] * wide).astype(BF16)
        gate_ref[m] = rows_sum(wide * mlp_ref[m])


def back_end_kernel(p0, p1, p2, p3, ga_ref, x_ref, mod_ref, some_ref, gate_ref, g_ref, gm_ref):
    for m in range(x_ref.shape[0]):
        g_ref[m] = back_attn_rows((p0, p1, p2, p3), ga_ref, x_ref, mod_ref, some_ref, gm_ref, m)
        gm_ref[m, 5:6] = gate_ref[m]


def scan_mask(columns_first):
    def place(number):
        if columns_first:
            return (number % SIDE) * SIDE + number // SIDE
        return number

    shape = (PATCHES, PATCHES)
    later = place(lax.broadcasted_iota(jnp.int32, shape, 0))
    return later >= place(lax.broadcasted_iota(jnp.int32, shape, 1))


def grid_column():
    return lax.broadcasted_iota(jnp.int32, (PATCHES, 1), 0) % SIDE


def side_shifts(a, column):
    left = jnp.where(column == 0, 0.0, pltpu.roll(a, 1, 0))
    right = jnp.where(column == SIDE - 1, 0.0, pltpu.roll(a, PATCHES - 1, 0))
    return left, a, right


def convolve(shifted, tap):
    sums = []
    for row in range(3):
        terms = [shifted[col] * tap(3 * row + col) for col in range(3)]
        sums.append(terms[0] + terms[1] + terms[2])
    zeros = jnp.zeros((SIDE, sums[0].shape[1]), F32)
    above = jnp.concatenate([zeros, sums[0][:-SIDE]], axis=0)
    below = jnp.concatenate([sums[2][SIDE:], zeros], axis=0)
    return shifted[1] + sums[1] + above + below


def tap_grads(shifted, grad):
    found = []
    for row in range(3):
        for col in range(3):
            if row == 0:
                product = shifted[col][:-SIDE] * grad[SIDE:]
            elif row == 1:
                product = shifted[col] * grad
            else:
                product = shifted[col][SIDE:] * grad[:-SIDE]
            found.append(rows_sum(product))
    return found


def lane_sets(width, first, head_width, heads):
    lane = lax.broadcasted_iota(jnp.int32, (1, width), 1)
    return [
        (lane >= first + h * head_width) & (lane < first + (h + 1) * head_width)
        for h in range(heads)
    ]


def decay_parts(logits, mask, gate_lane, heads):
    rates = -(jnp.maximum(logits, 0.0) + jnp.log1p(jnp.exp(-jnp.abs(logits))))
    ones = jnp.where(mask, 1.0, 0.0)
    totals = lax.dot_general(
        ones, rates, (((1,), (0,)), ((), ())), precision=HIGHEST, preferred_element_type=F32
    )
    turned = totals.T
    decays = []
    for h in range(heads):
        at = gate_lane + h
        spans = jnp.where(mask, totals[:, at : at + 1] - turned[at : at + 1, :], -1e30)
        w = jnp.exp(spans)
        decays.append((w, jnp.sum(w, axis=1, keepdims=True)))
    return decays, ones


def send_order(k):
    return (0, 1, None, None, 2, 3, None, None)[k], (None, None, 0, 1, None, None, 2, 3)[k]


def write_pieces(me, total_ref, other_ref, own_refs):
    rows = total_ref.shape[1] // 8
    for k in range(8):
        spot = pl.ds(pl.multiple_of(jnp.bitwise_xor(me, k) * rows, rows), rows)
        own, other = send_order(k)
        if own is None:
            other_ref[other] = total_ref[:, spot, :]
        else:
            own_refs[own][...] = total_ref[:, spot, :]


def each_shard(refs):
    own, x, y, xy, core, core_x, core_y, core_xy = refs
    return own, x, core, core_x, y, xy, core_y, core_xy


def gather_pieces(me, shard_refs, full_ref):
    rows = full_ref.shape[1] // 8
    for k, shard in enumerate(each_shard(shard_refs)):
        spot = pl.ds(pl.multiple_of(jnp.bitwise_xor(me, k) * rows, rows), rows)
        full_ref[:, spot, :] = shard[...]


def tail_spots(heads):
    return (0, 32, 48, 64, 80)


def join_tail(packed, piece, tails, lane):
    tile = packed[:, piece * LANES : (piece + 1) * LANES]
    return jnp.concatenate([tile, pltpu.roll(tails, (LANES - lane) % LANES, 1)], axis=1)


def lanes():
    return lax.broadcasted_iota(jnp.int32, (1, LANES), 1)


def half_tiles(tiles, at):
    if at == 0:
        return tiles[0], tiles[1]
    shift = 2 * LANES - at
    first = jnp.where(lanes() < shift, pltpu.roll(tiles[1], shift, 1), pltpu.roll(tiles[2], shift, 1))
    return first, pltpu.roll(tiles[2], shift, 1)


def pack_kernel(cfg, sec_ref, in_ref, gate_ref, out_ref, up_ref, down_ref, keep_ref, send_ref, keep_b_ref, send_b_ref):
    heads, channels, main, left = cfg
    spots = tail_spots(heads)
    tail = channels - LANES
    rows = in_ref.shape[1]
    short = jnp.zeros((rows, 3 * LANES - 2 * channels), F32)
    keep_first = sec_ref[0] == 0
    lane = lanes()
    tails = [gate_ref[...], pltpu.roll(gate_ref[...], LANES - heads, 1)]
    tails = [
        jnp.where((lane >= tail) & (lane < tail + heads), pltpu.roll(v, tail, 1), 0.0) for v in tails
    ]
    for j in range(5):
        ref = out_ref if j == 4 else in_ref.at[j]
        tiles = [ref[:, :LANES].astype(F32), ref[:, LANES : 2 * LANES].astype(F32)]
        tiles.append(jnp.concatenate([ref[:, 2 * LANES :].astype(F32), short], axis=1))
        whole = []
        for h in range(2):
            tile, rest = half_tiles(tiles, h * channels)
            whole.append(tile)
            tails[h] = tails[h] + pltpu.roll(jnp.where(lane < tail, rest, 0.0), spots[j], 1)
        cols = slice(j * LANES, (j + 1) * LANES)
        keep_ref[:, cols] = jnp.where(keep_first, whole[0], whole[1]).astype(BF16)
        send_ref[:, cols] = jnp.where(keep_first, whole[1], whole[0]).astype(BF16)
    cols = slice(5 * LANES, 6 * LANES)
    keep_ref[:, cols] = jnp.where(keep_first, tails[0], tails[1]).astype(BF16)
    send_ref[:, cols] = jnp.where(keep_first, tails[1], tails[0]).astype(BF16)
    at = 0
    for ref in (up_ref, down_ref):
        low, high = ref[:, :main], ref[:, main : 2 * main]
        keep_b_ref[:, at : at + main] = jnp.where(keep_first, low, high)
        send_b_ref[:, at : at + main] = jnp.where(keep_first, high, low)
        at += main
    up, down = (ref[:, 2 * main :].astype(F32) for ref in (up_ref, down_ref))
    low = jnp.where(lane < left, up, pltpu.roll(down, left, 1)).astype(BF16)
    high = jnp.where(lane < left, pltpu.roll(up, left, 1), down).astype(BF16)
    keep_b_ref[:, at:] = jnp.where(keep_first, low, high)
    send_b_ref[:, at:] = jnp.where(keep_first, high, low)


def unpack_attn_kernel(cfg, sec_ref, mine_ref, recv_ref, in_ref, gate_ref, out_ref):
    heads, channels = cfg
    spots = tail_spots(heads)
    tail = channels - LANES
    mine_first = sec_ref[0] == 0
    lane = lanes()
    shift = channels - LANES

    def both(cols):
        mine, recv = mine_ref[:, cols].astype(F32), recv_ref[:, cols].astype(F32)
        return jnp.where(mine_first, mine, recv), jnp.where(mine_first, recv, mine)

    low_tails, high_tails = both(slice(5 * LANES, 6 * LANES))
    for j in range(5):
        ref = out_ref if j == 4 else in_ref.at[j]
        low, high = both(slice(j * LANES, (j + 1) * LANES))
        ref[:, :LANES] = low
        high = pltpu.roll(high, shift, 1)
        low_tail = pltpu.roll(low_tails, (LANES - spots[j]) % LANES, 1)
        high_tail = pltpu.roll(high_tails, (LANES - spots[j] + shift) % LANES, 1)
        ref[:, LANES : 2 * LANES] = jnp.where(lane < tail, low_tail, high)
        last = jnp.where(lane < shift, high, high_tail)
        ref[:, 2 * LANES :] = last[:, : 2 * channels - 2 * LANES]
    low_gate = pltpu.roll(low_tails, LANES - tail, 1)
    high_gate = pltpu.roll(high_tails, LANES - tail + heads, 1)
    gate_ref[...] = jnp.where(lane < heads, low_gate, high_gate)[:, : 2 * heads]


def attn_forward_kernel(cfg, traffic, me_ref, *refs):
    columns_first, heads, head_width = cfg
    shards, (w_ref, gb_ref, tap_ref) = refs[:8], refs[8:11]
    n_ref, proj_ref, log_ref, attn_ref, mix_ref, other_ref = refs[11:17]
    own_refs, total_ref = refs[17:21], refs[21]
    me = me_ref[0]
    wide = 2 * LANES
    gate_lane = heads * head_width - LANES
    spots = tail_spots(heads)
    mask = scan_mask(columns_first)
    column = grid_column()
    sets = lane_sets(wide, 0, head_width, heads)
    gather_pieces(me, shards, n_ref)
    traffic.flush(0)
    traffic.wait(9)
    for m in range(n_ref.shape[0]):
        projected = mm(n_ref[m], w_ref[:, : 4 * LANES])
        tails = mm(n_ref[m], w_ref[:, 5 * LANES :])
        logits = tails + gb_ref[...]
        log_ref[m] = logits
        decays, _ = decay_parts(logits, mask, gate_lane, heads)
        query, key, value, gate = (join_tail(projected, j, tails, spots[j]) for j in range(4))
        in_head = sets[0]
        for own in sets[1:]:
            in_head = in_head | own
        query, key, value = (jnp.where(in_head, v, 0.0).astype(BF16) for v in (query, key, value))
        gate = gate.astype(BF16)
        for j, v in enumerate((query, key, value, gate)):
            proj_ref[m, :, j * wide : (j + 1) * wide] = v
        attn = None
        for h in range(heads):
            w, mass = decays[h]
            raw = mm_nt(jnp.where(sets[h], query, jnp.zeros_like(query)), key)
            scores = (raw * head_width ** (-0.5) * w).astype(BF16)
            normed = mm(scores, value) * lax.rsqrt(mass)
            attn = jnp.where(sets[h], normed, 0.0 if attn is None else attn)
        attn_ref[m] = attn
        spread = convolve(side_shifts(attn, column), lambda i: tap_ref[i : i + 1, :])
        gate = gate.astype(F32)
        mixed = spread * (gate * jax.nn.sigmoid(gate))
        mixed = jnp.where(in_head, mixed, 0.0)
        mixed = jnp.concatenate(
            [mixed[:, :LANES], pltpu.roll(mixed[:, LANES:], spots[4], 1)], axis=1
        ).astype(BF16)
        mix_ref[m] = mixed
        if m == n_ref.shape[0] - 1:
            traffic.flush(1, 2, 3, 4)
        total_ref[m] = mm_nt(mixed, w_ref[:, 4 * LANES :]).astype(BF16)
    write_pieces(me, total_ref, other_ref, own_refs)


def attn_backward_kernel(cfg, traffic, me_ref, *refs):
    columns_first, heads, head_width = cfg
    shards, (proj_ref, log_ref, attn_ref, w_ref, tap_ref) = refs[:8], refs[8:13]
    g_ref, gproj_ref, gtap_ref, other_ref = refs[13:17]
    own_refs, total_ref = refs[17:21], refs[21]
    me = me_ref[0]
    wide = 2 * LANES
    gate_lane = heads * head_width - LANES
    spots = tail_spots(heads)
    scale = head_width ** (-0.5)
    mask = scan_mask(columns_first)
    column = grid_column()
    sets = lane_sets(wide, 0, head_width, heads)
    gate_sets = lane_sets(LANES, gate_lane, 1, heads)
    sublane = lax.broadcasted_iota(jnp.int32, (LANES, 1), 0)
    in_head = sets[0]
    for own in sets[1:]:
        in_head = in_head | own
    gather_pieces(me, shards, g_ref)
    gtap_ref[...] = jnp.zeros(gtap_ref.shape, F32)
    traffic.wait(9, 10, 11, 12)
    for m in range(g_ref.shape[0]):
        g_packed = mm(g_ref[m], w_ref[:, 4 * LANES :])
        g_mixed = jnp.where(in_head, join_tail(g_packed, 0, g_packed[:, LANES:], spots[4]), 0.0)
        query, key, value, gate = (proj_ref[m, :, j * wide : (j + 1) * wide] for j in range(4))
        gate = gate.astype(F32)
        sig = jax.nn.sigmoid(gate)
        attn = attn_ref[m]
        shifted = side_shifts(attn, column)
        spread = convolve(shifted, lambda i: tap_ref[i : i + 1, :])
        g_spread = g_mixed * (gate * sig)
        g_gate = g_mixed * spread * (sig * (1.0 + gate * (1.0 - sig)))
        for i, grad in enumerate(tap_grads(shifted, g_spread)):
            gtap_ref[i : i + 1, :] = grad if m == 0 else gtap_ref[i : i + 1, :] + grad
        g_attn = convolve(side_shifts(g_spread, column), lambda i: tap_ref[8 - i : 9 - i, :])
        logits = log_ref[m]
        decays, ones = decay_parts(logits, mask, gate_lane, heads)
        g_query = g_key = g_value = 0.0
        across = jnp.zeros((PATCHES, LANES), F32)
        down = jnp.zeros((LANES, PATCHES), F32)
        for h in range(heads):
            w, mass = decays[h]
            own_query = jnp.where(sets[h], query, jnp.zeros_like(query))
            raw = mm_nt(own_query, key) * scale
            own_grad = jnp.where(sets[h], g_attn, 0.0)
            g_mass = -0.5 * jnp.sum(own_grad * attn, axis=1, keepdims=True) / mass
            g_out = (own_grad * lax.rsqrt(mass)).astype(BF16)
            g_value = g_value + mm_tn((raw * w).astype(BF16), g_out)
            g_scores = mm_nt(g_out, value)
            g_raw = (g_scores * w * scale).astype(BF16)
            g_query = jnp.where(sets[h], mm(g_raw, key), g_query)
            g_key = g_key + mm_tn(g_raw, own_query)
            g_span = (g_scores * raw + g_mass) * w
            across = jnp.where(gate_sets[h], jnp.sum(g_span, axis=1, keepdims=True), across)
            down = jnp.where(sublane == gate_lane + h, rows_sum(g_span), down)
        g_rates = lax.dot_general(
            ones,
            across - down.T,
            (((0,), (0,)), ((), ())),
            precision=HIGHEST,
            preferred_element_type=F32,
        )
        g_logits = (-g_rates * jax.nn.sigmoid(logits)).astype(BF16).astype(F32)
        g_bias = rows_sum(g_logits)
        gtap_ref[9:10, :LANES] = g_bias if m == 0 else gtap_ref[9:10, :LANES] + g_bias
        tails = g_logits
        for j, v in enumerate((g_query, g_key, g_value, g_gate)):
            gproj_ref[m, :, j * LANES : (j + 1) * LANES] = v[:, :LANES].astype(BF16)
            tails = tails + pltpu.roll(v[:, LANES:], spots[j], 1)
        gproj_ref[m, :, 4 * LANES :] = tails.astype(BF16)
        total = mm_nt(gproj_ref[m, :, : 4 * LANES], w_ref[:, : 4 * LANES])
        total = total + mm_nt(gproj_ref[m, :, 4 * LANES :], w_ref[:, 5 * LANES :])
        total_ref[m] = total.astype(BF16)
    write_pieces(me, total_ref, other_ref, own_refs)


def attn_weights_kernel(traffic, n_ref, gproj_ref, g_ref, mix_ref, gw_ref):
    traffic.wait(0, 3)
    for part in range(2):
        cols = slice(part * 2 * LANES, (part + 1) * 2 * LANES)
        total = mm_tn(n_ref[0], gproj_ref[0, :, cols])
        for m in range(1, n_ref.shape[0]):
            total = total + mm_tn(n_ref[m], gproj_ref[m, :, cols])
        gw_ref[:, cols] = total.astype(BF16)
    total = mm_tn(g_ref[0], mix_ref[0])
    tails = mm_tn(n_ref[0], gproj_ref[0, :, 4 * LANES :])
    for m in range(1, n_ref.shape[0]):
        total = total + mm_tn(g_ref[m], mix_ref[m])
        tails = tails + mm_tn(n_ref[m], gproj_ref[m, :, 4 * LANES :])
    gw_ref[:, 4 * LANES : 5 * LANES] = total[:, :LANES].astype(BF16)
    gw_ref[:, 5 * LANES :] = (total[:, LANES:] + tails).astype(BF16)


def stack_shards(shards, full_ref):
    for k, shard in enumerate(each_shard(shards)):
        images, rows, width = shard.shape
        full_ref[k * images * rows : (k + 1) * images * rows, :] = shard[...].reshape(
            images * rows, width
        )


def stack_kernel(traffic, *refs):
    stack_shards(refs[:8], refs[8])


def put_shard(k, value, shape, other_ref, own_refs):
    own, other = send_order(k)
    if own is None:
        other_ref[other] = value.astype(BF16).reshape(shape)
    else:
        own_refs[own][...] = value.astype(BF16).reshape(shape)


def put_shards(total, shape, other_ref, own_refs):
    rows = total.shape[0] // 8
    for k in range(8):
        put_shard(k, total[k * rows : (k + 1) * rows], shape, other_ref, own_refs)


def mlp_forward_kernel(left, traffic, *refs):
    shards, (w_ref, ub_ref) = refs[:8], refs[8:10]
    n_ref, pre_ref, hid_ref, other_ref = refs[10:14]
    own_refs = refs[14:18]
    main = (w_ref.shape[1] - LANES) // 2
    stack_shards(shards, n_ref)
    traffic.flush(0)
    traffic.wait(8)
    n = n_ref[...]
    pre = mm(n, w_ref[:, :main]) + ub_ref[:, :main]
    pre_ref[:, :main] = pre
    hidden = gelu_terms(pre)[0].astype(BF16)
    hid_ref[:, :main] = hidden
    last = mm(n, w_ref[:, 2 * main :]) + ub_ref[:, main:]
    pre_ref[:, main:] = last
    lane = lax.broadcasted_iota(jnp.int32, (1, LANES), 1)
    tail = jnp.where(lane < left, gelu_terms(last)[0], 0.0)
    tail = pltpu.roll(tail, LANES - left, 1).astype(BF16)
    hid_ref[:, main:] = tail
    traffic.flush(1, 2)
    total = mm_nt(hidden, w_ref[:, main : 2 * main]) + mm_nt(tail, w_ref[:, 2 * main :])
    put_shards(total, shards[0].shape, other_ref, own_refs)


def mlp_backward_kernel(left, traffic, *refs):
    count = 1 if len(refs) == 10 else 8
    given, (pre_ref, w_ref) = refs[:count], refs[count : count + 2]
    rest = refs[count + 2 :]
    if count == 8:
        g_ref, rest = rest[0], rest[1:]
        stack_shards(given, g_ref)
        traffic.wait(8, 9)
    else:
        g_ref = given[0]
        traffic.wait(0, 1, 2)
    gpre_ref, gub_ref, other_ref = rest[:3]
    own_refs = rest[3:]
    main = (w_ref.shape[1] - LANES) // 2
    g = g_ref[...]
    g_pre = mm(g, w_ref[:, main : 2 * main]) * gelu_terms(pre_ref[:, :main])[1]
    g_pre = g_pre.astype(BF16)
    gpre_ref[:, :main] = g_pre
    gub_ref[:, :main] = rows_sum(g_pre.astype(F32))
    lane = lax.broadcasted_iota(jnp.int32, (1, LANES), 1)
    last = pltpu.roll(mm(g, w_ref[:, 2 * main :]), left, 1) * gelu_terms(pre_ref[:, main:])[1]
    last = jnp.where(lane < left, last, 0.0).astype(BF16)
    gpre_ref[:, main:] = last
    gub_ref[:, main:] = rows_sum(last.astype(F32))
    total = mm_nt(g_pre, w_ref[:, :main]) + mm_nt(last, w_ref[:, 2 * main :])
    put_shards(total, own_refs[0].shape, other_ref, own_refs)


def mlp_weights_kernel(traffic, n_ref, gpre_ref, g_ref, hid_ref, gw_ref):
    main = gpre_ref.shape[1] - LANES
    traffic.wait(0, 3)
    gw_ref[:, :main] = mm_tn(n_ref[...], gpre_ref[:, :main]).astype(BF16)
    gw_ref[:, main : 2 * main] = mm_tn(g_ref[...], hid_ref[:, :main]).astype(BF16)
    last = mm_tn(n_ref[...], gpre_ref[:, main:]) + mm_tn(g_ref[...], hid_ref[:, main:])
    gw_ref[:, 2 * main :] = last.astype(BF16)


def swap(value, tensor_bits, section_bit):
    tensors, sections = lax.axis_size("tensor"), lax.axis_size("section")
    route = [
        (t * sections + s, (t ^ tensor_bits) * sections + (s ^ section_bit))
        for t in range(tensors)
        for s in range(sections)
    ]
    return lax.ppermute(value, PLANE, route)


def gather_plane(own):
    xy, x, y = swap(own, 2, 1), swap(own, 0, 1), swap(own, 2, 0)
    return own, x, y, xy, *(swap(v, 1, 0) for v in (own, x, y, xy))


def scatter_plane(other, own):
    received = swap(other, 1, 0)
    sums = call(add_kernel, (out(own[0].shape, BF16),) * 4, *own, received)
    return (sums[0], swap(sums[3], 2, 1), swap(sums[1], 0, 1), swap(sums[2], 2, 0))


def spread_over(value, axes):
    count = math.prod(lax.axis_size(a) for a in axes)
    copies = jnp.broadcast_to(value[None], (count,) + value.shape)
    return lax.all_to_all(copies, axes, split_axis=0, concat_axis=0, tiled=True)


def gather_all(own):
    return lax.all_gather(own, "dp", axis=0, tiled=True)


def scatter_rows(partial):
    return lax.psum_scatter(partial, "dp", scatter_dimension=0, tiled=True)


def sinusoid(time_steps, channels):
    half_width = channels // 2
    frequency = jnp.exp(
        jnp.arange(half_width, dtype=jnp.float32) * (-math.log(10000.0) / half_width)
    )
    angles = time_steps.astype(jnp.float32)[:, None] * frequency[None, :]
    return jnp.concatenate([jnp.cos(angles), jnp.sin(angles)], axis=1)


def per_device(
    section_inputs,
    condition,
    timesteps,
    ada_weight,
    ada_bias,
    in_weight,
    gate_weight,
    gate_bias,
    conv_taps,
    out_weight,
    up_weight,
    up_bias,
    down_weight,
):
    d = lax.axis_index("dp")
    t = lax.axis_index("tensor")
    s = lax.axis_index("section")
    dps, tensors, sections = (lax.axis_size(a) for a in ("dp", "tensor", "section"))
    first = s == 0
    me = (t * sections + s).astype(jnp.int32).reshape(1)
    images = condition.shape[0]
    width = condition.shape[1]
    slab = in_weight.shape[2]
    heads = gate_weight.shape[2] // sections
    channels = in_weight.shape[3] // sections
    head_width = channels // heads
    units = up_weight.shape[2] // sections
    wide = 2 * LANES
    tail = channels - LANES
    rows = section_inputs.shape[2] // sections
    main = units // LANES * LANES
    left = units - main
    spots = tail_spots(heads)

    def cut(value, axis):
        half = value.shape[axis] // 2
        return (
            lax.slice_in_dim(value, 0, half, axis=axis),
            lax.slice_in_dim(value, half, 2 * half, axis=axis),
        )

    def swap_halves(keep, send):
        received = lax.ppermute(send, "section", [(0, 1), (1, 0)])
        return jnp.where(first, keep, received), jnp.where(first, received, keep)

    def choose(pair):
        return jnp.where(first, pair[0], pair[1]), jnp.where(first, pair[1], pair[0])

    cfg = (heads, channels)
    section = s.astype(jnp.int32).reshape(1)
    shape_a, shape_b = (slab, 6 * LANES), (slab, 2 * main + LANES)
    kept_a, sent_a, kept_b, sent_b = call(
        functools.partial(pack_kernel, (*cfg, main, left)),
        (out(shape_a, BF16),) * 2 + (out(shape_b, BF16),) * 2,
        section,
        in_weight[0],
        jnp.pad(gate_weight[0].astype(F32), ((0, 0), (0, LANES - gate_weight.shape[2]))),
        out_weight[0].T,
        up_weight[0],
        down_weight[0].T,
        scalars=1,
    )
    sent_a, condition = lax.optimization_barrier((sent_a, condition))
    received_a = lax.ppermute(sent_a, "section", [(0, 1), (1, 0)])
    received_b = lax.ppermute(sent_b, "section", [(0, 1), (1, 0)])

    def unit_halves(value):
        rest = sections * main
        return tuple(
            (value[:, h * main : (h + 1) * main], value[:, rest + h * left : rest + (h + 1) * left])
            for h in (0, 1)
        )

    def pack_small(gate_half, taps_half, up_half):
        return jnp.concatenate([gate_half.reshape(-1), taps_half.reshape(-1), up_half.reshape(-1)])

    def pack_halves(pack, *pairs):
        return tuple(pack(*(pair[i] for pair in pairs)) for i in (0, 1))

    x_pair = cut(section_inputs[0], 1)
    x_received = lax.ppermute(
        jnp.where(first, x_pair[1], x_pair[0]), "section", [(0, 1), (1, 0)]
    )
    x0 = jnp.where(first, x_pair[0], x_received)
    g1 = jnp.where(first, x_received, x_pair[1])
    taps_count = conv_taps.shape[1]
    up_row = up_bias[0].astype(F32)[None]
    small = swap_halves(
        *choose(
            pack_halves(
                pack_small,
                cut(gate_bias[0].astype(F32), 0),
                cut(conv_taps[0].astype(F32), 1),
                tuple(jnp.concatenate(v, axis=1) for v in unit_halves(up_row)),
            )
        )
    )

    def unpack_small(packed):
        gate_row = jnp.pad(packed[:heads][None], ((0, 0), (tail, LANES - heads - tail)))
        taps = packed[heads : heads + taps_count * channels].reshape(taps_count, channels)
        taps = jnp.pad(taps, ((0, 16 - taps_count), (0, wide - channels)))
        up_row = packed[heads + taps_count * channels :][None]
        return gate_row, taps, jnp.pad(up_row, ((0, 0), (0, main + LANES - units)))

    cond_vec = condition + sinusoid(timesteps, width)
    activated = jax.nn.silu(cond_vec).astype(BF16)
    slab_active = activated.reshape(images, dps, slab).transpose(1, 0, 2)
    slab_active = lax.all_to_all(slab_active, "dp", split_axis=0, concat_axis=0, tiled=True)
    slab_active = slab_active.reshape(dps * images, slab)
    slab_active, received_a = lax.optimization_barrier((slab_active, received_a))
    mod_part = jnp.dot(slab_active, ada_weight[0], preferred_element_type=F32)
    mod_parts = lax.all_to_all(
        mod_part.reshape(dps, images, -1), "dp", split_axis=0, concat_axis=0, tiled=True
    )
    mod_share = jnp.sum(mod_parts, axis=0) + ada_bias[0].astype(F32)
    mod_all = spread_over(mod_share, ("section", "tensor"))
    received_b, mod_all = lax.optimization_barrier((received_b, mod_all))
    mod_all = mod_all.reshape(sections, tensors, images, -1).transpose(0, 2, 1, 3)
    mod_all = mod_all.reshape(sections, images, 6, width)
    mods = (mod_all[0], mod_all[1])

    shard = out((images, rows, width), BF16)
    shard_wide = out((images, rows, width), F32)
    vector = out((images, 1, width), F32)
    pieces_out = (out((4, images, rows, width), BF16),) + (shard,) * 4
    full = out((images, PATCHES, width), BF16)
    flat = out((images * PATCHES, width), BF16)
    total_rows = images * PATCHES
    kept = pltpu.VMEM((images, PATCHES, width), BF16)
    middle_flops = 2 * total_rows * PATCHES * wide * heads * 6
    attn_flops = 2 * total_rows * width * wide * 5 + middle_flops
    mlp_flops = 4 * total_rows * width * units

    def attn_forward(b, shards):
        w, _, gate_row, taps, _ = weights[b]
        body = functools.partial(attn_forward_kernel, (b == 1, heads, head_width))
        found = call(
            body,
            (
                full,
                out((images, PATCHES, 4 * wide), BF16),
                out((images, PATCHES, LANES), F32),
                out((images, PATCHES, wide), F32),
                out((images, PATCHES, wide), BF16),
                *pieces_out,
            ),
            me,
            *shards,
            w,
            gate_row,
            taps,
            scalars=1,
            flops=attn_flops,
            scratch=[kept],
            streamed=(9,),
            saved=(0, 1, 2, 3, 4),
        )
        return found[:5], scatter_plane(found[5], found[6:])

    def attn_backward(b, shards, saved, after=()):
        w, _, _, taps, _ = weights[b]
        body = functools.partial(attn_backward_kernel, (b == 1, heads, head_width))
        found = call(
            body,
            (
                full,
                out((images, PATCHES, 5 * LANES), BF16),
                out((16, wide), F32),
                *pieces_out,
            ),
            me,
            *shards,
            saved[1],
            saved[2],
            saved[3],
            w,
            taps,
            scalars=1,
            flops=2 * attn_flops,
            scratch=[kept],
            streamed=(9, 10, 11, 12),
            after=after,
        )
        terms = scatter_plane(found[3], found[4:])
        (grads,) = call(
            attn_weights_kernel,
            (out((width, 6 * LANES), BF16),),
            saved[0],
            found[1],
            found[0],
            saved[4],
            flops=2 * total_rows * width * wide * 5,
            after=terms if b else (),
            streamed=(0, 3),
            saved=(0,),
        )
        return terms, grads, found[2]

    def mlp_forward(b, normed, late):
        _, w, _, _, up_row = weights[b]
        found = call(
            functools.partial(mlp_forward_kernel, left),
            (
                flat,
                out((total_rows, main + LANES), F32),
                out((total_rows, main + LANES), BF16),
                *pieces_out,
            ),
            *gather_plane(normed),
            w,
            up_row,
            flops=mlp_flops,
            streamed=(8,),
            saved=tuple(range(8)) if late else (0, 1, 2),
        )
        return found[:3], found[3:]

    def mlp_backward(b, given, saved, after=()):
        _, w, _, _, _ = weights[b]
        gathered = len(given) == 1
        outs = (out((total_rows, main + LANES), BF16), out((1, main + LANES), F32), *pieces_out)
        found = call(
            functools.partial(mlp_backward_kernel, left),
            outs if gathered else (flat, *outs),
            *given,
            saved[1],
            w,
            flops=mlp_flops,
            streamed=(0, 1, 2) if gathered else (8, 9),
            after=after,
        )
        if gathered:
            found = (given[0], *found)
        terms = scatter_plane(found[3], found[4:])
        (grads,) = call(
            mlp_weights_kernel,
            (out((width, 2 * main + LANES), BF16),),
            saved[0],
            found[1],
            found[0],
            saved[2],
            flops=mlp_flops,
            after=() if b else terms,
            streamed=(0, 3),
            saved=(0,),
        )
        return terms, grads, found[2]

    def of_block(b, kept, received):
        return jnp.where(first == (b == 0), kept, received)

    full_a0 = gather_all(of_block(0, kept_a, received_a))
    full_b0 = gather_all(of_block(0, kept_b, received_b))
    (g_mlp,) = call(scale_rows_kernel, (shard,), g1, mods[1])
    (g_mlp1,) = call(stack_kernel, (flat,), *gather_plane(g_mlp), saved=(0,))
    (normed,) = call(start_kernel, (shard,), x0, mods[0])
    shards, g_mlp1, next_a, next_b = lax.optimization_barrier(
        (
            gather_plane(normed),
            g_mlp1,
            of_block(1, kept_a, received_a),
            of_block(1, kept_b, received_b),
        )
    )
    weights = [
        (full_a0, full_b0, *unpack_small(small[0])),
        (gather_all(next_a), gather_all(next_b), *unpack_small(small[1])),
    ]

    def to_second(value):
        return lax.ppermute(value, "section", [(0, 1)])

    def to_first(value):
        return lax.ppermute(value, "section", [(1, 0)])

    attn0, terms = attn_forward(0, shards)
    att0, aft0, normed = call(
        after_attn_kernel, (shard_wide, shard_wide, shard), *terms, x0, mods[0], saved=(0, 1)
    )
    mlp0, pieces = mlp_forward(0, normed, False)
    mlp_out0, x1, normed = call(
        between_kernel,
        (shard_wide, shard, shard),
        *scatter_plane(pieces[0], pieces[1:]),
        aft0,
        mods[0],
        mods[1],
        saved=(0, 1),
    )
    attn1, terms = attn_forward(1, gather_plane(normed))
    att1, aft1, normed = call(
        after_attn_kernel, (shard_wide, shard_wide, shard), *terms, x1, mods[1], saved=(0, 1)
    )
    mlp1, end_pieces = mlp_forward(1, normed, True)

    three, five, six = (out((images, n, width), F32) for n in (3, 5, 6))
    terms, mlp_grads1, g_up_bias1 = mlp_backward(1, (g_mlp1,), mlp1)
    g_after, g_attn, g_some = call(
        back_mlp_rows_kernel,
        (shard_wide, shard, three),
        *terms,
        g1,
        aft1,
        att1,
        mods[1],
        after=(mlp_grads1,),
        saved=(0,),
    )
    sum_b1 = scatter_rows(mlp_grads1)
    terms, attn_grads1, g_taps1 = attn_backward(1, gather_plane(g_attn), attn1)
    g0, g_mlp, g_more, g_gate_two0 = call(
        back_between_kernel,
        (shard, shard, five, vector),
        *terms,
        g_after,
        x1,
        mods[1],
        g_some,
        mods[0],
        mlp_out0,
    )
    sum_a1 = scatter_rows(attn_grads1)
    terms, mlp_grads0, g_up_bias0 = mlp_backward(0, gather_plane(g_mlp), mlp0, (attn_grads1,))
    g_after, g_attn, g_some = call(
        back_mlp_rows_kernel,
        (shard_wide, shard, three),
        *terms,
        g0,
        aft0,
        att0,
        mods[0],
        after=(sum_b1,),
        saved=(0,),
    )
    shards, sum_b1, sum_a1 = lax.optimization_barrier((gather_plane(g_attn), sum_b1, sum_a1))
    terms, attn_grads0, g_taps0 = attn_backward(0, shards, attn0, (mlp_grads0,))
    other_b1, other_a1 = to_second(sum_b1), to_second(sum_a1)
    g_in, g_mods0 = call(
        back_end_kernel,
        (shard, six),
        *terms,
        g_after,
        x0,
        mods[0],
        g_some,
        g_gate_two0,
        after=(attn_grads0, other_b1, other_a1),
    )

    sum_b0, sum_a0 = scatter_rows(mlp_grads0), scatter_rows(attn_grads0)

    end_pieces, g_mods0 = lax.optimization_barrier((end_pieces, g_mods0))
    block_out, g_mods1 = call(
        end_kernel,
        (shard, six),
        *scatter_plane(end_pieces[0], end_pieces[1:]),
        aft1,
        mods[1],
        g1,
        g_more,
    )

    g_mod = jnp.stack([g_mods0.reshape(images, -1), g_mods1.reshape(images, -1)])
    g_mod = g_mod.reshape(sections, images, tensors, -1).transpose(0, 2, 1, 3)
    columns = g_mod.shape[3]
    g_mod = g_mod.reshape(sections, tensors, images * columns)
    taps_rows = taps_count + 1

    def small_grads(g_taps, g_up_bias):
        return jnp.concatenate([g_taps[:taps_rows].reshape(-1), g_up_bias.reshape(-1)])

    g_small = jnp.stack([small_grads(g_taps0, g_up_bias0), small_grads(g_taps1, g_up_bias1)])
    to_tensor = (jnp.arange(tensors) == t)[None, :, None]
    g_small = jnp.where(to_tensor, g_small[:, None], 0.0)
    g_sent = jnp.concatenate([g_mod, g_small], axis=2).reshape(sections * tensors, -1)
    g_parts = lax.all_to_all(
        g_sent, ("section", "tensor"), split_axis=0, concat_axis=0, tiled=True
    )
    block_out, sum_b0 = lax.optimization_barrier((block_out, sum_b0))
    other_b0 = to_first(sum_b0)
    g_share = jnp.sum(g_parts[:, : images * columns], axis=0)
    small_parts = g_parts[:, images * columns :].reshape(sections, tensors, -1).sum(1)
    g_all = spread_over(jnp.concatenate([g_share, small_parts.reshape(-1)]), ("dp",))
    small_own = jnp.sum(g_all[:, images * columns :], axis=0).reshape(sections, -1)
    g_all = g_all[:, : images * columns].reshape(dps * images, columns).astype(BF16)
    grad_ada_bias = jnp.sum(g_all.astype(F32), axis=0)
    grad_ada = jnp.einsum("md,me->de", slab_active, g_all, preferred_element_type=F32)
    act_part = jnp.einsum("me,de->md", g_all, ada_weight[0], preferred_element_type=F32)
    act_part, other_b0, sum_a0 = lax.optimization_barrier((act_part, other_b0, sum_a0))
    act_all = lax.all_to_all(
        act_part.reshape(dps, images, slab), "dp", split_axis=0, concat_axis=0, tiled=True
    )
    act_all = jnp.sum(spread_over(act_all, ("section", "tensor")), axis=0)
    act_grad = act_all.reshape(dps, images, slab).transpose(1, 0, 2).reshape(images, width)
    cond_grad = jax.vjp(jax.nn.silu, cond_vec)[1](act_grad)[0]

    small_taps = small_own[:, : taps_rows * wide].reshape(sections, taps_rows, wide)
    grad_gateb = small_taps[:, taps_count, tail : tail + heads].reshape(-1)
    grad_taps = small_taps[:, :taps_count, :channels].transpose(1, 0, 2)
    grad_taps = grad_taps.reshape(taps_count, sections * channels)
    up_halves = small_own[:, taps_rows * wide :]
    grad_up_bias = jnp.concatenate(
        [up_halves[:, :main].reshape(-1), up_halves[:, main : main + left].reshape(-1)]
    )

    mine_b = jnp.where(first, sum_b0, sum_b1)
    received = jnp.where(first, other_b0, other_b1)
    pair_b = choose((mine_b.astype(F32), received.astype(F32)))
    end = 2 * main + left
    grad_up = [g[:, :main] for g in pair_b] + [g[:, 2 * main : end] for g in pair_b]
    grad_up = jnp.concatenate(grad_up, axis=1)
    grad_down = [g[:, main : 2 * main].T for g in pair_b] + [g[:, end:].T for g in pair_b]
    grad_down = jnp.concatenate(grad_down, axis=0)
    grad_in, grad_gate, grad_out = call(
        functools.partial(unpack_attn_kernel, cfg),
        (
            out(in_weight.shape[1:], F32),
            out(gate_weight.shape[1:], F32),
            out((slab, out_weight.shape[1]), F32),
        ),
        section,
        jnp.where(first, sum_a0, sum_a1),
        jnp.where(first, to_first(sum_a0), other_a1),
        scalars=1,
    )
    grad_out = grad_out.T

    ends_from_first = lax.ppermute(block_out, "section", [(0, 1)])
    ends_from_second = lax.ppermute(g_in, "section", [(1, 0)])
    mine = jnp.where(first, g_in, block_out)
    received = jnp.where(first, ends_from_second, ends_from_first)
    section_ends = jnp.concatenate(
        [jnp.where(first, mine, received), jnp.where(first, received, mine)], axis=1
    )
    return (
        section_ends[None],
        cond_grad,
        grad_ada[None],
        grad_ada_bias[None],
        grad_in[None],
        grad_gate[None],
        grad_gateb[None],
        grad_taps[None],
        grad_out[None],
        grad_up[None],
        grad_up_bias[None],
        grad_down[None],
    )


def solution(mesh):
    in_specs = (
        P("section", "dp", "tensor", None),
        P("dp", None),
        P("dp"),
        P("section", "dp", "tensor"),
        P("section", "tensor"),
        P("section", None, "dp", "tensor"),
        P("section", "dp", "tensor"),
        P("section", "tensor"),
        P("section", None, "tensor"),
        P("section", "tensor", "dp"),
        P("section", "dp", "tensor"),
        P("section", "tensor"),
        P("section", "tensor", "dp"),
    )
    out_specs = (
        P("section", "dp", "tensor", None),
        P("dp", None),
        P("section", "dp", "tensor"),
        P("section", "tensor"),
        P("section", None, "dp", "tensor"),
        P("section", "dp", "tensor"),
        P("section", "tensor"),
        P("section", None, "tensor"),
        P("section", "tensor", "dp"),
        P("section", "dp", "tensor"),
        P("section", "tensor"),
        P("section", "tensor", "dp"),
    )
    return jax.shard_map(
        per_device, mesh=mesh, in_specs=in_specs, out_specs=out_specs, check_vma=False
    )
```

```python
import functools
import math

import jax
import jax.numpy as jnp
from jax import lax
from jax.experimental import pallas as pl
from jax.experimental.pallas import tpu as pltpu
from jax.sharding import PartitionSpec as P

SIDE = 16
PATCHES = SIDE * SIDE
LANES = 128
F32 = jnp.float32
BF16 = jnp.bfloat16
HIGHEST = lax.Precision.HIGHEST
PLANE = ("tensor", "section")


class Traffic:
    def __init__(self, arriving, leaving):
        self.arriving, self.leaving, self.left = arriving, leaving, set()

    def wait(self, *places):
        for at in places:
            self.arriving[at].wait()

    def flush(self, *places):
        for at in places:
            self.leaving[at].start()
            self.left.add(at)


class Columns:
    def __init__(self, array, start, width):
        self.array, self.start = array, start
        self.shape, self.dtype = (array.shape[0], width), array.dtype
        self.size = array.shape[0] * width

    def source(self, ref):
        return ref.at[:, self.start : self.start + self.shape[1]]


def call(body, outs, *args, scalars=0, flops=0, scratch=(), after=(), streamed=(), saved=()):
    count, waits, many = len(args), len(after), len(outs)
    given = args
    moving = bool(streamed or saved)

    def kernel(*refs):
        ins, out_refs = list(refs[:count]), list(refs[count + waits : count + waits + many])
        rest = refs[count + waits + many :]
        own, held = rest[: len(scratch)], rest[len(scratch) :]
        arriving, leaving = {}, {}
        for i, at in enumerate(streamed):
            source = given[at].source(ins[at]) if isinstance(given[at], Columns) else ins[at]
            arriving[at] = pltpu.make_async_copy(source, held[i], held[-1].at[i])
            ins[at] = held[i]
        for i, at in enumerate(saved, len(streamed)):
            leaving[at] = pltpu.make_async_copy(held[i], out_refs[at], held[-1].at[i])
            out_refs[at] = held[i]
        traffic = Traffic(arriving, leaving)
        for copy in arriving.values():
            copy.start()
        if moving:
            body(traffic, *ins, *out_refs, *own)
        else:
            body(*ins, *out_refs, *own)
        traffic.flush(*[at for at in saved if at not in traffic.left])
        for copy in leaving.values():
            copy.wait()

    moved = sum(a.size * a.dtype.itemsize for a in args)
    moved += sum(math.prod(o.shape) * o.dtype.itemsize for o in outs)
    specs = [pl.BlockSpec(memory_space=pltpu.SMEM)] * scalars
    specs += [
        pl.BlockSpec(memory_space=pltpu.HBM if i in streamed else pltpu.VMEM)
        for i in range(scalars, count)
    ]
    large = [a.size > 2**17 for a in after]
    specs += [pl.BlockSpec(memory_space=pltpu.HBM if v else pl.ANY) for v in large]
    after = [
        pltpu.with_memory_space_constraint(a, pltpu.HBM) if v else a for a, v in zip(after, large)
    ]
    spaces = [pltpu.HBM if i in saved else pltpu.VMEM for i in range(many)]
    shapes = [
        pltpu.HBM(o.shape, o.dtype) if i in saved else o for i, o in enumerate(outs)
    ]
    args = [a.array if isinstance(a, Columns) else a for a in args]
    args = [
        pltpu.with_memory_space_constraint(a, pltpu.HBM) if i in streamed else a
        for i, a in enumerate(args)
    ]
    hold = [pltpu.VMEM(given[i].shape, given[i].dtype) for i in streamed]
    hold += [pltpu.VMEM(outs[i].shape, outs[i].dtype) for i in saved]
    if moving:
        hold.append(pltpu.SemaphoreType.DMA((len(hold),)))
    return pl.pallas_call(
        kernel,
        out_shape=tuple(shapes),
        in_specs=specs,
        out_specs=tuple(pl.BlockSpec(memory_space=space) for space in spaces),
        scratch_shapes=[*scratch, *hold],
        compiler_params=pltpu.CompilerParams(vmem_limit_bytes=6 * 2**20 + moved * 3 // 2),
        cost_estimate=pl.CostEstimate(flops=flops, bytes_accessed=moved, transcendentals=0),
    )(*args, *after)


def out(shape, dtype):
    return jax.ShapeDtypeStruct(shape, dtype)


def mm(a, b):
    return lax.dot_general(a, b, (((1,), (0,)), ((), ())), preferred_element_type=F32)


def mm_nt(a, b):
    return lax.dot_general(a, b, (((1,), (1,)), ((), ())), preferred_element_type=F32)


def mm_tn(a, b):
    return lax.dot_general(a, b, (((0,), (0,)), ((), ())), preferred_element_type=F32)


def normalize(v):
    centered = v - jnp.mean(v, axis=-1, keepdims=True)
    scale = lax.rsqrt(jnp.mean(centered * centered, axis=-1, keepdims=True) + 1e-06)
    return centered * scale, scale


def norm_grad(hat, rstd, grad):
    inner = jnp.mean(grad * hat, axis=-1, keepdims=True)
    return rstd * (grad - jnp.mean(grad, axis=-1, keepdims=True) - hat * inner)


def gather_total(pieces):
    total = pieces[0][...].astype(F32)
    for piece in pieces[1:]:
        total = total + piece[...].astype(F32)
    return total


def rows_sum(v):
    return jnp.sum(v, axis=0, keepdims=True)


def gelu_terms(x):
    k = math.sqrt(2.0 / math.pi)
    th = jnp.tanh(k * (x + 0.044715 * x * x * x))
    value = 0.5 * x * (1.0 + th)
    slope = 0.5 * (1.0 + th) + 0.5 * x * (1.0 - th * th) * k * (1.0 + 3 * 0.044715 * x * x)
    return value, slope


def start_kernel(x_ref, mod_ref, n_ref):
    for m in range(x_ref.shape[0]):
        hat, _ = normalize(x_ref[m].astype(F32))
        n_ref[m] = (hat * (1.0 + mod_ref[m, 1:2]) + mod_ref[m, 0:1]).astype(BF16)


def add_kernel(a, b, c, d, recv, *outs):
    for j, own in enumerate((a, b, c, d)):
        outs[j][...] = (own[...].astype(F32) + recv[j].astype(F32)).astype(BF16)


def after_attn_kernel(traffic, p0, p1, p2, p3, x_ref, mod_ref, att_ref, aft_ref, n_ref):
    for m in range(x_ref.shape[0]):
        att = gather_total([p.at[m] for p in (p0, p1, p2, p3)])
        aft = x_ref[m].astype(F32) + mod_ref[m, 2:3] * att
        hat, _ = normalize(aft)
        att_ref[m] = att
        aft_ref[m] = aft
        n_ref[m] = (hat * (1.0 + mod_ref[m, 4:5]) + mod_ref[m, 3:4]).astype(BF16)


def between_kernel(traffic, p0, p1, p2, p3, aft_ref, mod_ref, next_ref, mlp_ref, x_ref, n_ref):
    for m in range(aft_ref.shape[0]):
        mlp = gather_total([p.at[m] for p in (p0, p1, p2, p3)])
        x = (aft_ref[m] + mod_ref[m, 5:6] * mlp).astype(BF16)
        hat, _ = normalize(x.astype(F32))
        mlp_ref[m] = mlp
        x_ref[m] = x
        n_ref[m] = (hat * (1.0 + next_ref[m, 1:2]) + next_ref[m, 0:1]).astype(BF16)


def end_kernel(p0, p1, p2, p3, aft_ref, mod_ref, x_ref):
    for m in range(aft_ref.shape[0]):
        mlp = gather_total([p.at[m] for p in (p0, p1, p2, p3)])
        x_ref[m] = (aft_ref[m] + mod_ref[m, 5:6] * mlp).astype(BF16)


def back_mlp_rows_kernel(traffic, p0, p1, p2, p3, g_ref, aft_ref, att_ref, mod_ref, ga_ref, gt_ref, gm_ref):
    for m in range(aft_ref.shape[0]):
        gn = gather_total([p.at[m] for p in (p0, p1, p2, p3)])
        hat, rstd = normalize(aft_ref[m])
        grad = g_ref[m].astype(F32) + norm_grad(hat, rstd, gn * (1.0 + mod_ref[m, 4:5]))
        ga_ref[m] = grad
        gt_ref[m] = (mod_ref[m, 2:3] * grad).astype(BF16)
        gm_ref[m, 0:1] = rows_sum(grad * att_ref[m])
        gm_ref[m, 1:2] = rows_sum(gn)
        gm_ref[m, 2:3] = rows_sum(gn * hat)


def back_attn_rows(pieces, ga_ref, x_ref, mod_ref, some_ref, gate_ref, gm_ref, m):
    gn = gather_total([p.at[m] for p in pieces])
    hat, rstd = normalize(x_ref[m].astype(F32))
    grad = ga_ref[m] + norm_grad(hat, rstd, gn * (1.0 + mod_ref[m, 1:2]))
    gm_ref[m, 0:1] = rows_sum(gn)
    gm_ref[m, 1:2] = rows_sum(gn * hat)
    gm_ref[m, 2:5] = some_ref[m]
    gm_ref[m, 5:6] = gate_ref[m]
    return grad.astype(BF16)


def back_between_kernel(p0, p1, p2, p3, ga_ref, x_ref, mod_ref, some_ref, gate_ref, prev_ref, mlp_ref, *outs):
    g_ref, gmlp_ref, gm_ref, next_ref = outs
    for m in range(x_ref.shape[0]):
        grad = back_attn_rows((p0, p1, p2, p3), ga_ref, x_ref, mod_ref, some_ref, gate_ref, gm_ref, m)
        g_ref[m] = grad
        wide = grad.astype(F32)
        gmlp_ref[m] = (prev_ref[m, 5:6] * wide).astype(BF16)
        next_ref[m] = rows_sum(wide * mlp_ref[m])


def back_end_kernel(p0, p1, p2, p3, ga_ref, x_ref, mod_ref, some_ref, gate_ref, g_ref, gm_ref):
    for m in range(x_ref.shape[0]):
        g_ref[m] = back_attn_rows((p0, p1, p2, p3), ga_ref, x_ref, mod_ref, some_ref, gate_ref, gm_ref, m)


def scan_mask(columns_first):
    def place(number):
        if columns_first:
            return (number % SIDE) * SIDE + number // SIDE
        return number

    shape = (PATCHES, PATCHES)
    later = place(lax.broadcasted_iota(jnp.int32, shape, 0))
    return later >= place(lax.broadcasted_iota(jnp.int32, shape, 1))


def grid_column():
    return lax.broadcasted_iota(jnp.int32, (PATCHES, 1), 0) % SIDE


def side_shifts(a, column):
    left = jnp.where(column == 0, 0.0, pltpu.roll(a, 1, 0))
    right = jnp.where(column == SIDE - 1, 0.0, pltpu.roll(a, PATCHES - 1, 0))
    return left, a, right


def convolve(shifted, tap):
    sums = []
    for row in range(3):
        terms = [shifted[col] * tap(3 * row + col) for col in range(3)]
        sums.append(terms[0] + terms[1] + terms[2])
    zeros = jnp.zeros((SIDE, sums[0].shape[1]), F32)
    above = jnp.concatenate([zeros, sums[0][:-SIDE]], axis=0)
    below = jnp.concatenate([sums[2][SIDE:], zeros], axis=0)
    return shifted[1] + sums[1] + above + below


def tap_grads(shifted, grad):
    found = []
    for row in range(3):
        for col in range(3):
            if row == 0:
                product = shifted[col][:-SIDE] * grad[SIDE:]
            elif row == 1:
                product = shifted[col] * grad
            else:
                product = shifted[col][SIDE:] * grad[:-SIDE]
            found.append(rows_sum(product))
    return found


def lane_sets(width, first, head_width, heads):
    lane = lax.broadcasted_iota(jnp.int32, (1, width), 1)
    return [
        (lane >= first + h * head_width) & (lane < first + (h + 1) * head_width)
        for h in range(heads)
    ]


def decay_parts(logits, mask, gate_lane, heads):
    rates = -(jnp.maximum(logits, 0.0) + jnp.log1p(jnp.exp(-jnp.abs(logits))))
    ones = jnp.where(mask, 1.0, 0.0)
    totals = lax.dot_general(
        ones, rates, (((1,), (0,)), ((), ())), precision=HIGHEST, preferred_element_type=F32
    )
    turned = totals.T
    decays = []
    for h in range(heads):
        at = gate_lane + h
        spans = jnp.where(mask, totals[:, at : at + 1] - turned[at : at + 1, :], -1e30)
        w = jnp.exp(spans)
        decays.append((w, jnp.sum(w, axis=1, keepdims=True)))
    return decays, ones


def send_order(k):
    return (0, 1, None, None, 2, 3, None, None)[k], (None, None, 0, 1, None, None, 2, 3)[k]


def write_pieces(me, total_ref, other_ref, own_refs):
    rows = total_ref.shape[1] // 8
    for k in range(8):
        spot = pl.ds(pl.multiple_of(jnp.bitwise_xor(me, k) * rows, rows), rows)
        own, other = send_order(k)
        if own is None:
            other_ref[other] = total_ref[:, spot, :]
        else:
            own_refs[own][...] = total_ref[:, spot, :]


def each_shard(refs):
    own, x, y, xy, core, core_x, core_y, core_xy = refs
    return own, x, core, core_x, y, xy, core_y, core_xy


def gather_pieces(me, shard_refs, full_ref):
    rows = full_ref.shape[1] // 8
    for k, shard in enumerate(each_shard(shard_refs)):
        spot = pl.ds(pl.multiple_of(jnp.bitwise_xor(me, k) * rows, rows), rows)
        full_ref[:, spot, :] = shard[...]


def tail_spots(heads):
    return (0, 32, 48, 64, 80)


def join_tail(packed, piece, tails, lane):
    tile = packed[:, piece * LANES : (piece + 1) * LANES]
    return jnp.concatenate([tile, pltpu.roll(tails, (LANES - lane) % LANES, 1)], axis=1)


def lanes():
    return lax.broadcasted_iota(jnp.int32, (1, LANES), 1)


def half_tiles(tiles, at):
    if at == 0:
        return tiles[0], tiles[1]
    shift = 2 * LANES - at
    first = jnp.where(lanes() < shift, pltpu.roll(tiles[1], shift, 1), pltpu.roll(tiles[2], shift, 1))
    return first, pltpu.roll(tiles[2], shift, 1)


def pack_attn_kernel(cfg, traffic, sec_ref, in_ref, gate_ref, out_ref, keep_ref, send_ref):
    heads, channels = cfg
    traffic.wait(1)
    spots = tail_spots(heads)
    tail = channels - LANES
    rows = in_ref.shape[1]
    short = jnp.zeros((rows, 3 * LANES - 2 * channels), F32)
    keep_first = sec_ref[0] == 0
    lane = lanes()
    tails = [gate_ref[...], pltpu.roll(gate_ref[...], LANES - heads, 1)]
    tails = [
        jnp.where((lane >= tail) & (lane < tail + heads), pltpu.roll(v, tail, 1), 0.0) for v in tails
    ]
    for j in range(5):
        ref = out_ref if j == 4 else in_ref.at[j]
        tiles = [ref[:, :LANES].astype(F32), ref[:, LANES : 2 * LANES].astype(F32)]
        tiles.append(jnp.concatenate([ref[:, 2 * LANES :].astype(F32), short], axis=1))
        whole = []
        for h in range(2):
            tile, rest = half_tiles(tiles, h * channels)
            whole.append(tile)
            tails[h] = tails[h] + pltpu.roll(jnp.where(lane < tail, rest, 0.0), spots[j], 1)
        cols = slice(j * LANES, (j + 1) * LANES)
        keep_ref[:, cols] = jnp.where(keep_first, whole[0], whole[1]).astype(BF16)
        send_ref[:, cols] = jnp.where(keep_first, whole[1], whole[0]).astype(BF16)
    cols = slice(5 * LANES, 6 * LANES)
    keep_ref[:, cols] = jnp.where(keep_first, tails[0], tails[1]).astype(BF16)
    send_ref[:, cols] = jnp.where(keep_first, tails[1], tails[0]).astype(BF16)


def pack_mlp_kernel(left, traffic, sec_ref, up_ref, down_ref, keep_b_ref, send_b_ref):
    keep_first = sec_ref[0] == 0
    lane = lanes()
    main = (keep_b_ref.shape[1] - LANES) // 2
    traffic.wait(1)
    at = 0
    for ref in (up_ref, down_ref):
        low, high = ref[:, :main], ref[:, main : 2 * main]
        keep_b_ref[:, at : at + main] = jnp.where(keep_first, low, high)
        send_b_ref[:, at : at + main] = jnp.where(keep_first, high, low)
        at += main
    up, down = (ref[:, 2 * main :].astype(F32) for ref in (up_ref, down_ref))
    low = jnp.where(lane < left, up, pltpu.roll(down, left, 1)).astype(BF16)
    high = jnp.where(lane < left, pltpu.roll(up, left, 1), down).astype(BF16)
    keep_b_ref[:, at:] = jnp.where(keep_first, low, high)
    send_b_ref[:, at:] = jnp.where(keep_first, high, low)


def unpack_mlp_kernel(left, sec_ref, sum0_ref, other0_ref, sum1_ref, other1_ref, up_ref, down_ref):
    in_first = sec_ref[0] == 0
    main = (sum0_ref.shape[1] - LANES) // 2
    lane = lanes()

    def both(cols):
        low = jnp.where(in_first, sum0_ref[:, cols], other1_ref[:, cols])
        return low.astype(F32), jnp.where(in_first, other0_ref[:, cols], sum1_ref[:, cols]).astype(F32)

    up_ref[:, :main], up_ref[:, main : 2 * main] = both(slice(0, main))
    down_ref[:, :main], down_ref[:, main : 2 * main] = both(slice(main, 2 * main))
    low, high = both(slice(2 * main, 2 * main + LANES))
    up_ref[:, 2 * main :] = jnp.where(lane < left, low, pltpu.roll(high, left, 1))
    down_ref[:, 2 * main :] = jnp.where(lane < left, pltpu.roll(low, LANES - left, 1), high)


def unpack_attn_kernel(
    cfg, sec_ref, sum0_ref, other0_ref, sum1_ref, other1_ref, in_ref, gate_ref, out_ref
):
    heads, channels = cfg
    spots = tail_spots(heads)
    tail = channels - LANES
    in_first = sec_ref[0] == 0
    lane = lanes()
    shift = channels - LANES

    def both(cols):
        low = jnp.where(in_first, sum0_ref[:, cols], other1_ref[:, cols])
        return low.astype(F32), jnp.where(in_first, other0_ref[:, cols], sum1_ref[:, cols]).astype(F32)

    low_tails, high_tails = both(slice(5 * LANES, 6 * LANES))
    for j in range(5):
        ref = out_ref if j == 4 else in_ref.at[j]
        low, high = both(slice(j * LANES, (j + 1) * LANES))
        ref[:, :LANES] = low
        high = pltpu.roll(high, shift, 1)
        low_tail = pltpu.roll(low_tails, (LANES - spots[j]) % LANES, 1)
        high_tail = pltpu.roll(high_tails, (LANES - spots[j] + shift) % LANES, 1)
        ref[:, LANES : 2 * LANES] = jnp.where(lane < tail, low_tail, high)
        last = jnp.where(lane < shift, high, high_tail)
        ref[:, 2 * LANES :] = last[:, : 2 * channels - 2 * LANES]
    low_gate = pltpu.roll(low_tails, LANES - tail, 1)
    high_gate = pltpu.roll(high_tails, LANES - tail + heads, 1)
    gate_ref[...] = jnp.where(lane < heads, low_gate, high_gate)[:, : 2 * heads]


def attn_forward_kernel(cfg, traffic, me_ref, *refs):
    columns_first, heads, head_width = cfg
    shards, (w_ref, gb_ref, tap_ref) = refs[:8], refs[8:11]
    n_ref, proj_ref, log_ref, attn_ref, mix_ref, other_ref = refs[11:17]
    own_refs, total_ref = refs[17:21], refs[21]
    me = me_ref[0]
    wide = 2 * LANES
    gate_lane = heads * head_width - LANES
    spots = tail_spots(heads)
    mask = scan_mask(columns_first)
    column = grid_column()
    sets = lane_sets(wide, 0, head_width, heads)
    gather_pieces(me, shards, n_ref)
    traffic.flush(0)
    traffic.wait(9)
    for m in range(n_ref.shape[0]):
        projected = mm(n_ref[m], w_ref[:, : 4 * LANES])
        tails = mm(n_ref[m], w_ref[:, 5 * LANES :])
        logits = tails + gb_ref[...]
        log_ref[m] = logits
        decays, _ = decay_parts(logits, mask, gate_lane, heads)
        query, key, value, gate = (join_tail(projected, j, tails, spots[j]) for j in range(4))
        in_head = sets[0]
        for own in sets[1:]:
            in_head = in_head | own
        query, key, value = (jnp.where(in_head, v, 0.0).astype(BF16) for v in (query, key, value))
        gate = gate.astype(BF16)
        for j, v in enumerate((query, key, value, gate)):
            proj_ref[m, :, j * wide : (j + 1) * wide] = v
        attn = None
        for h in range(heads):
            w, mass = decays[h]
            raw = mm_nt(jnp.where(sets[h], query, jnp.zeros_like(query)), key)
            scores = (raw * head_width ** (-0.5) * w).astype(BF16)
            normed = mm(scores, value) * lax.rsqrt(mass)
            attn = jnp.where(sets[h], normed, 0.0 if attn is None else attn)
        attn_ref[m] = attn
        spread = convolve(side_shifts(attn, column), lambda i: tap_ref[i : i + 1, :])
        gate = gate.astype(F32)
        mixed = spread * (gate * jax.nn.sigmoid(gate))
        mixed = jnp.where(in_head, mixed, 0.0)
        mixed = jnp.concatenate(
            [mixed[:, :LANES], pltpu.roll(mixed[:, LANES:], spots[4], 1)], axis=1
        ).astype(BF16)
        mix_ref[m] = mixed
        if m == n_ref.shape[0] - 1:
            traffic.flush(1, 2, 3, 4)
        total_ref[m] = mm_nt(mixed, w_ref[:, 4 * LANES :]).astype(BF16)
    write_pieces(me, total_ref, other_ref, own_refs)


def attn_backward_kernel(cfg, traffic, me_ref, *refs):
    columns_first, heads, head_width = cfg
    shards, (proj_ref, log_ref, attn_ref, w_ref, tap_ref) = refs[:8], refs[8:13]
    g_ref, gproj_ref, gtap_ref, other_ref = refs[13:17]
    own_refs, total_ref = refs[17:21], refs[21]
    me = me_ref[0]
    wide = 2 * LANES
    gate_lane = heads * head_width - LANES
    spots = tail_spots(heads)
    scale = head_width ** (-0.5)
    mask = scan_mask(columns_first)
    column = grid_column()
    sets = lane_sets(wide, 0, head_width, heads)
    gate_sets = lane_sets(LANES, gate_lane, 1, heads)
    sublane = lax.broadcasted_iota(jnp.int32, (LANES, 1), 0)
    in_head = sets[0]
    for own in sets[1:]:
        in_head = in_head | own
    gather_pieces(me, shards, g_ref)
    gtap_ref[...] = jnp.zeros(gtap_ref.shape, F32)
    traffic.wait(9, 10, 11, 12)
    for m in range(g_ref.shape[0]):
        g_packed = mm(g_ref[m], w_ref[:, 4 * LANES :])
        g_mixed = jnp.where(in_head, join_tail(g_packed, 0, g_packed[:, LANES:], spots[4]), 0.0)
        query, key, value, gate = (proj_ref[m, :, j * wide : (j + 1) * wide] for j in range(4))
        gate = gate.astype(F32)
        sig = jax.nn.sigmoid(gate)
        attn = attn_ref[m]
        shifted = side_shifts(attn, column)
        spread = convolve(shifted, lambda i: tap_ref[i : i + 1, :])
        g_spread = g_mixed * (gate * sig)
        g_gate = g_mixed * spread * (sig * (1.0 + gate * (1.0 - sig)))
        for i, grad in enumerate(tap_grads(shifted, g_spread)):
            gtap_ref[i : i + 1, :] = grad if m == 0 else gtap_ref[i : i + 1, :] + grad
        g_attn = convolve(side_shifts(g_spread, column), lambda i: tap_ref[8 - i : 9 - i, :])
        logits = log_ref[m]
        decays, ones = decay_parts(logits, mask, gate_lane, heads)
        g_query = g_key = g_value = 0.0
        across = jnp.zeros((PATCHES, LANES), F32)
        down = jnp.zeros((LANES, PATCHES), F32)
        for h in range(heads):
            w, mass = decays[h]
            own_query = jnp.where(sets[h], query, jnp.zeros_like(query))
            raw = mm_nt(own_query, key) * scale
            own_grad = jnp.where(sets[h], g_attn, 0.0)
            g_mass = -0.5 * jnp.sum(own_grad * attn, axis=1, keepdims=True) / mass
            g_out = (own_grad * lax.rsqrt(mass)).astype(BF16)
            g_value = g_value + mm_tn((raw * w).astype(BF16), g_out)
            g_scores = mm_nt(g_out, value)
            g_raw = (g_scores * w * scale).astype(BF16)
            g_query = jnp.where(sets[h], mm(g_raw, key), g_query)
            g_key = g_key + mm_tn(g_raw, own_query)
            g_span = (g_scores * raw + g_mass) * w
            across = jnp.where(gate_sets[h], jnp.sum(g_span, axis=1, keepdims=True), across)
            down = jnp.where(sublane == gate_lane + h, rows_sum(g_span), down)
        g_rates = lax.dot_general(
            ones,
            across - down.T,
            (((0,), (0,)), ((), ())),
            precision=HIGHEST,
            preferred_element_type=F32,
        )
        g_logits = (-g_rates * jax.nn.sigmoid(logits)).astype(BF16).astype(F32)
        g_bias = rows_sum(g_logits)
        gtap_ref[9:10, :LANES] = g_bias if m == 0 else gtap_ref[9:10, :LANES] + g_bias
        tails = g_logits
        for j, v in enumerate((g_query, g_key, g_value, g_gate)):
            gproj_ref[m, :, j * LANES : (j + 1) * LANES] = v[:, :LANES].astype(BF16)
            tails = tails + pltpu.roll(v[:, LANES:], spots[j], 1)
        gproj_ref[m, :, 4 * LANES :] = tails.astype(BF16)
        total = mm_nt(gproj_ref[m, :, : 4 * LANES], w_ref[:, : 4 * LANES])
        total = total + mm_nt(gproj_ref[m, :, 4 * LANES :], w_ref[:, 5 * LANES :])
        total_ref[m] = total.astype(BF16)
    write_pieces(me, total_ref, other_ref, own_refs)


def attn_weights_kernel(traffic, n_ref, gproj_ref, g_ref, mix_ref, gw_ref):
    traffic.wait(0, 3)
    for part in range(2):
        cols = slice(part * 2 * LANES, (part + 1) * 2 * LANES)
        total = mm_tn(n_ref[0], gproj_ref[0, :, cols])
        for m in range(1, n_ref.shape[0]):
            total = total + mm_tn(n_ref[m], gproj_ref[m, :, cols])
        gw_ref[:, cols] = total.astype(BF16)
    total = mm_tn(g_ref[0], mix_ref[0])
    tails = mm_tn(n_ref[0], gproj_ref[0, :, 4 * LANES :])
    for m in range(1, n_ref.shape[0]):
        total = total + mm_tn(g_ref[m], mix_ref[m])
        tails = tails + mm_tn(n_ref[m], gproj_ref[m, :, 4 * LANES :])
    gw_ref[:, 4 * LANES : 5 * LANES] = total[:, :LANES].astype(BF16)
    gw_ref[:, 5 * LANES :] = (total[:, LANES:] + tails).astype(BF16)


def stack_shards(shards, full_ref):
    for k, shard in enumerate(each_shard(shards)):
        images, rows, width = shard.shape
        full_ref[k * images * rows : (k + 1) * images * rows, :] = shard[...].reshape(
            images * rows, width
        )


def stack_kernel(traffic, *refs):
    stack_shards(refs[:8], refs[8])


def put_shard(k, value, shape, other_ref, own_refs):
    own, other = send_order(k)
    if own is None:
        other_ref[other] = value.astype(BF16).reshape(shape)
    else:
        own_refs[own][...] = value.astype(BF16).reshape(shape)


def put_shards(total, shape, other_ref, own_refs):
    rows = total.shape[0] // 8
    for k in range(8):
        put_shard(k, total[k * rows : (k + 1) * rows], shape, other_ref, own_refs)


def mlp_forward_kernel(left, traffic, *refs):
    shards, (w_ref, ub_ref) = refs[:8], refs[8:10]
    n_ref, pre_ref, hid_ref, other_ref = refs[10:14]
    own_refs = refs[14:18]
    main = (w_ref.shape[1] - LANES) // 2
    stack_shards(shards, n_ref)
    traffic.flush(0)
    traffic.wait(8)
    n = n_ref[...]
    pre = mm(n, w_ref[:, :main]) + ub_ref[:, :main]
    pre_ref[:, :main] = pre
    hidden = gelu_terms(pre)[0].astype(BF16)
    hid_ref[:, :main] = hidden
    last = mm(n, w_ref[:, 2 * main :]) + ub_ref[:, main:]
    pre_ref[:, main:] = last
    lane = lax.broadcasted_iota(jnp.int32, (1, LANES), 1)
    tail = jnp.where(lane < left, gelu_terms(last)[0], 0.0)
    tail = pltpu.roll(tail, LANES - left, 1).astype(BF16)
    hid_ref[:, main:] = tail
    traffic.flush(1, 2)
    total = mm_nt(hidden, w_ref[:, main : 2 * main]) + mm_nt(tail, w_ref[:, 2 * main :])
    put_shards(total, shards[0].shape, other_ref, own_refs)


def mlp_backward_kernel(left, traffic, *refs):
    given, (pre_ref, w_ref) = refs[:8], refs[8:10]
    g_ref, rest = refs[10], refs[11:]
    stack_shards(given, g_ref)
    traffic.wait(8, 9)
    gpre_ref, gub_ref, other_ref = rest[:3]
    own_refs = rest[3:]
    main = (w_ref.shape[1] - LANES) // 2
    g = g_ref[...]
    g_pre = mm(g, w_ref[:, main : 2 * main]) * gelu_terms(pre_ref[:, :main])[1]
    g_pre = g_pre.astype(BF16)
    gpre_ref[:, :main] = g_pre
    gub_ref[:, :main] = rows_sum(g_pre.astype(F32))
    lane = lax.broadcasted_iota(jnp.int32, (1, LANES), 1)
    last = pltpu.roll(mm(g, w_ref[:, 2 * main :]), left, 1) * gelu_terms(pre_ref[:, main:])[1]
    last = jnp.where(lane < left, last, 0.0).astype(BF16)
    gpre_ref[:, main:] = last
    gub_ref[:, main:] = rows_sum(last.astype(F32))
    total = mm_nt(g_pre, w_ref[:, :main]) + mm_nt(last, w_ref[:, 2 * main :])
    put_shards(total, own_refs[0].shape, other_ref, own_refs)


def mlp_both_kernel(left, traffic, n_ref, raw_ref, w_ref, ub_ref, mod_ref, *refs):
    gw_ref, gub_ref, gate_ref, other_ref = refs[:4]
    own_refs, end_ref, end_refs = refs[4:8], refs[8], refs[9:13]
    g_ref = refs[13]
    images, rows = own_refs[0].shape[:2]
    main = (w_ref.shape[1] - LANES) // 2
    lane = lax.broadcasted_iota(jnp.int32, (1, LANES), 1)
    spans = [(i % images, slice(i * rows, (i + 1) * rows)) for i in range(8 * images)]
    traffic.wait(0, 1)
    for m, span in spans:
        g_ref[span] = (mod_ref[m, 5:6] * raw_ref[span].astype(F32)).astype(BF16)
    traffic.wait(2)
    n, g = n_ref[...], g_ref[...]
    value, slope = gelu_terms(mm(n, w_ref[:, :main]) + ub_ref[:, :main])
    hidden = value.astype(BF16)
    g_pre = (mm(g, w_ref[:, main : 2 * main]) * slope).astype(BF16)
    value, slope = gelu_terms(mm(n, w_ref[:, 2 * main :]) + ub_ref[:, main:])
    tail = pltpu.roll(jnp.where(lane < left, value, 0.0), LANES - left, 1).astype(BF16)
    last = pltpu.roll(mm(g, w_ref[:, 2 * main :]), left, 1) * slope
    last = jnp.where(lane < left, last, 0.0).astype(BF16)
    gw_ref[:, :main] = mm_tn(n, g_pre).astype(BF16)
    gw_ref[:, main : 2 * main] = mm_tn(g, hidden).astype(BF16)
    gw_ref[:, 2 * main :] = (mm_tn(n, last) + mm_tn(g, tail)).astype(BF16)
    traffic.flush(0)
    gub_ref[:, :main] = rows_sum(g_pre.astype(F32))
    gub_ref[:, main:] = rows_sum(last.astype(F32))
    total = mm_nt(hidden, w_ref[:, main : 2 * main]) + mm_nt(tail, w_ref[:, 2 * main :])
    put_shards(total, own_refs[0].shape, end_ref, end_refs)
    traffic.flush(8, 9, 10, 11, 12)
    gates = [0.0] * images
    for m, span in spans:
        gates[m] = gates[m] + rows_sum(raw_ref[span].astype(F32) * total[span])
    for m in range(images):
        gate_ref[m] = gates[m]
    total = mm_nt(g_pre, w_ref[:, :main]) + mm_nt(last, w_ref[:, 2 * main :])
    put_shards(total, own_refs[0].shape, other_ref, own_refs)


def mlp_weights_kernel(traffic, n_ref, gpre_ref, g_ref, hid_ref, gw_ref):
    main = gpre_ref.shape[1] - LANES
    traffic.wait(0, 3)
    gw_ref[:, :main] = mm_tn(n_ref[...], gpre_ref[:, :main]).astype(BF16)
    gw_ref[:, main : 2 * main] = mm_tn(g_ref[...], hid_ref[:, :main]).astype(BF16)
    last = mm_tn(n_ref[...], gpre_ref[:, main:]) + mm_tn(g_ref[...], hid_ref[:, main:])
    gw_ref[:, 2 * main :] = last.astype(BF16)


def swap(value, tensor_bits, section_bit):
    tensors, sections = lax.axis_size("tensor"), lax.axis_size("section")
    route = [
        (t * sections + s, (t ^ tensor_bits) * sections + (s ^ section_bit))
        for t in range(tensors)
        for s in range(sections)
    ]
    return lax.ppermute(value, PLANE, route)


def gather_plane(own):
    xy, x, y = swap(own, 2, 1), swap(own, 0, 1), swap(own, 2, 0)
    return own, x, y, xy, *(swap(v, 1, 0) for v in (own, x, y, xy))


def scatter_plane(other, own):
    received = swap(other, 1, 0)
    sums = call(add_kernel, (out(own[0].shape, BF16),) * 4, *own, received)
    return (sums[0], swap(sums[3], 2, 1), swap(sums[1], 0, 1), swap(sums[2], 2, 0))


def spread_over(value, axes):
    count = math.prod(lax.axis_size(a) for a in axes)
    copies = jnp.broadcast_to(value[None], (count,) + value.shape)
    return lax.all_to_all(copies, axes, split_axis=0, concat_axis=0, tiled=True)


def gather_all(own):
    return lax.all_gather(own, "dp", axis=0, tiled=True)


def scatter_rows(partial):
    return lax.psum_scatter(partial, "dp", scatter_dimension=0, tiled=True)


def sinusoid(time_steps, channels):
    half_width = channels // 2
    frequency = jnp.exp(
        jnp.arange(half_width, dtype=jnp.float32) * (-math.log(10000.0) / half_width)
    )
    angles = time_steps.astype(jnp.float32)[:, None] * frequency[None, :]
    return jnp.concatenate([jnp.cos(angles), jnp.sin(angles)], axis=1)


def per_device(
    section_inputs,
    condition,
    timesteps,
    ada_weight,
    ada_bias,
    in_weight,
    gate_weight,
    gate_bias,
    conv_taps,
    out_weight,
    up_weight,
    up_bias,
    down_weight,
):
    d = lax.axis_index("dp")
    t = lax.axis_index("tensor")
    s = lax.axis_index("section")
    dps, tensors, sections = (lax.axis_size(a) for a in ("dp", "tensor", "section"))
    first = s == 0
    me = (t * sections + s).astype(jnp.int32).reshape(1)
    images = condition.shape[0]
    width = condition.shape[1]
    slab = in_weight.shape[2]
    heads = gate_weight.shape[2] // sections
    channels = in_weight.shape[3] // sections
    head_width = channels // heads
    units = up_weight.shape[2] // sections
    wide = 2 * LANES
    tail = channels - LANES
    rows = section_inputs.shape[2] // sections
    main = units // LANES * LANES
    left = units - main
    spots = tail_spots(heads)

    def cut(value, axis):
        half = value.shape[axis] // 2
        return (
            lax.slice_in_dim(value, 0, half, axis=axis),
            lax.slice_in_dim(value, half, 2 * half, axis=axis),
        )

    def swap_halves(keep, send):
        received = lax.ppermute(send, "section", [(0, 1), (1, 0)])
        return jnp.where(first, keep, received), jnp.where(first, received, keep)

    def choose(pair):
        return jnp.where(first, pair[0], pair[1]), jnp.where(first, pair[1], pair[0])

    cfg = (heads, channels)
    section = s.astype(jnp.int32).reshape(1)
    shape_a, shape_b = (slab, 6 * LANES), (slab, 2 * main + LANES)
    kept_a, sent_a = call(
        functools.partial(pack_attn_kernel, cfg),
        (out(shape_a, BF16),) * 2,
        section,
        in_weight[0],
        jnp.pad(gate_weight[0].astype(F32), ((0, 0), (0, LANES - gate_weight.shape[2]))),
        out_weight[0].T,
        scalars=1,
        streamed=(1,),
    )
    sent_a, condition, down_in = lax.optimization_barrier((sent_a, condition, down_weight[0]))
    received_a = lax.ppermute(sent_a, "section", [(0, 1), (1, 0)])
    kept_b, sent_b = call(
        functools.partial(pack_mlp_kernel, left),
        (out(shape_b, BF16),) * 2,
        section,
        up_weight[0],
        down_in.T,
        scalars=1,
        streamed=(1,),
    )
    received_b = lax.ppermute(sent_b, "section", [(0, 1), (1, 0)])

    def unit_halves(value):
        rest = sections * main
        return tuple(
            (value[:, h * main : (h + 1) * main], value[:, rest + h * left : rest + (h + 1) * left])
            for h in (0, 1)
        )

    def pack_small(gate_half, taps_half, up_half):
        return jnp.concatenate([gate_half.reshape(-1), taps_half.reshape(-1), up_half.reshape(-1)])

    def pack_halves(pack, *pairs):
        return tuple(pack(*(pair[i] for pair in pairs)) for i in (0, 1))

    x_pair = cut(section_inputs[0], 1)
    x_received = lax.ppermute(
        jnp.where(first, x_pair[1], x_pair[0]), "section", [(0, 1), (1, 0)]
    )
    x0 = jnp.where(first, x_pair[0], x_received)
    g1 = jnp.where(first, x_received, x_pair[1])
    taps_count = conv_taps.shape[1]
    up_row = up_bias[0].astype(F32)[None]
    small = swap_halves(
        *choose(
            pack_halves(
                pack_small,
                cut(gate_bias[0].astype(F32), 0),
                cut(conv_taps[0].astype(F32), 1),
                tuple(jnp.concatenate(v, axis=1) for v in unit_halves(up_row)),
            )
        )
    )

    def unpack_small(packed):
        gate_row = jnp.pad(packed[:heads][None], ((0, 0), (tail, LANES - heads - tail)))
        taps = packed[heads : heads + taps_count * channels].reshape(taps_count, channels)
        taps = jnp.pad(taps, ((0, 16 - taps_count), (0, wide - channels)))
        up_row = packed[heads + taps_count * channels :][None]
        return gate_row, taps, jnp.pad(up_row, ((0, 0), (0, main + LANES - units)))

    cond_vec = condition + sinusoid(timesteps, width)
    activated = jax.nn.silu(cond_vec).astype(BF16)
    slab_active = activated.reshape(images, dps, slab).transpose(1, 0, 2)
    slab_active = lax.all_to_all(slab_active, "dp", split_axis=0, concat_axis=0, tiled=True)
    slab_active = slab_active.reshape(dps * images, slab)
    slab_active, received_a = lax.optimization_barrier((slab_active, received_a))
    mod_part = jnp.dot(slab_active, ada_weight[0], preferred_element_type=F32)
    mod_parts = lax.all_to_all(
        mod_part.reshape(dps, images, -1), "dp", split_axis=0, concat_axis=0, tiled=True
    )
    mod_share = jnp.sum(mod_parts, axis=0) + ada_bias[0].astype(F32)
    mod_all = spread_over(mod_share, ("section", "tensor"))
    received_b, mod_all = lax.optimization_barrier((received_b, mod_all))
    mod_all = mod_all.reshape(sections, tensors, images, -1).transpose(0, 2, 1, 3)
    mod_all = mod_all.reshape(sections, images, 6, width)
    mods = (mod_all[0], mod_all[1])

    shard = out((images, rows, width), BF16)
    shard_wide = out((images, rows, width), F32)
    vector = out((images, 1, width), F32)
    pieces_out = (out((4, images, rows, width), BF16),) + (shard,) * 4
    full = out((images, PATCHES, width), BF16)
    flat = out((images * PATCHES, width), BF16)
    total_rows = images * PATCHES
    kept = pltpu.VMEM((images, PATCHES, width), BF16)
    middle_flops = 2 * total_rows * PATCHES * wide * heads * 6
    attn_flops = 2 * total_rows * width * wide * 5 + middle_flops
    mlp_flops = 4 * total_rows * width * units

    def attn_forward(b, shards):
        w, _, gate_row, taps, _ = weights[b]
        body = functools.partial(attn_forward_kernel, (b == 1, heads, head_width))
        found = call(
            body,
            (
                full,
                out((images, PATCHES, 4 * wide), BF16),
                out((images, PATCHES, LANES), F32),
                out((images, PATCHES, wide), F32),
                out((images, PATCHES, wide), BF16),
                *pieces_out,
            ),
            me,
            *shards,
            w,
            gate_row,
            taps,
            scalars=1,
            flops=attn_flops,
            scratch=[kept],
            streamed=(9,),
            saved=(0, 1, 2, 3, 4),
        )
        return found[:5], scatter_plane(found[5], found[6:])

    def attn_backward(b, shards, saved, after=()):
        w, _, _, taps, _ = weights[b]
        body = functools.partial(attn_backward_kernel, (b == 1, heads, head_width))
        found = call(
            body,
            (
                full,
                out((images, PATCHES, 5 * LANES), BF16),
                out((16, wide), F32),
                *pieces_out,
            ),
            me,
            *shards,
            saved[1],
            saved[2],
            saved[3],
            w,
            taps,
            scalars=1,
            flops=2 * attn_flops,
            scratch=[kept],
            streamed=(9, 10, 11, 12),
            after=after,
        )
        terms = scatter_plane(found[3], found[4:])
        (grads,) = call(
            attn_weights_kernel,
            (out((width, 6 * LANES), BF16),),
            saved[0],
            found[1],
            found[0],
            saved[4],
            flops=2 * total_rows * width * wide * 5,
            after=terms if b else (),
            streamed=(0, 3),
            saved=(0,),
        )
        return terms, grads, found[2]

    def mlp_forward(b, normed):
        _, w, _, _, up_row = weights[b]
        found = call(
            functools.partial(mlp_forward_kernel, left),
            (
                flat,
                out((total_rows, main + LANES), F32),
                out((total_rows, main + LANES), BF16),
                *pieces_out,
            ),
            *gather_plane(normed),
            w,
            up_row,
            flops=mlp_flops,
            streamed=(8,),
            saved=(0, 1, 2),
        )
        return found[:3], scatter_plane(found[3], found[4:])

    shape_gw = out((width, 2 * main + LANES), BF16)
    shape_gub = out((1, main + LANES), F32)

    def mlp_both(b, gathered, gradient):
        _, w, _, _, up_row = weights[b]
        found = call(
            functools.partial(mlp_both_kernel, left),
            (shape_gw, shape_gub, vector, *pieces_out, *pieces_out),
            gathered,
            gradient,
            w,
            up_row,
            mods[b],
            flops=3 * mlp_flops,
            scratch=[pltpu.VMEM(flat.shape, flat.dtype)],
            streamed=(0, 1, 2),
            saved=(0, 8, 9, 10, 11, 12),
        )
        return scatter_plane(found[3], found[4:8]), found[0], found[1], found[2], found[8:]

    def mlp_backward(b, given, saved, after=()):
        _, w, _, _, _ = weights[b]
        found = call(
            functools.partial(mlp_backward_kernel, left),
            (flat, out((total_rows, main + LANES), BF16), shape_gub, *pieces_out),
            *given,
            saved[1],
            w,
            flops=mlp_flops,
            streamed=(8, 9),
            after=after,
        )
        terms = scatter_plane(found[3], found[4:])
        (grads,) = call(
            mlp_weights_kernel,
            (shape_gw,),
            saved[0],
            found[1],
            found[0],
            saved[2],
            flops=mlp_flops,
            after=terms,
            streamed=(0, 3),
            saved=(0,),
        )
        return terms, grads, found[2]

    def of_block(b, kept, received):
        return jnp.where(first == (b == 0), kept, received)

    full_a0 = gather_all(of_block(0, kept_a, received_a))
    middle = [of_block(0, kept_b, received_b), of_block(1, kept_a, received_a)]
    full_middle = gather_all(jnp.concatenate(middle, axis=1))
    full_b0 = Columns(full_middle, 0, middle[0].shape[1])
    full_a1 = Columns(full_middle, middle[0].shape[1], middle[1].shape[1])
    (g1_all,) = call(stack_kernel, (flat,), *gather_plane(g1), saved=(0,))
    (normed,) = call(start_kernel, (shard,), x0, mods[0])
    shards, g1_all, next_b = lax.optimization_barrier(
        (
            gather_plane(normed),
            g1_all,
            of_block(1, kept_b, received_b),
        )
    )
    weights = [
        (full_a0, full_b0, *unpack_small(small[0])),
        (full_a1, gather_all(next_b), *unpack_small(small[1])),
    ]

    def to_second(value):
        return lax.ppermute(value, "section", [(0, 1)])

    def to_first(value):
        return lax.ppermute(value, "section", [(1, 0)])

    attn0, terms = attn_forward(0, shards)
    att0, aft0, normed = call(
        after_attn_kernel, (shard_wide, shard_wide, shard), *terms, x0, mods[0], saved=(0, 1)
    )
    mlp0, terms = mlp_forward(0, normed)
    mlp_out0, x1, normed = call(
        between_kernel,
        (shard_wide, shard, shard),
        *terms,
        aft0,
        mods[0],
        mods[1],
        saved=(0, 1),
    )
    attn1, terms = attn_forward(1, gather_plane(normed))
    att1, aft1, normed = call(
        after_attn_kernel, (shard_wide, shard_wide, shard), *terms, x1, mods[1], saved=(0, 1)
    )

    three, six = (out((images, n, width), F32) for n in (3, 6))
    (n_all,) = call(stack_kernel, (flat,), *gather_plane(normed), saved=(0,))
    terms, mlp_grads1, g_up_bias1, g_gate_two1, end_pieces = mlp_both(1, n_all, g1_all)
    g_after, g_attn, g_some = call(
        back_mlp_rows_kernel,
        (shard_wide, shard, three),
        *terms,
        g1,
        aft1,
        att1,
        mods[1],
        saved=(0,),
    )
    sum_b1 = scatter_rows(mlp_grads1)
    terms, attn_grads1, g_taps1 = attn_backward(1, gather_plane(g_attn), attn1)
    g0, g_mlp, g_mods1, g_gate_two0 = call(
        back_between_kernel,
        (shard, shard, six, vector),
        *terms,
        g_after,
        x1,
        mods[1],
        g_some,
        g_gate_two1,
        mods[0],
        mlp_out0,
    )
    sum_a1 = scatter_rows(attn_grads1)
    terms, mlp_grads0, g_up_bias0 = mlp_backward(0, gather_plane(g_mlp), mlp0, (attn_grads1,))
    g_after, g_attn, g_some = call(
        back_mlp_rows_kernel,
        (shard_wide, shard, three),
        *terms,
        g0,
        aft0,
        att0,
        mods[0],
        after=(sum_b1,),
        saved=(0,),
    )
    terms, attn_grads0, g_taps0 = attn_backward(0, gather_plane(g_attn), attn0, (mlp_grads0,))
    g_in, g_mods0 = call(
        back_end_kernel,
        (shard, six),
        *terms,
        g_after,
        x0,
        mods[0],
        g_some,
        g_gate_two0,
        after=(attn_grads0,),
    )

    sum_b0, sum_a0 = scatter_rows(mlp_grads0), scatter_rows(attn_grads0)

    g_mod = jnp.stack([g_mods0.reshape(images, -1), g_mods1.reshape(images, -1)])
    g_mod = g_mod.reshape(sections, images, tensors, -1).transpose(0, 2, 1, 3)
    columns = g_mod.shape[3]
    g_mod = g_mod.reshape(sections, tensors, images * columns)
    taps_rows = taps_count + 1

    def small_grads(g_taps, g_up_bias):
        return jnp.concatenate([g_taps[:taps_rows].reshape(-1), g_up_bias.reshape(-1)])

    g_small = jnp.stack([small_grads(g_taps0, g_up_bias0), small_grads(g_taps1, g_up_bias1)])
    to_tensor = (jnp.arange(tensors) == t)[None, :, None]
    g_small = jnp.where(to_tensor, g_small[:, None], 0.0)
    g_sent = jnp.concatenate([g_mod, g_small], axis=2).reshape(sections * tensors, -1)
    g_parts = lax.all_to_all(
        g_sent, ("section", "tensor"), split_axis=0, concat_axis=0, tiled=True
    )
    g_parts, sum_b1, sum_a1 = lax.optimization_barrier((g_parts, sum_b1, sum_a1))
    other_b1, other_a1 = to_second(sum_b1), to_second(sum_a1)
    g_share = jnp.sum(g_parts[:, : images * columns], axis=0)
    small_parts = g_parts[:, images * columns :].reshape(sections, tensors, -1).sum(1)
    g_all = spread_over(jnp.concatenate([g_share, small_parts.reshape(-1)]), ("dp",))
    g_all, end_pieces, sum_b0 = lax.optimization_barrier((g_all, end_pieces, sum_b0))
    others = other_b1, other_a1, to_first(sum_b0)
    (block_out,) = call(
        end_kernel, (shard,), *scatter_plane(end_pieces[0], end_pieces[1:]), aft1, mods[1]
    )
    small_own = jnp.sum(g_all[:, images * columns :], axis=0).reshape(sections, -1)
    g_all = g_all[:, : images * columns].reshape(dps * images, columns).astype(BF16)
    grad_ada_bias = jnp.sum(g_all.astype(F32), axis=0)
    act_part = jnp.einsum("me,de->md", g_all, ada_weight[0], preferred_element_type=F32)
    act_all = lax.all_to_all(
        act_part.reshape(dps, images, slab), "dp", split_axis=0, concat_axis=0, tiled=True
    )
    act_all, others = lax.optimization_barrier((act_all, others))
    act_all = spread_over(act_all, ("section", "tensor"))
    act_all = jnp.sum(act_all, axis=0)
    act_grad = act_all.reshape(dps, images, slab).transpose(1, 0, 2).reshape(images, width)
    cond_grad = jax.vjp(jax.nn.silu, cond_vec)[1](act_grad)[0]

    ends_from_first = lax.ppermute(block_out, "section", [(0, 1)])
    ends_from_second = lax.ppermute(g_in, "section", [(1, 0)])
    mine = jnp.where(first, g_in, block_out)
    received = jnp.where(first, ends_from_second, ends_from_first)
    section_ends = jnp.concatenate(
        [jnp.where(first, mine, received), jnp.where(first, received, mine)], axis=1
    )
    cond_grad, section_ends, sum_a0, g_all, others = lax.optimization_barrier(
        (cond_grad, section_ends, sum_a0, g_all, others)
    )
    other_b1, other_a1, other_b0 = others
    other_a0 = to_first(sum_a0)
    grad_ada = jnp.einsum("md,me->de", slab_active, g_all, preferred_element_type=F32)

    small_taps = small_own[:, : taps_rows * wide].reshape(sections, taps_rows, wide)
    grad_gateb = small_taps[:, taps_count, tail : tail + heads].reshape(-1)
    grad_taps = small_taps[:, :taps_count, :channels].transpose(1, 0, 2)
    grad_taps = grad_taps.reshape(taps_count, sections * channels)
    up_halves = small_own[:, taps_rows * wide :]
    grad_up_bias = jnp.concatenate(
        [up_halves[:, :main].reshape(-1), up_halves[:, main : main + left].reshape(-1)]
    )

    grad_up, grad_down = call(
        functools.partial(unpack_mlp_kernel, left),
        (out(up_weight.shape[1:], F32),) * 2,
        section,
        sum_b0,
        other_b0,
        sum_b1,
        other_b1,
        scalars=1,
    )
    grad_down = grad_down.T
    grad_in, grad_gate, grad_out = call(
        functools.partial(unpack_attn_kernel, cfg),
        (
            out(in_weight.shape[1:], F32),
            out(gate_weight.shape[1:], F32),
            out((slab, out_weight.shape[1]), F32),
        ),
        section,
        sum_a0,
        other_a0,
        sum_a1,
        other_a1,
        scalars=1,
    )
    grad_out = grad_out.T

    return (
        section_ends[None],
        cond_grad,
        grad_ada[None],
        grad_ada_bias[None],
        grad_in[None],
        grad_gate[None],
        grad_gateb[None],
        grad_taps[None],
        grad_out[None],
        grad_up[None],
        grad_up_bias[None],
        grad_down[None],
    )


def solution(mesh):
    in_specs = (
        P("section", "dp", "tensor", None),
        P("dp", None),
        P("dp"),
        P("section", "dp", "tensor"),
        P("section", "tensor"),
        P("section", None, "dp", "tensor"),
        P("section", "dp", "tensor"),
        P("section", "tensor"),
        P("section", None, "tensor"),
        P("section", "tensor", "dp"),
        P("section", "dp", "tensor"),
        P("section", "tensor"),
        P("section", "tensor", "dp"),
    )
    out_specs = (
        P("section", "dp", "tensor", None),
        P("dp", None),
        P("section", "dp", "tensor"),
        P("section", "tensor"),
        P("section", None, "dp", "tensor"),
        P("section", "dp", "tensor"),
        P("section", "tensor"),
        P("section", None, "tensor"),
        P("section", "tensor", "dp"),
        P("section", "dp", "tensor"),
        P("section", "tensor"),
        P("section", "tensor", "dp"),
    )
    return jax.shard_map(
        per_device, mesh=mesh, in_specs=in_specs, out_specs=out_specs, check_vma=False
    )
```

```python
import functools
import math

import jax
import jax.numpy as jnp
from jax import lax
from jax.experimental import pallas as pl
from jax.experimental.pallas import tpu as pltpu
from jax.sharding import PartitionSpec as P

SIDE = 16
PATCHES = SIDE * SIDE
LANES = 128
F32 = jnp.float32
BF16 = jnp.bfloat16
HIGHEST = lax.Precision.HIGHEST
PLANE = ("tensor", "section")


class Traffic:
    def __init__(self, arriving, leaving):
        self.arriving, self.leaving, self.left = arriving, leaving, set()

    def wait(self, *places):
        for at in places:
            self.arriving[at].wait()

    def flush(self, *places):
        for at in places:
            self.leaving[at].start()
            self.left.add(at)


class Columns:
    def __init__(self, array, start, width):
        self.array, self.start = array, start
        self.shape, self.dtype = (array.shape[0], width), array.dtype
        self.size = array.shape[0] * width

    def source(self, ref):
        return ref.at[:, self.start : self.start + self.shape[1]]


def call(body, outs, *args, scalars=0, flops=0, scratch=(), after=(), streamed=(), saved=()):
    count, waits, many = len(args), len(after), len(outs)
    given = args
    moving = bool(streamed or saved)

    def kernel(*refs):
        ins, out_refs = list(refs[:count]), list(refs[count + waits : count + waits + many])
        rest = refs[count + waits + many :]
        own, held = rest[: len(scratch)], rest[len(scratch) :]
        arriving, leaving = {}, {}
        for i, at in enumerate(streamed):
            source = given[at].source(ins[at]) if isinstance(given[at], Columns) else ins[at]
            arriving[at] = pltpu.make_async_copy(source, held[i], held[-1].at[i])
            ins[at] = held[i]
        for i, at in enumerate(saved, len(streamed)):
            leaving[at] = pltpu.make_async_copy(held[i], out_refs[at], held[-1].at[i])
            out_refs[at] = held[i]
        traffic = Traffic(arriving, leaving)
        for copy in arriving.values():
            copy.start()
        if moving:
            body(traffic, *ins, *out_refs, *own)
        else:
            body(*ins, *out_refs, *own)
        traffic.flush(*[at for at in saved if at not in traffic.left])
        for copy in leaving.values():
            copy.wait()

    moved = sum(a.size * a.dtype.itemsize for a in args)
    moved += sum(math.prod(o.shape) * o.dtype.itemsize for o in outs)
    specs = [pl.BlockSpec(memory_space=pltpu.SMEM)] * scalars
    specs += [
        pl.BlockSpec(memory_space=pltpu.HBM if i in streamed else pltpu.VMEM)
        for i in range(scalars, count)
    ]
    large = [a.size > 2**17 for a in after]
    specs += [pl.BlockSpec(memory_space=pltpu.HBM if v else pl.ANY) for v in large]
    after = [
        pltpu.with_memory_space_constraint(a, pltpu.HBM) if v else a for a, v in zip(after, large)
    ]
    spaces = [pltpu.HBM if i in saved else pltpu.VMEM for i in range(many)]
    shapes = [
        pltpu.HBM(o.shape, o.dtype) if i in saved else o for i, o in enumerate(outs)
    ]
    args = [a.array if isinstance(a, Columns) else a for a in args]
    args = [
        pltpu.with_memory_space_constraint(a, pltpu.HBM) if i in streamed else a
        for i, a in enumerate(args)
    ]
    hold = [pltpu.VMEM(given[i].shape, given[i].dtype) for i in streamed]
    hold += [pltpu.VMEM(outs[i].shape, outs[i].dtype) for i in saved]
    if moving:
        hold.append(pltpu.SemaphoreType.DMA((len(hold),)))
    return pl.pallas_call(
        kernel,
        out_shape=tuple(shapes),
        in_specs=specs,
        out_specs=tuple(pl.BlockSpec(memory_space=space) for space in spaces),
        scratch_shapes=[*scratch, *hold],
        compiler_params=pltpu.CompilerParams(vmem_limit_bytes=6 * 2**20 + moved * 3 // 2),
        cost_estimate=pl.CostEstimate(flops=flops, bytes_accessed=moved, transcendentals=0),
    )(*args, *after)


def out(shape, dtype):
    return jax.ShapeDtypeStruct(shape, dtype)


def mm(a, b):
    return lax.dot_general(a, b, (((1,), (0,)), ((), ())), preferred_element_type=F32)


def mm_nt(a, b):
    return lax.dot_general(a, b, (((1,), (1,)), ((), ())), preferred_element_type=F32)


def mm_tn(a, b):
    return lax.dot_general(a, b, (((0,), (0,)), ((), ())), preferred_element_type=F32)


def normalize(v):
    centered = v - jnp.mean(v, axis=-1, keepdims=True)
    scale = lax.rsqrt(jnp.mean(centered * centered, axis=-1, keepdims=True) + 1e-06)
    return centered * scale, scale


def norm_grad(hat, rstd, grad):
    inner = jnp.mean(grad * hat, axis=-1, keepdims=True)
    return rstd * (grad - jnp.mean(grad, axis=-1, keepdims=True) - hat * inner)


def gather_total(pieces):
    total = pieces[0][...].astype(F32)
    for piece in pieces[1:]:
        total = total + piece[...].astype(F32)
    return total


def rows_sum(v):
    return jnp.sum(v, axis=0, keepdims=True)


def gelu_terms(x):
    k = math.sqrt(2.0 / math.pi)
    th = jnp.tanh(k * (x + 0.044715 * x * x * x))
    value = 0.5 * x * (1.0 + th)
    slope = 0.5 * (1.0 + th) + 0.5 * x * (1.0 - th * th) * k * (1.0 + 3 * 0.044715 * x * x)
    return value, slope


def start_kernel(x_ref, mod_ref, n_ref):
    for m in range(x_ref.shape[0]):
        hat, _ = normalize(x_ref[m].astype(F32))
        n_ref[m] = (hat * (1.0 + mod_ref[m, 1:2]) + mod_ref[m, 0:1]).astype(BF16)


def add_kernel(a, b, c, d, recv, *outs):
    for j, own in enumerate((a, b, c, d)):
        outs[j][...] = (own[...].astype(F32) + recv[j].astype(F32)).astype(BF16)


def add_late_kernel(traffic, a, b, c, d, recv, *outs):
    traffic.wait(0, 1, 2, 3)
    add_kernel(a, b, c, d, recv, *outs)


def after_attn_kernel(traffic, p0, p1, p2, p3, x_ref, mod_ref, att_ref, aft_ref, n_ref):
    for m in range(x_ref.shape[0]):
        att = gather_total([p.at[m] for p in (p0, p1, p2, p3)])
        aft = x_ref[m].astype(F32) + mod_ref[m, 2:3] * att
        hat, _ = normalize(aft)
        att_ref[m] = att
        aft_ref[m] = aft
        n_ref[m] = (hat * (1.0 + mod_ref[m, 4:5]) + mod_ref[m, 3:4]).astype(BF16)


def between_kernel(traffic, p0, p1, p2, p3, aft_ref, mod_ref, next_ref, mlp_ref, x_ref, n_ref):
    for m in range(aft_ref.shape[0]):
        mlp = gather_total([p.at[m] for p in (p0, p1, p2, p3)])
        x = (aft_ref[m] + mod_ref[m, 5:6] * mlp).astype(BF16)
        hat, _ = normalize(x.astype(F32))
        mlp_ref[m] = mlp
        x_ref[m] = x
        n_ref[m] = (hat * (1.0 + next_ref[m, 1:2]) + next_ref[m, 0:1]).astype(BF16)


def end_kernel(p0, p1, p2, p3, aft_ref, mod_ref, x_ref):
    for m in range(aft_ref.shape[0]):
        mlp = gather_total([p.at[m] for p in (p0, p1, p2, p3)])
        x_ref[m] = (aft_ref[m] + mod_ref[m, 5:6] * mlp).astype(BF16)


def back_mlp_rows_kernel(traffic, p0, p1, p2, p3, g_ref, aft_ref, att_ref, mod_ref, ga_ref, gt_ref, gm_ref):
    for m in range(aft_ref.shape[0]):
        gn = gather_total([p.at[m] for p in (p0, p1, p2, p3)])
        hat, rstd = normalize(aft_ref[m])
        grad = g_ref[m].astype(F32) + norm_grad(hat, rstd, gn * (1.0 + mod_ref[m, 4:5]))
        ga_ref[m] = grad
        gt_ref[m] = (mod_ref[m, 2:3] * grad).astype(BF16)
        gm_ref[m, 0:1] = rows_sum(grad * att_ref[m])
        gm_ref[m, 1:2] = rows_sum(gn)
        gm_ref[m, 2:3] = rows_sum(gn * hat)


def back_attn_rows(pieces, ga_ref, x_ref, mod_ref, some_ref, gate_ref, gm_ref, m):
    gn = gather_total([p.at[m] for p in pieces])
    hat, rstd = normalize(x_ref[m].astype(F32))
    grad = ga_ref[m] + norm_grad(hat, rstd, gn * (1.0 + mod_ref[m, 1:2]))
    gm_ref[m, 0:1] = rows_sum(gn)
    gm_ref[m, 1:2] = rows_sum(gn * hat)
    gm_ref[m, 2:5] = some_ref[m]
    gm_ref[m, 5:6] = gate_ref[m]
    return grad.astype(BF16)


def back_between_kernel(p0, p1, p2, p3, ga_ref, x_ref, mod_ref, some_ref, gate_ref, prev_ref, mlp_ref, *outs):
    g_ref, gmlp_ref, gm_ref, next_ref = outs
    for m in range(x_ref.shape[0]):
        grad = back_attn_rows((p0, p1, p2, p3), ga_ref, x_ref, mod_ref, some_ref, gate_ref, gm_ref, m)
        g_ref[m] = grad
        wide = grad.astype(F32)
        gmlp_ref[m] = (prev_ref[m, 5:6] * wide).astype(BF16)
        next_ref[m] = rows_sum(wide * mlp_ref[m])


def back_end_kernel(p0, p1, p2, p3, ga_ref, x_ref, mod_ref, some_ref, gate_ref, g_ref, gm_ref):
    for m in range(x_ref.shape[0]):
        g_ref[m] = back_attn_rows((p0, p1, p2, p3), ga_ref, x_ref, mod_ref, some_ref, gate_ref, gm_ref, m)


def scan_mask(columns_first):
    def place(number):
        if columns_first:
            return (number % SIDE) * SIDE + number // SIDE
        return number

    shape = (PATCHES, PATCHES)
    later = place(lax.broadcasted_iota(jnp.int32, shape, 0))
    return later >= place(lax.broadcasted_iota(jnp.int32, shape, 1))


def grid_column():
    return lax.broadcasted_iota(jnp.int32, (PATCHES, 1), 0) % SIDE


def side_shifts(a, column):
    left = jnp.where(column == 0, 0.0, pltpu.roll(a, 1, 0))
    right = jnp.where(column == SIDE - 1, 0.0, pltpu.roll(a, PATCHES - 1, 0))
    return left, a, right


def convolve(shifted, tap):
    sums = []
    for row in range(3):
        terms = [shifted[col] * tap(3 * row + col) for col in range(3)]
        sums.append(terms[0] + terms[1] + terms[2])
    zeros = jnp.zeros((SIDE, sums[0].shape[1]), F32)
    above = jnp.concatenate([zeros, sums[0][:-SIDE]], axis=0)
    below = jnp.concatenate([sums[2][SIDE:], zeros], axis=0)
    return shifted[1] + sums[1] + above + below


def tap_grads(shifted, grad):
    found = []
    for row in range(3):
        for col in range(3):
            if row == 0:
                product = shifted[col][:-SIDE] * grad[SIDE:]
            elif row == 1:
                product = shifted[col] * grad
            else:
                product = shifted[col][SIDE:] * grad[:-SIDE]
            found.append(rows_sum(product))
    return found


def lane_sets(width, first, head_width, heads):
    lane = lax.broadcasted_iota(jnp.int32, (1, width), 1)
    return [
        (lane >= first + h * head_width) & (lane < first + (h + 1) * head_width)
        for h in range(heads)
    ]


def decay_parts(logits, mask, gate_lane, heads):
    rates = -(jnp.maximum(logits, 0.0) + jnp.log1p(jnp.exp(-jnp.abs(logits))))
    ones = jnp.where(mask, 1.0, 0.0)
    totals = lax.dot_general(
        ones, rates, (((1,), (0,)), ((), ())), precision=HIGHEST, preferred_element_type=F32
    )
    turned = totals.T
    decays = []
    for h in range(heads):
        at = gate_lane + h
        spans = jnp.where(mask, totals[:, at : at + 1] - turned[at : at + 1, :], -1e30)
        w = jnp.exp(spans)
        decays.append((w, jnp.sum(w, axis=1, keepdims=True)))
    return decays, ones


def send_order(k):
    return (0, 1, None, None, 2, 3, None, None)[k], (None, None, 0, 1, None, None, 2, 3)[k]


def write_pieces(me, total_ref, other_ref, own_refs):
    rows = total_ref.shape[1] // 8
    for k in range(8):
        spot = pl.ds(pl.multiple_of(jnp.bitwise_xor(me, k) * rows, rows), rows)
        own, other = send_order(k)
        if own is None:
            other_ref[other] = total_ref[:, spot, :]
        else:
            own_refs[own][...] = total_ref[:, spot, :]


def each_shard(refs):
    own, x, y, xy, core, core_x, core_y, core_xy = refs
    return own, x, core, core_x, y, xy, core_y, core_xy


def gather_pieces(me, shard_refs, full_ref):
    rows = full_ref.shape[1] // 8
    for k, shard in enumerate(each_shard(shard_refs)):
        spot = pl.ds(pl.multiple_of(jnp.bitwise_xor(me, k) * rows, rows), rows)
        full_ref[:, spot, :] = shard[...]


def tail_spots(heads):
    return (0, 32, 48, 64, 80)


def join_tail(packed, piece, tails, lane):
    tile = packed[:, piece * LANES : (piece + 1) * LANES]
    return jnp.concatenate([tile, pltpu.roll(tails, (LANES - lane) % LANES, 1)], axis=1)


def lanes():
    return lax.broadcasted_iota(jnp.int32, (1, LANES), 1)


def half_tiles(tiles, at):
    if at == 0:
        return tiles[0], tiles[1]
    shift = 2 * LANES - at
    first = jnp.where(lanes() < shift, pltpu.roll(tiles[1], shift, 1), pltpu.roll(tiles[2], shift, 1))
    return first, pltpu.roll(tiles[2], shift, 1)


def pack_attn_kernel(cfg, traffic, sec_ref, in_ref, gate_ref, out_ref, keep_ref, send_ref):
    heads, channels = cfg
    traffic.wait(1)
    spots = tail_spots(heads)
    tail = channels - LANES
    rows = in_ref.shape[1]
    short = jnp.zeros((rows, 3 * LANES - 2 * channels), F32)
    keep_first = sec_ref[0] == 0
    lane = lanes()
    tails = [gate_ref[...], pltpu.roll(gate_ref[...], LANES - heads, 1)]
    tails = [
        jnp.where((lane >= tail) & (lane < tail + heads), pltpu.roll(v, tail, 1), 0.0) for v in tails
    ]
    for j in range(5):
        ref = out_ref if j == 4 else in_ref.at[j]
        tiles = [ref[:, :LANES].astype(F32), ref[:, LANES : 2 * LANES].astype(F32)]
        tiles.append(jnp.concatenate([ref[:, 2 * LANES :].astype(F32), short], axis=1))
        whole = []
        for h in range(2):
            tile, rest = half_tiles(tiles, h * channels)
            whole.append(tile)
            tails[h] = tails[h] + pltpu.roll(jnp.where(lane < tail, rest, 0.0), spots[j], 1)
        cols = slice(j * LANES, (j + 1) * LANES)
        keep_ref[:, cols] = jnp.where(keep_first, whole[0], whole[1]).astype(BF16)
        send_ref[:, cols] = jnp.where(keep_first, whole[1], whole[0]).astype(BF16)
    cols = slice(5 * LANES, 6 * LANES)
    keep_ref[:, cols] = jnp.where(keep_first, tails[0], tails[1]).astype(BF16)
    send_ref[:, cols] = jnp.where(keep_first, tails[1], tails[0]).astype(BF16)


def pack_mlp_kernel(left, traffic, sec_ref, up_ref, down_ref, keep_b_ref, send_b_ref):
    keep_first = sec_ref[0] == 0
    lane = lanes()
    main = (keep_b_ref.shape[1] - LANES) // 2
    traffic.wait(1)
    at = 0
    for ref in (up_ref, down_ref):
        low, high = ref[:, :main], ref[:, main : 2 * main]
        keep_b_ref[:, at : at + main] = jnp.where(keep_first, low, high)
        send_b_ref[:, at : at + main] = jnp.where(keep_first, high, low)
        at += main
    up, down = (ref[:, 2 * main :].astype(F32) for ref in (up_ref, down_ref))
    low = jnp.where(lane < left, up, pltpu.roll(down, left, 1)).astype(BF16)
    high = jnp.where(lane < left, pltpu.roll(up, left, 1), down).astype(BF16)
    keep_b_ref[:, at:] = jnp.where(keep_first, low, high)
    send_b_ref[:, at:] = jnp.where(keep_first, high, low)


def unpack_mlp_kernel(left, sec_ref, sum0_ref, other0_ref, sum1_ref, other1_ref, up_ref, down_ref):
    in_first = sec_ref[0] == 0
    main = (sum0_ref.shape[1] - LANES) // 2
    lane = lanes()

    def both(cols):
        low = jnp.where(in_first, sum0_ref[:, cols], other1_ref[:, cols])
        return low.astype(F32), jnp.where(in_first, other0_ref[:, cols], sum1_ref[:, cols]).astype(F32)

    up_ref[:, :main], up_ref[:, main : 2 * main] = both(slice(0, main))
    down_ref[:, :main], down_ref[:, main : 2 * main] = both(slice(main, 2 * main))
    low, high = both(slice(2 * main, 2 * main + LANES))
    up_ref[:, 2 * main :] = jnp.where(lane < left, low, pltpu.roll(high, left, 1))
    down_ref[:, 2 * main :] = jnp.where(lane < left, pltpu.roll(low, LANES - left, 1), high)


def unpack_attn_kernel(
    cfg, sec_ref, sum0_ref, other0_ref, sum1_ref, other1_ref, in_ref, gate_ref, out_ref
):
    heads, channels = cfg
    spots = tail_spots(heads)
    tail = channels - LANES
    in_first = sec_ref[0] == 0
    lane = lanes()
    shift = channels - LANES

    def both(cols):
        low = jnp.where(in_first, sum0_ref[:, cols], other1_ref[:, cols])
        return low.astype(F32), jnp.where(in_first, other0_ref[:, cols], sum1_ref[:, cols]).astype(F32)

    low_tails, high_tails = both(slice(5 * LANES, 6 * LANES))
    for j in range(5):
        ref = out_ref if j == 4 else in_ref.at[j]
        low, high = both(slice(j * LANES, (j + 1) * LANES))
        ref[:, :LANES] = low
        high = pltpu.roll(high, shift, 1)
        low_tail = pltpu.roll(low_tails, (LANES - spots[j]) % LANES, 1)
        high_tail = pltpu.roll(high_tails, (LANES - spots[j] + shift) % LANES, 1)
        ref[:, LANES : 2 * LANES] = jnp.where(lane < tail, low_tail, high)
        last = jnp.where(lane < shift, high, high_tail)
        ref[:, 2 * LANES :] = last[:, : 2 * channels - 2 * LANES]
    low_gate = pltpu.roll(low_tails, LANES - tail, 1)
    high_gate = pltpu.roll(high_tails, LANES - tail + heads, 1)
    gate_ref[...] = jnp.where(lane < heads, low_gate, high_gate)[:, : 2 * heads]


def attn_forward_kernel(cfg, traffic, me_ref, *refs):
    columns_first, heads, head_width = cfg
    shards, (w_ref, gb_ref, tap_ref) = refs[:8], refs[8:11]
    n_ref, proj_ref, log_ref, attn_ref, mix_ref, other_ref = refs[11:17]
    own_refs, total_ref = refs[17:21], refs[21]
    me = me_ref[0]
    wide = 2 * LANES
    gate_lane = heads * head_width - LANES
    spots = tail_spots(heads)
    mask = scan_mask(columns_first)
    column = grid_column()
    sets = lane_sets(wide, 0, head_width, heads)
    gather_pieces(me, shards, n_ref)
    traffic.flush(0)
    traffic.wait(9)
    for m in range(n_ref.shape[0]):
        projected = mm(n_ref[m], w_ref[:, : 4 * LANES])
        tails = mm(n_ref[m], w_ref[:, 5 * LANES :])
        logits = tails + gb_ref[...]
        log_ref[m] = logits
        decays, _ = decay_parts(logits, mask, gate_lane, heads)
        query, key, value, gate = (join_tail(projected, j, tails, spots[j]) for j in range(4))
        in_head = sets[0]
        for own in sets[1:]:
            in_head = in_head | own
        query, key, value = (jnp.where(in_head, v, 0.0).astype(BF16) for v in (query, key, value))
        gate = gate.astype(BF16)
        for j, v in enumerate((query, key, value, gate)):
            proj_ref[m, :, j * wide : (j + 1) * wide] = v
        attn = None
        for h in range(heads):
            w, mass = decays[h]
            raw = mm_nt(jnp.where(sets[h], query, jnp.zeros_like(query)), key)
            scores = (raw * head_width ** (-0.5) * w).astype(BF16)
            normed = mm(scores, value) * lax.rsqrt(mass)
            attn = jnp.where(sets[h], normed, 0.0 if attn is None else attn)
        attn_ref[m] = attn
        spread = convolve(side_shifts(attn, column), lambda i: tap_ref[i : i + 1, :])
        gate = gate.astype(F32)
        mixed = spread * (gate * jax.nn.sigmoid(gate))
        mixed = jnp.where(in_head, mixed, 0.0)
        mixed = jnp.concatenate(
            [mixed[:, :LANES], pltpu.roll(mixed[:, LANES:], spots[4], 1)], axis=1
        ).astype(BF16)
        mix_ref[m] = mixed
        if m == n_ref.shape[0] - 1:
            traffic.flush(1, 2, 3, 4)
        total_ref[m] = mm_nt(mixed, w_ref[:, 4 * LANES :]).astype(BF16)
    write_pieces(me, total_ref, other_ref, own_refs)


def attn_backward_kernel(cfg, traffic, me_ref, *refs):
    columns_first, heads, head_width = cfg
    shards, (proj_ref, log_ref, attn_ref, w_ref, tap_ref) = refs[:8], refs[8:13]
    g_ref, gproj_ref, gtap_ref, other_ref = refs[13:17]
    own_refs, total_ref = refs[17:21], refs[21]
    me = me_ref[0]
    wide = 2 * LANES
    gate_lane = heads * head_width - LANES
    spots = tail_spots(heads)
    scale = head_width ** (-0.5)
    mask = scan_mask(columns_first)
    column = grid_column()
    sets = lane_sets(wide, 0, head_width, heads)
    gate_sets = lane_sets(LANES, gate_lane, 1, heads)
    sublane = lax.broadcasted_iota(jnp.int32, (LANES, 1), 0)
    in_head = sets[0]
    for own in sets[1:]:
        in_head = in_head | own
    gather_pieces(me, shards, g_ref)
    gtap_ref[...] = jnp.zeros(gtap_ref.shape, F32)
    traffic.wait(9, 10, 11, 12)
    for m in range(g_ref.shape[0]):
        g_packed = mm(g_ref[m], w_ref[:, 4 * LANES :])
        g_mixed = jnp.where(in_head, join_tail(g_packed, 0, g_packed[:, LANES:], spots[4]), 0.0)
        query, key, value, gate = (proj_ref[m, :, j * wide : (j + 1) * wide] for j in range(4))
        gate = gate.astype(F32)
        sig = jax.nn.sigmoid(gate)
        attn = attn_ref[m]
        shifted = side_shifts(attn, column)
        spread = convolve(shifted, lambda i: tap_ref[i : i + 1, :])
        g_spread = g_mixed * (gate * sig)
        g_gate = g_mixed * spread * (sig * (1.0 + gate * (1.0 - sig)))
        for i, grad in enumerate(tap_grads(shifted, g_spread)):
            gtap_ref[i : i + 1, :] = grad if m == 0 else gtap_ref[i : i + 1, :] + grad
        g_attn = convolve(side_shifts(g_spread, column), lambda i: tap_ref[8 - i : 9 - i, :])
        logits = log_ref[m]
        decays, ones = decay_parts(logits, mask, gate_lane, heads)
        g_query = g_key = g_value = 0.0
        across = jnp.zeros((PATCHES, LANES), F32)
        down = jnp.zeros((LANES, PATCHES), F32)
        for h in range(heads):
            w, mass = decays[h]
            own_query = jnp.where(sets[h], query, jnp.zeros_like(query))
            raw = mm_nt(own_query, key) * scale
            own_grad = jnp.where(sets[h], g_attn, 0.0)
            g_mass = -0.5 * jnp.sum(own_grad * attn, axis=1, keepdims=True) / mass
            g_out = (own_grad * lax.rsqrt(mass)).astype(BF16)
            g_value = g_value + mm_tn((raw * w).astype(BF16), g_out)
            g_scores = mm_nt(g_out, value)
            g_raw = (g_scores * w * scale).astype(BF16)
            g_query = jnp.where(sets[h], mm(g_raw, key), g_query)
            g_key = g_key + mm_tn(g_raw, own_query)
            g_span = (g_scores * raw + g_mass) * w
            across = jnp.where(gate_sets[h], jnp.sum(g_span, axis=1, keepdims=True), across)
            down = jnp.where(sublane == gate_lane + h, rows_sum(g_span), down)
        g_rates = lax.dot_general(
            ones,
            across - down.T,
            (((0,), (0,)), ((), ())),
            precision=HIGHEST,
            preferred_element_type=F32,
        )
        g_logits = (-g_rates * jax.nn.sigmoid(logits)).astype(BF16).astype(F32)
        g_bias = rows_sum(g_logits)
        gtap_ref[9:10, :LANES] = g_bias if m == 0 else gtap_ref[9:10, :LANES] + g_bias
        tails = g_logits
        for j, v in enumerate((g_query, g_key, g_value, g_gate)):
            gproj_ref[m, :, j * LANES : (j + 1) * LANES] = v[:, :LANES].astype(BF16)
            tails = tails + pltpu.roll(v[:, LANES:], spots[j], 1)
        gproj_ref[m, :, 4 * LANES :] = tails.astype(BF16)
        total = mm_nt(gproj_ref[m, :, : 4 * LANES], w_ref[:, : 4 * LANES])
        total = total + mm_nt(gproj_ref[m, :, 4 * LANES :], w_ref[:, 5 * LANES :])
        total_ref[m] = total.astype(BF16)
    write_pieces(me, total_ref, other_ref, own_refs)


def attn_weights_kernel(traffic, n_ref, gproj_ref, g_ref, mix_ref, gw_ref):
    traffic.wait(0, 3)
    for part in range(2):
        cols = slice(part * 2 * LANES, (part + 1) * 2 * LANES)
        total = mm_tn(n_ref[0], gproj_ref[0, :, cols])
        for m in range(1, n_ref.shape[0]):
            total = total + mm_tn(n_ref[m], gproj_ref[m, :, cols])
        gw_ref[:, cols] = total.astype(BF16)
    total = mm_tn(g_ref[0], mix_ref[0])
    tails = mm_tn(n_ref[0], gproj_ref[0, :, 4 * LANES :])
    for m in range(1, n_ref.shape[0]):
        total = total + mm_tn(g_ref[m], mix_ref[m])
        tails = tails + mm_tn(n_ref[m], gproj_ref[m, :, 4 * LANES :])
    gw_ref[:, 4 * LANES : 5 * LANES] = total[:, :LANES].astype(BF16)
    gw_ref[:, 5 * LANES :] = (total[:, LANES:] + tails).astype(BF16)


def stack_shards(shards, full_ref):
    for k, shard in enumerate(each_shard(shards)):
        images, rows, width = shard.shape
        full_ref[k * images * rows : (k + 1) * images * rows, :] = shard[...].reshape(
            images * rows, width
        )


def stack_kernel(traffic, *refs):
    stack_shards(refs[:8], refs[8])


def put_shard(k, value, shape, other_ref, own_refs):
    own, other = send_order(k)
    if own is None:
        other_ref[other] = value.astype(BF16).reshape(shape)
    else:
        own_refs[own][...] = value.astype(BF16).reshape(shape)


def put_shards(total, shape, other_ref, own_refs):
    rows = total.shape[0] // 8
    for k in range(8):
        put_shard(k, total[k * rows : (k + 1) * rows], shape, other_ref, own_refs)


def mlp_forward_kernel(left, traffic, *refs):
    shards, (w_ref, ub_ref) = refs[:8], refs[8:10]
    n_ref, pre_ref, hid_ref, other_ref = refs[10:14]
    own_refs = refs[14:18]
    main = (w_ref.shape[1] - LANES) // 2
    stack_shards(shards, n_ref)
    traffic.flush(0)
    traffic.wait(8)
    n = n_ref[...]
    pre = mm(n, w_ref[:, :main]) + ub_ref[:, :main]
    pre_ref[:, :main] = pre
    hidden = gelu_terms(pre)[0].astype(BF16)
    hid_ref[:, :main] = hidden
    last = mm(n, w_ref[:, 2 * main :]) + ub_ref[:, main:]
    pre_ref[:, main:] = last
    lane = lax.broadcasted_iota(jnp.int32, (1, LANES), 1)
    tail = jnp.where(lane < left, gelu_terms(last)[0], 0.0)
    tail = pltpu.roll(tail, LANES - left, 1).astype(BF16)
    hid_ref[:, main:] = tail
    traffic.flush(1, 2)
    total = mm_nt(hidden, w_ref[:, main : 2 * main]) + mm_nt(tail, w_ref[:, 2 * main :])
    put_shards(total, shards[0].shape, other_ref, own_refs)


def mlp_backward_kernel(left, traffic, *refs):
    given, (pre_ref, w_ref) = refs[:8], refs[8:10]
    g_ref, rest = refs[10], refs[11:]
    stack_shards(given, g_ref)
    traffic.wait(8, 9)
    gpre_ref, gub_ref, other_ref = rest[:3]
    own_refs = rest[3:]
    main = (w_ref.shape[1] - LANES) // 2
    g = g_ref[...]
    g_pre = mm(g, w_ref[:, main : 2 * main]) * gelu_terms(pre_ref[:, :main])[1]
    g_pre = g_pre.astype(BF16)
    gpre_ref[:, :main] = g_pre
    gub_ref[:, :main] = rows_sum(g_pre.astype(F32))
    lane = lax.broadcasted_iota(jnp.int32, (1, LANES), 1)
    last = pltpu.roll(mm(g, w_ref[:, 2 * main :]), left, 1) * gelu_terms(pre_ref[:, main:])[1]
    last = jnp.where(lane < left, last, 0.0).astype(BF16)
    gpre_ref[:, main:] = last
    gub_ref[:, main:] = rows_sum(last.astype(F32))
    total = mm_nt(g_pre, w_ref[:, :main]) + mm_nt(last, w_ref[:, 2 * main :])
    put_shards(total, own_refs[0].shape, other_ref, own_refs)


def mlp_both_kernel(left, traffic, n_ref, raw_ref, w_ref, ub_ref, mod_ref, *refs):
    gw_ref, gub_ref, gate_ref, other_ref = refs[:4]
    own_refs, end_ref, end_refs = refs[4:8], refs[8], refs[9:13]
    g_ref = refs[13]
    images, rows = own_refs[0].shape[:2]
    main = (w_ref.shape[1] - LANES) // 2
    lane = lax.broadcasted_iota(jnp.int32, (1, LANES), 1)
    spans = [(i % images, slice(i * rows, (i + 1) * rows)) for i in range(8 * images)]
    traffic.wait(0, 1)
    for m, span in spans:
        g_ref[span] = (mod_ref[m, 5:6] * raw_ref[span].astype(F32)).astype(BF16)
    traffic.wait(2)
    n, g = n_ref[...], g_ref[...]
    value, slope = gelu_terms(mm(n, w_ref[:, :main]) + ub_ref[:, :main])
    hidden = value.astype(BF16)
    g_pre = (mm(g, w_ref[:, main : 2 * main]) * slope).astype(BF16)
    value, slope = gelu_terms(mm(n, w_ref[:, 2 * main :]) + ub_ref[:, main:])
    tail = pltpu.roll(jnp.where(lane < left, value, 0.0), LANES - left, 1).astype(BF16)
    last = pltpu.roll(mm(g, w_ref[:, 2 * main :]), left, 1) * slope
    last = jnp.where(lane < left, last, 0.0).astype(BF16)
    gw_ref[:, :main] = mm_tn(n, g_pre).astype(BF16)
    gw_ref[:, main : 2 * main] = mm_tn(g, hidden).astype(BF16)
    gw_ref[:, 2 * main :] = (mm_tn(n, last) + mm_tn(g, tail)).astype(BF16)
    traffic.flush(0)
    gub_ref[:, :main] = rows_sum(g_pre.astype(F32))
    gub_ref[:, main:] = rows_sum(last.astype(F32))
    total = mm_nt(hidden, w_ref[:, main : 2 * main]) + mm_nt(tail, w_ref[:, 2 * main :])
    put_shards(total, own_refs[0].shape, end_ref, end_refs)
    traffic.flush(8, 9, 10, 11, 12)
    gates = [0.0] * images
    for m, span in spans:
        gates[m] = gates[m] + rows_sum(raw_ref[span].astype(F32) * total[span])
    for m in range(images):
        gate_ref[m] = gates[m]
    total = mm_nt(g_pre, w_ref[:, :main]) + mm_nt(last, w_ref[:, 2 * main :])
    put_shards(total, own_refs[0].shape, other_ref, own_refs)


def mlp_weights_kernel(traffic, n_ref, gpre_ref, g_ref, hid_ref, gw_ref):
    main = gpre_ref.shape[1] - LANES
    traffic.wait(0, 3)
    gw_ref[:, :main] = mm_tn(n_ref[...], gpre_ref[:, :main]).astype(BF16)
    gw_ref[:, main : 2 * main] = mm_tn(g_ref[...], hid_ref[:, :main]).astype(BF16)
    last = mm_tn(n_ref[...], gpre_ref[:, main:]) + mm_tn(g_ref[...], hid_ref[:, main:])
    gw_ref[:, 2 * main :] = last.astype(BF16)


def swap(value, tensor_bits, section_bit):
    tensors, sections = lax.axis_size("tensor"), lax.axis_size("section")
    route = [
        (t * sections + s, (t ^ tensor_bits) * sections + (s ^ section_bit))
        for t in range(tensors)
        for s in range(sections)
    ]
    return lax.ppermute(value, PLANE, route)


def gather_plane(own):
    xy, x, y = swap(own, 2, 1), swap(own, 0, 1), swap(own, 2, 0)
    return own, x, y, xy, *(swap(v, 1, 0) for v in (own, x, y, xy))


def scatter_plane(other, own, late=False):
    received = swap(other, 1, 0)
    sums = call(
        add_late_kernel if late else add_kernel,
        (out(own[0].shape, BF16),) * 4,
        *own,
        received,
        streamed=(0, 1, 2, 3) if late else (),
    )
    return (sums[0], swap(sums[3], 2, 1), swap(sums[1], 0, 1), swap(sums[2], 2, 0))


def spread_over(value, axes):
    count = math.prod(lax.axis_size(a) for a in axes)
    copies = jnp.broadcast_to(value[None], (count,) + value.shape)
    return lax.all_to_all(copies, axes, split_axis=0, concat_axis=0, tiled=True)


def gather_all(own):
    return lax.all_gather(own, "dp", axis=0, tiled=True)


def scatter_rows(partial):
    return lax.psum_scatter(partial, "dp", scatter_dimension=0, tiled=True)


def sinusoid(time_steps, channels):
    half_width = channels // 2
    frequency = jnp.exp(
        jnp.arange(half_width, dtype=jnp.float32) * (-math.log(10000.0) / half_width)
    )
    angles = time_steps.astype(jnp.float32)[:, None] * frequency[None, :]
    return jnp.concatenate([jnp.cos(angles), jnp.sin(angles)], axis=1)


def per_device(
    section_inputs,
    condition,
    timesteps,
    ada_weight,
    ada_bias,
    in_weight,
    gate_weight,
    gate_bias,
    conv_taps,
    out_weight,
    up_weight,
    up_bias,
    down_weight,
):
    d = lax.axis_index("dp")
    t = lax.axis_index("tensor")
    s = lax.axis_index("section")
    dps, tensors, sections = (lax.axis_size(a) for a in ("dp", "tensor", "section"))
    first = s == 0
    me = (t * sections + s).astype(jnp.int32).reshape(1)
    images = condition.shape[0]
    width = condition.shape[1]
    slab = in_weight.shape[2]
    heads = gate_weight.shape[2] // sections
    channels = in_weight.shape[3] // sections
    head_width = channels // heads
    units = up_weight.shape[2] // sections
    wide = 2 * LANES
    tail = channels - LANES
    rows = section_inputs.shape[2] // sections
    main = units // LANES * LANES
    left = units - main
    spots = tail_spots(heads)

    def cut(value, axis):
        half = value.shape[axis] // 2
        return (
            lax.slice_in_dim(value, 0, half, axis=axis),
            lax.slice_in_dim(value, half, 2 * half, axis=axis),
        )

    def swap_halves(keep, send):
        received = lax.ppermute(send, "section", [(0, 1), (1, 0)])
        return jnp.where(first, keep, received), jnp.where(first, received, keep)

    def choose(pair):
        return jnp.where(first, pair[0], pair[1]), jnp.where(first, pair[1], pair[0])

    cfg = (heads, channels)
    section = s.astype(jnp.int32).reshape(1)
    shape_a, shape_b = (slab, 6 * LANES), (slab, 2 * main + LANES)
    kept_a, sent_a = call(
        functools.partial(pack_attn_kernel, cfg),
        (out(shape_a, BF16),) * 2,
        section,
        in_weight[0],
        jnp.pad(gate_weight[0].astype(F32), ((0, 0), (0, LANES - gate_weight.shape[2]))),
        out_weight[0].T,
        scalars=1,
        streamed=(1,),
    )
    sent_a, condition, down_in = lax.optimization_barrier((sent_a, condition, down_weight[0]))
    received_a = lax.ppermute(sent_a, "section", [(0, 1), (1, 0)])
    kept_b, sent_b = call(
        functools.partial(pack_mlp_kernel, left),
        (out(shape_b, BF16),) * 2,
        section,
        up_weight[0],
        down_in.T,
        scalars=1,
        streamed=(1,),
    )
    received_b = lax.ppermute(sent_b, "section", [(0, 1), (1, 0)])

    def unit_halves(value):
        rest = sections * main
        return tuple(
            (value[:, h * main : (h + 1) * main], value[:, rest + h * left : rest + (h + 1) * left])
            for h in (0, 1)
        )

    def pack_small(gate_half, taps_half, up_half):
        return jnp.concatenate([gate_half.reshape(-1), taps_half.reshape(-1), up_half.reshape(-1)])

    def pack_halves(pack, *pairs):
        return tuple(pack(*(pair[i] for pair in pairs)) for i in (0, 1))

    x_pair = cut(section_inputs[0], 1)
    x_received = lax.ppermute(
        jnp.where(first, x_pair[1], x_pair[0]), "section", [(0, 1), (1, 0)]
    )
    x0 = jnp.where(first, x_pair[0], x_received)
    g1 = jnp.where(first, x_received, x_pair[1])
    taps_count = conv_taps.shape[1]
    up_row = up_bias[0].astype(F32)[None]
    small = swap_halves(
        *choose(
            pack_halves(
                pack_small,
                cut(gate_bias[0].astype(F32), 0),
                cut(conv_taps[0].astype(F32), 1),
                tuple(jnp.concatenate(v, axis=1) for v in unit_halves(up_row)),
            )
        )
    )

    def unpack_small(packed):
        gate_row = jnp.pad(packed[:heads][None], ((0, 0), (tail, LANES - heads - tail)))
        taps = packed[heads : heads + taps_count * channels].reshape(taps_count, channels)
        taps = jnp.pad(taps, ((0, 16 - taps_count), (0, wide - channels)))
        up_row = packed[heads + taps_count * channels :][None]
        return gate_row, taps, jnp.pad(up_row, ((0, 0), (0, main + LANES - units)))

    cond_vec = condition + sinusoid(timesteps, width)
    activated = jax.nn.silu(cond_vec).astype(BF16)
    slab_active = activated.reshape(images, dps, slab).transpose(1, 0, 2)
    slab_active = lax.all_to_all(slab_active, "dp", split_axis=0, concat_axis=0, tiled=True)
    slab_active = slab_active.reshape(dps * images, slab)
    slab_active, received_a = lax.optimization_barrier((slab_active, received_a))
    mod_part = jnp.dot(slab_active, ada_weight[0], preferred_element_type=F32)
    mod_parts = lax.all_to_all(
        mod_part.reshape(dps, images, -1), "dp", split_axis=0, concat_axis=0, tiled=True
    )
    mod_share = jnp.sum(mod_parts, axis=0) + ada_bias[0].astype(F32)
    mod_all = spread_over(mod_share, ("section", "tensor"))
    received_b, mod_all = lax.optimization_barrier((received_b, mod_all))
    mod_all = mod_all.reshape(sections, tensors, images, -1).transpose(0, 2, 1, 3)
    mod_all = mod_all.reshape(sections, images, 6, width)
    mods = (mod_all[0], mod_all[1])

    shard = out((images, rows, width), BF16)
    shard_wide = out((images, rows, width), F32)
    vector = out((images, 1, width), F32)
    pieces_out = (out((4, images, rows, width), BF16),) + (shard,) * 4
    full = out((images, PATCHES, width), BF16)
    flat = out((images * PATCHES, width), BF16)
    total_rows = images * PATCHES
    kept = pltpu.VMEM((images, PATCHES, width), BF16)
    middle_flops = 2 * total_rows * PATCHES * wide * heads * 6
    attn_flops = 2 * total_rows * width * wide * 5 + middle_flops
    mlp_flops = 4 * total_rows * width * units

    def attn_forward(b, shards):
        w, _, gate_row, taps, _ = weights[b]
        body = functools.partial(attn_forward_kernel, (b == 1, heads, head_width))
        found = call(
            body,
            (
                full,
                out((images, PATCHES, 4 * wide), BF16),
                out((images, PATCHES, LANES), F32),
                out((images, PATCHES, wide), F32),
                out((images, PATCHES, wide), BF16),
                *pieces_out,
            ),
            me,
            *shards,
            w,
            gate_row,
            taps,
            scalars=1,
            flops=attn_flops,
            scratch=[kept],
            streamed=(9,),
            saved=(0, 1, 2, 3, 4),
        )
        return found[:5], scatter_plane(found[5], found[6:])

    def attn_backward(b, shards, saved, after=()):
        w, _, _, taps, _ = weights[b]
        body = functools.partial(attn_backward_kernel, (b == 1, heads, head_width))
        found = call(
            body,
            (
                full,
                out((images, PATCHES, 5 * LANES), BF16),
                out((16, wide), F32),
                *pieces_out,
            ),
            me,
            *shards,
            saved[1],
            saved[2],
            saved[3],
            w,
            taps,
            scalars=1,
            flops=2 * attn_flops,
            scratch=[kept],
            streamed=(9, 10, 11, 12),
            after=after,
        )
        terms = scatter_plane(found[3], found[4:])
        (grads,) = call(
            attn_weights_kernel,
            (out((width, 6 * LANES), BF16),),
            saved[0],
            found[1],
            found[0],
            saved[4],
            flops=2 * total_rows * width * wide * 5,
            after=terms if b else (),
            streamed=(0, 3),
            saved=(0,),
        )
        return terms, grads, found[2]

    def mlp_forward(b, normed):
        _, w, _, _, up_row = weights[b]
        found = call(
            functools.partial(mlp_forward_kernel, left),
            (
                flat,
                out((total_rows, main + LANES), F32),
                out((total_rows, main + LANES), BF16),
                *pieces_out,
            ),
            *gather_plane(normed),
            w,
            up_row,
            flops=mlp_flops,
            streamed=(8,),
            saved=(0, 1, 2),
        )
        return found[:3], scatter_plane(found[3], found[4:])

    shape_gw = out((width, 2 * main + LANES), BF16)
    shape_gub = out((1, main + LANES), F32)

    def mlp_both(b, gathered, gradient):
        _, w, _, _, up_row = weights[b]
        found = call(
            functools.partial(mlp_both_kernel, left),
            (shape_gw, shape_gub, vector, *pieces_out, *pieces_out),
            gathered,
            gradient,
            w,
            up_row,
            mods[b],
            flops=3 * mlp_flops,
            scratch=[pltpu.VMEM(flat.shape, flat.dtype)],
            streamed=(0, 1, 2),
            saved=(0, 8, 9, 10, 11, 12),
        )
        return scatter_plane(found[3], found[4:8]), found[0], found[1], found[2], found[8:]

    def mlp_backward(b, given, saved, after=()):
        _, w, _, _, _ = weights[b]
        found = call(
            functools.partial(mlp_backward_kernel, left),
            (flat, out((total_rows, main + LANES), BF16), shape_gub, *pieces_out),
            *given,
            saved[1],
            w,
            flops=mlp_flops,
            streamed=(8, 9),
            after=after,
        )
        terms = scatter_plane(found[3], found[4:])
        (grads,) = call(
            mlp_weights_kernel,
            (shape_gw,),
            saved[0],
            found[1],
            found[0],
            saved[2],
            flops=mlp_flops,
            after=terms,
            streamed=(0, 3),
            saved=(0,),
        )
        return terms, grads, found[2]

    def of_block(b, kept, received):
        return jnp.where(first == (b == 0), kept, received)

    full_a0 = gather_all(of_block(0, kept_a, received_a))
    middle = [of_block(0, kept_b, received_b), of_block(1, kept_a, received_a)]
    full_middle = gather_all(jnp.concatenate(middle, axis=1))
    full_b0 = Columns(full_middle, 0, middle[0].shape[1])
    full_a1 = Columns(full_middle, middle[0].shape[1], middle[1].shape[1])
    (g1_all,) = call(stack_kernel, (flat,), *gather_plane(g1), saved=(0,))
    (normed,) = call(start_kernel, (shard,), x0, mods[0])
    shards, g1_all, next_b = lax.optimization_barrier(
        (
            gather_plane(normed),
            g1_all,
            of_block(1, kept_b, received_b),
        )
    )
    weights = [
        (full_a0, full_b0, *unpack_small(small[0])),
        (full_a1, gather_all(next_b), *unpack_small(small[1])),
    ]

    def to_second(value):
        return lax.ppermute(value, "section", [(0, 1)])

    def to_first(value):
        return lax.ppermute(value, "section", [(1, 0)])

    attn0, terms = attn_forward(0, shards)
    att0, aft0, normed = call(
        after_attn_kernel, (shard_wide, shard_wide, shard), *terms, x0, mods[0], saved=(0, 1)
    )
    mlp0, terms = mlp_forward(0, normed)
    mlp_out0, x1, normed = call(
        between_kernel,
        (shard_wide, shard, shard),
        *terms,
        aft0,
        mods[0],
        mods[1],
        saved=(0, 1),
    )
    attn1, terms = attn_forward(1, gather_plane(normed))
    att1, aft1, normed = call(
        after_attn_kernel, (shard_wide, shard_wide, shard), *terms, x1, mods[1], saved=(0, 1)
    )

    three, six = (out((images, n, width), F32) for n in (3, 6))
    (n_all,) = call(stack_kernel, (flat,), *gather_plane(normed), saved=(0,))
    terms, mlp_grads1, g_up_bias1, g_gate_two1, end_pieces = mlp_both(1, n_all, g1_all)
    g_after, g_attn, g_some = call(
        back_mlp_rows_kernel,
        (shard_wide, shard, three),
        *terms,
        g1,
        aft1,
        att1,
        mods[1],
        saved=(0,),
    )
    sum_b1 = scatter_rows(mlp_grads1)
    terms, attn_grads1, g_taps1 = attn_backward(1, gather_plane(g_attn), attn1)
    g0, g_mlp, g_mods1, g_gate_two0 = call(
        back_between_kernel,
        (shard, shard, six, vector),
        *terms,
        g_after,
        x1,
        mods[1],
        g_some,
        g_gate_two1,
        mods[0],
        mlp_out0,
    )
    sum_a1 = scatter_rows(attn_grads1)
    terms, mlp_grads0, g_up_bias0 = mlp_backward(0, gather_plane(g_mlp), mlp0, (attn_grads1,))
    g_after, g_attn, g_some = call(
        back_mlp_rows_kernel,
        (shard_wide, shard, three),
        *terms,
        g0,
        aft0,
        att0,
        mods[0],
        after=(sum_b1,),
        saved=(0,),
    )
    terms, attn_grads0, g_taps0 = attn_backward(0, gather_plane(g_attn), attn0, (mlp_grads0,))
    g_in, g_mods0 = call(
        back_end_kernel,
        (shard, six),
        *terms,
        g_after,
        x0,
        mods[0],
        g_some,
        g_gate_two0,
        after=(attn_grads0,),
    )

    sum_b0, sum_a0 = scatter_rows(mlp_grads0), scatter_rows(attn_grads0)

    g_mod = jnp.stack([g_mods0.reshape(images, -1), g_mods1.reshape(images, -1)])
    g_mod = g_mod.reshape(sections, images, tensors, -1).transpose(0, 2, 1, 3)
    columns = g_mod.shape[3]
    g_mod = g_mod.reshape(sections, tensors, images * columns)
    taps_rows = taps_count + 1

    def small_grads(g_taps, g_up_bias):
        return jnp.concatenate([g_taps[:taps_rows].reshape(-1), g_up_bias.reshape(-1)])

    g_small = jnp.stack([small_grads(g_taps0, g_up_bias0), small_grads(g_taps1, g_up_bias1)])
    to_tensor = (jnp.arange(tensors) == t)[None, :, None]
    g_small = jnp.where(to_tensor, g_small[:, None], 0.0)
    g_sent = jnp.concatenate([g_mod, g_small], axis=2).reshape(sections * tensors, -1)
    g_parts = lax.all_to_all(
        g_sent, ("section", "tensor"), split_axis=0, concat_axis=0, tiled=True
    )
    g_parts, sum_b1, sum_a1 = lax.optimization_barrier((g_parts, sum_b1, sum_a1))
    other_b1, other_a1 = to_second(sum_b1), to_second(sum_a1)
    g_share = jnp.sum(g_parts[:, : images * columns], axis=0)
    small_parts = g_parts[:, images * columns :].reshape(sections, tensors, -1).sum(1)
    g_all = spread_over(jnp.concatenate([g_share, small_parts.reshape(-1)]), ("dp",))
    g_all, end_pieces, sum_b0 = lax.optimization_barrier((g_all, end_pieces, sum_b0))
    others = other_b1, other_a1, to_first(sum_b0)
    (block_out,) = call(
        end_kernel, (shard,), *scatter_plane(end_pieces[0], end_pieces[1:], True), aft1, mods[1]
    )
    small_own = jnp.sum(g_all[:, images * columns :], axis=0).reshape(sections, -1)
    g_all = g_all[:, : images * columns].reshape(dps * images, columns).astype(BF16)
    grad_ada_bias = jnp.sum(g_all.astype(F32), axis=0)
    act_part = jnp.einsum("me,de->md", g_all, ada_weight[0], preferred_element_type=F32)
    act_part, other_b1 = lax.optimization_barrier((act_part, others[0]))
    others = other_b1, *others[1:]
    plane = sections * tensors
    act_sent = jnp.broadcast_to(
        act_part.reshape(dps, 1, images, slab), (dps, plane, images, slab)
    )
    act_all = lax.all_to_all(
        act_sent.reshape(-1, images, slab),
        ("dp", "section", "tensor"),
        split_axis=0,
        concat_axis=0,
        tiled=True,
    )
    act_all, other_b0 = lax.optimization_barrier((act_all, others[2]))
    others = *others[:2], other_b0
    act_all = jnp.sum(act_all.reshape(dps, plane, images, slab), axis=1)
    act_grad = act_all.reshape(dps, images, slab).transpose(1, 0, 2).reshape(images, width)
    cond_grad = jax.vjp(jax.nn.silu, cond_vec)[1](act_grad)[0]

    ends_from_first = lax.ppermute(block_out, "section", [(0, 1)])
    ends_from_second = lax.ppermute(g_in, "section", [(1, 0)])
    mine = jnp.where(first, g_in, block_out)
    received = jnp.where(first, ends_from_second, ends_from_first)
    section_ends = jnp.concatenate(
        [jnp.where(first, mine, received), jnp.where(first, received, mine)], axis=1
    )
    cond_grad, section_ends, sum_a0, g_all, others = lax.optimization_barrier(
        (cond_grad, section_ends, sum_a0, g_all, others)
    )
    other_b1, other_a1, other_b0 = others
    other_a0 = to_first(sum_a0)
    grad_ada = jnp.einsum("md,me->de", slab_active, g_all, preferred_element_type=F32)

    small_taps = small_own[:, : taps_rows * wide].reshape(sections, taps_rows, wide)
    grad_gateb = small_taps[:, taps_count, tail : tail + heads].reshape(-1)
    grad_taps = small_taps[:, :taps_count, :channels].transpose(1, 0, 2)
    grad_taps = grad_taps.reshape(taps_count, sections * channels)
    up_halves = small_own[:, taps_rows * wide :]
    grad_up_bias = jnp.concatenate(
        [up_halves[:, :main].reshape(-1), up_halves[:, main : main + left].reshape(-1)]
    )

    grad_up, grad_down = call(
        functools.partial(unpack_mlp_kernel, left),
        (out(up_weight.shape[1:], F32),) * 2,
        section,
        sum_b0,
        other_b0,
        sum_b1,
        other_b1,
        scalars=1,
    )
    grad_down = grad_down.T
    grad_in, grad_gate, grad_out = call(
        functools.partial(unpack_attn_kernel, cfg),
        (
            out(in_weight.shape[1:], F32),
            out(gate_weight.shape[1:], F32),
            out((slab, out_weight.shape[1]), F32),
        ),
        section,
        sum_a0,
        other_a0,
        sum_a1,
        other_a1,
        scalars=1,
    )
    grad_out = grad_out.T

    return (
        section_ends[None],
        cond_grad,
        grad_ada[None],
        grad_ada_bias[None],
        grad_in[None],
        grad_gate[None],
        grad_gateb[None],
        grad_taps[None],
        grad_out[None],
        grad_up[None],
        grad_up_bias[None],
        grad_down[None],
    )


def solution(mesh):
    in_specs = (
        P("section", "dp", "tensor", None),
        P("dp", None),
        P("dp"),
        P("section", "dp", "tensor"),
        P("section", "tensor"),
        P("section", None, "dp", "tensor"),
        P("section", "dp", "tensor"),
        P("section", "tensor"),
        P("section", None, "tensor"),
        P("section", "tensor", "dp"),
        P("section", "dp", "tensor"),
        P("section", "tensor"),
        P("section", "tensor", "dp"),
    )
    out_specs = (
        P("section", "dp", "tensor", None),
        P("dp", None),
        P("section", "dp", "tensor"),
        P("section", "tensor"),
        P("section", None, "dp", "tensor"),
        P("section", "dp", "tensor"),
        P("section", "tensor"),
        P("section", None, "tensor"),
        P("section", "tensor", "dp"),
        P("section", "dp", "tensor"),
        P("section", "tensor"),
        P("section", "tensor", "dp"),
    )
    return jax.shard_map(
        per_device, mesh=mesh, in_specs=in_specs, out_specs=out_specs, check_vma=False
    )
```

```python
import functools
import math

import jax
import jax.numpy as jnp
from jax import lax
from jax.experimental import pallas as pl
from jax.experimental.pallas import tpu as pltpu
from jax.sharding import PartitionSpec as P

SIDE = 16
PATCHES = SIDE * SIDE
LANES = 128
F32 = jnp.float32
BF16 = jnp.bfloat16
PLANE = ("tensor", "section")


class Traffic:
    def __init__(self, arriving, leaving):
        self.arriving, self.leaving, self.left = arriving, leaving, set()

    def wait(self, *places):
        for at in places:
            self.arriving[at].wait()

    def flush(self, *places):
        for at in places:
            self.leaving[at].start()
            self.left.add(at)


class Columns:
    def __init__(self, array, start, width):
        self.array, self.start = array, start
        self.shape, self.dtype = (array.shape[0], width), array.dtype
        self.size = array.shape[0] * width

    def source(self, ref):
        return ref.at[:, self.start : self.start + self.shape[1]]


def call(body, outs, *args, scalars=0, flops=0, scratch=(), after=(), streamed=(), saved=()):
    count, waits, many = len(args), len(after), len(outs)
    given = args
    moving = bool(streamed or saved)

    def kernel(*refs):
        ins, out_refs = list(refs[:count]), list(refs[count + waits : count + waits + many])
        rest = refs[count + waits + many :]
        own, held = rest[: len(scratch)], rest[len(scratch) :]
        arriving, leaving = {}, {}
        for i, at in enumerate(streamed):
            source = given[at].source(ins[at]) if isinstance(given[at], Columns) else ins[at]
            arriving[at] = pltpu.make_async_copy(source, held[i], held[-1].at[i])
            ins[at] = held[i]
        for i, at in enumerate(saved, len(streamed)):
            leaving[at] = pltpu.make_async_copy(held[i], out_refs[at], held[-1].at[i])
            out_refs[at] = held[i]
        traffic = Traffic(arriving, leaving)
        for copy in arriving.values():
            copy.start()
        if moving:
            body(traffic, *ins, *out_refs, *own)
        else:
            body(*ins, *out_refs, *own)
        traffic.flush(*[at for at in saved if at not in traffic.left])
        for copy in leaving.values():
            copy.wait()

    moved = sum(a.size * a.dtype.itemsize for a in args)
    moved += sum(math.prod(o.shape) * o.dtype.itemsize for o in outs)
    specs = [pl.BlockSpec(memory_space=pltpu.SMEM)] * scalars
    specs += [
        pl.BlockSpec(memory_space=pltpu.HBM if i in streamed else pltpu.VMEM)
        for i in range(scalars, count)
    ]
    large = [a.size > 2**17 for a in after]
    specs += [pl.BlockSpec(memory_space=pltpu.HBM if v else pl.ANY) for v in large]
    after = [
        pltpu.with_memory_space_constraint(a, pltpu.HBM) if v else a for a, v in zip(after, large)
    ]
    spaces = [pltpu.HBM if i in saved else pltpu.VMEM for i in range(many)]
    shapes = [
        pltpu.HBM(o.shape, o.dtype) if i in saved else o for i, o in enumerate(outs)
    ]
    args = [a.array if isinstance(a, Columns) else a for a in args]
    args = [
        pltpu.with_memory_space_constraint(a, pltpu.HBM) if i in streamed else a
        for i, a in enumerate(args)
    ]
    hold = [pltpu.VMEM(given[i].shape, given[i].dtype) for i in streamed]
    hold += [pltpu.VMEM(outs[i].shape, outs[i].dtype) for i in saved]
    if moving:
        hold.append(pltpu.SemaphoreType.DMA((len(hold),)))
    return pl.pallas_call(
        kernel,
        out_shape=tuple(shapes),
        in_specs=specs,
        out_specs=tuple(pl.BlockSpec(memory_space=space) for space in spaces),
        scratch_shapes=[*scratch, *hold],
        compiler_params=pltpu.CompilerParams(vmem_limit_bytes=6 * 2**20 + moved * 3 // 2),
        cost_estimate=pl.CostEstimate(flops=flops, bytes_accessed=moved, transcendentals=0),
    )(*args, *after)


def out(shape, dtype):
    return jax.ShapeDtypeStruct(shape, dtype)


def mm(a, b):
    return lax.dot_general(a, b, (((1,), (0,)), ((), ())), preferred_element_type=F32)


def mm_nt(a, b):
    return lax.dot_general(a, b, (((1,), (1,)), ((), ())), preferred_element_type=F32)


def mm_tn(a, b):
    return lax.dot_general(a, b, (((0,), (0,)), ((), ())), preferred_element_type=F32)


def normalize(v):
    centered = v - jnp.mean(v, axis=-1, keepdims=True)
    scale = lax.rsqrt(jnp.mean(centered * centered, axis=-1, keepdims=True) + 1e-06)
    return centered * scale, scale


def norm_grad(hat, rstd, grad):
    inner = jnp.mean(grad * hat, axis=-1, keepdims=True)
    return rstd * (grad - jnp.mean(grad, axis=-1, keepdims=True) - hat * inner)


def gather_total(pieces):
    total = pieces[0][...].astype(F32)
    for piece in pieces[1:]:
        total = total + piece[...].astype(F32)
    return total


def rows_sum(v):
    return jnp.sum(v, axis=0, keepdims=True)


def gelu_terms(x):
    k = math.sqrt(2.0 / math.pi)
    th = jnp.tanh(k * (x + 0.044715 * x * x * x))
    value = 0.5 * x * (1.0 + th)
    slope = 0.5 * (1.0 + th) + 0.5 * x * (1.0 - th * th) * k * (1.0 + 3 * 0.044715 * x * x)
    return value, slope


def start_kernel(x_ref, mod_ref, n_ref):
    for m in range(x_ref.shape[0]):
        hat, _ = normalize(x_ref[m].astype(F32))
        n_ref[m] = (hat * (1.0 + mod_ref[m, 1:2]) + mod_ref[m, 0:1]).astype(BF16)


def add_kernel(a, b, c, d, recv, *outs):
    for j, own in enumerate((a, b, c, d)):
        outs[j][...] = (own[...].astype(F32) + recv[j].astype(F32)).astype(BF16)


def add_late_kernel(traffic, a, b, c, d, recv, *outs):
    traffic.wait(0, 1, 2, 3)
    add_kernel(a, b, c, d, recv, *outs)


def after_attn_kernel(traffic, p0, p1, p2, p3, x_ref, mod_ref, att_ref, aft_ref, n_ref):
    for m in range(x_ref.shape[0]):
        att = gather_total([p.at[m] for p in (p0, p1, p2, p3)])
        aft = x_ref[m].astype(F32) + mod_ref[m, 2:3] * att
        hat, _ = normalize(aft)
        att_ref[m] = att
        aft_ref[m] = aft
        n_ref[m] = (hat * (1.0 + mod_ref[m, 4:5]) + mod_ref[m, 3:4]).astype(BF16)


def between_kernel(traffic, p0, p1, p2, p3, aft_ref, mod_ref, next_ref, mlp_ref, x_ref, n_ref):
    for m in range(aft_ref.shape[0]):
        mlp = gather_total([p.at[m] for p in (p0, p1, p2, p3)])
        x = (aft_ref[m] + mod_ref[m, 5:6] * mlp).astype(BF16)
        hat, _ = normalize(x.astype(F32))
        mlp_ref[m] = mlp
        x_ref[m] = x
        n_ref[m] = (hat * (1.0 + next_ref[m, 1:2]) + next_ref[m, 0:1]).astype(BF16)


def end_kernel(p0, p1, p2, p3, aft_ref, mod_ref, x_ref):
    for m in range(aft_ref.shape[0]):
        mlp = gather_total([p.at[m] for p in (p0, p1, p2, p3)])
        x_ref[m] = (aft_ref[m] + mod_ref[m, 5:6] * mlp).astype(BF16)


def back_mlp_rows_kernel(traffic, p0, p1, p2, p3, g_ref, aft_ref, att_ref, mod_ref, ga_ref, gt_ref, gm_ref):
    for m in range(aft_ref.shape[0]):
        gn = gather_total([p.at[m] for p in (p0, p1, p2, p3)])
        hat, rstd = normalize(aft_ref[m])
        grad = g_ref[m].astype(F32) + norm_grad(hat, rstd, gn * (1.0 + mod_ref[m, 4:5]))
        ga_ref[m] = grad
        gt_ref[m] = (mod_ref[m, 2:3] * grad).astype(BF16)
        gm_ref[m, 0:1] = rows_sum(grad * att_ref[m])
        gm_ref[m, 1:2] = rows_sum(gn)
        gm_ref[m, 2:3] = rows_sum(gn * hat)


def back_attn_rows(pieces, ga_ref, x_ref, mod_ref, some_ref, gate_ref, gm_ref, m):
    gn = gather_total([p.at[m] for p in pieces])
    hat, rstd = normalize(x_ref[m].astype(F32))
    grad = ga_ref[m] + norm_grad(hat, rstd, gn * (1.0 + mod_ref[m, 1:2]))
    gm_ref[m, 0:1] = rows_sum(gn)
    gm_ref[m, 1:2] = rows_sum(gn * hat)
    gm_ref[m, 2:5] = some_ref[m]
    gm_ref[m, 5:6] = gate_ref[m]
    return grad.astype(BF16)


def back_between_kernel(p0, p1, p2, p3, ga_ref, x_ref, mod_ref, some_ref, gate_ref, prev_ref, mlp_ref, *outs):
    g_ref, gmlp_ref, gm_ref, next_ref = outs
    for m in range(x_ref.shape[0]):
        grad = back_attn_rows((p0, p1, p2, p3), ga_ref, x_ref, mod_ref, some_ref, gate_ref, gm_ref, m)
        g_ref[m] = grad
        wide = grad.astype(F32)
        gmlp_ref[m] = (prev_ref[m, 5:6] * wide).astype(BF16)
        next_ref[m] = rows_sum(wide * mlp_ref[m])


def back_end_kernel(p0, p1, p2, p3, ga_ref, x_ref, mod_ref, some_ref, gate_ref, g_ref, gm_ref):
    for m in range(x_ref.shape[0]):
        g_ref[m] = back_attn_rows((p0, p1, p2, p3), ga_ref, x_ref, mod_ref, some_ref, gate_ref, gm_ref, m)


def scan_mask(columns_first):
    def place(number):
        if columns_first:
            return (number % SIDE) * SIDE + number // SIDE
        return number

    shape = (PATCHES, PATCHES)
    later = place(lax.broadcasted_iota(jnp.int32, shape, 0))
    return later >= place(lax.broadcasted_iota(jnp.int32, shape, 1))


def grid_column():
    return lax.broadcasted_iota(jnp.int32, (PATCHES, 1), 0) % SIDE


def side_shifts(a, column):
    left = jnp.where(column == 0, 0.0, pltpu.roll(a, 1, 0))
    right = jnp.where(column == SIDE - 1, 0.0, pltpu.roll(a, PATCHES - 1, 0))
    return left, a, right


def convolve(shifted, tap):
    sums = []
    for row in range(3):
        terms = [shifted[col] * tap(3 * row + col) for col in range(3)]
        sums.append(terms[0] + terms[1] + terms[2])
    zeros = jnp.zeros((SIDE, sums[0].shape[1]), F32)
    above = jnp.concatenate([zeros, sums[0][:-SIDE]], axis=0)
    below = jnp.concatenate([sums[2][SIDE:], zeros], axis=0)
    return shifted[1] + sums[1] + above + below


def tap_grads(shifted, grad):
    found = []
    for row in range(3):
        for col in range(3):
            if row == 0:
                product = shifted[col][:-SIDE] * grad[SIDE:]
            elif row == 1:
                product = shifted[col] * grad
            else:
                product = shifted[col][SIDE:] * grad[:-SIDE]
            found.append(rows_sum(product))
    return found


def lane_sets(width, first, head_width, heads):
    lane = lax.broadcasted_iota(jnp.int32, (1, width), 1)
    return [
        (lane >= first + h * head_width) & (lane < first + (h + 1) * head_width)
        for h in range(heads)
    ]


def three_parts(v):
    parts = []
    for _ in range(3):
        parts.append(v.astype(BF16))
        v = v - parts[-1].astype(F32)
    return jnp.concatenate(parts, axis=1)


def add_parts(v):
    return v[:, :LANES] + v[:, LANES : 2 * LANES] + v[:, 2 * LANES :]


def decay_parts(logits, mask, gate_lane, heads):
    rates = -(jnp.maximum(logits, 0.0) + jnp.log1p(jnp.exp(-jnp.abs(logits))))
    ones = jnp.where(mask, 1.0, 0.0).astype(BF16)
    totals = add_parts(mm(ones, three_parts(rates)))
    turned = totals.T
    decays = []
    for h in range(heads):
        at = gate_lane + h
        spans = jnp.where(mask, totals[:, at : at + 1] - turned[at : at + 1, :], -1e30)
        w = jnp.exp(spans)
        decays.append((w, jnp.sum(w, axis=1, keepdims=True)))
    return decays, ones


def send_order(k):
    return (0, 1, None, None, 2, 3, None, None)[k], (None, None, 0, 1, None, None, 2, 3)[k]


def write_pieces(me, total_ref, other_ref, own_refs):
    rows = total_ref.shape[1] // 8
    for k in range(8):
        spot = pl.ds(pl.multiple_of(jnp.bitwise_xor(me, k) * rows, rows), rows)
        own, other = send_order(k)
        if own is None:
            other_ref[other] = total_ref[:, spot, :]
        else:
            own_refs[own][...] = total_ref[:, spot, :]


def each_shard(refs):
    own, x, y, xy, core, core_x, core_y, core_xy = refs
    return own, x, core, core_x, y, xy, core_y, core_xy


def gather_pieces(me, shard_refs, full_ref):
    rows = full_ref.shape[1] // 8
    for k, shard in enumerate(each_shard(shard_refs)):
        spot = pl.ds(pl.multiple_of(jnp.bitwise_xor(me, k) * rows, rows), rows)
        full_ref[:, spot, :] = shard[...]


def tail_spots(heads):
    return (0, 32, 48, 64, 80)


def join_tail(packed, piece, tails, lane):
    tile = packed[:, piece * LANES : (piece + 1) * LANES]
    return jnp.concatenate([tile, pltpu.roll(tails, (LANES - lane) % LANES, 1)], axis=1)


def lanes():
    return lax.broadcasted_iota(jnp.int32, (1, LANES), 1)


def half_tiles(tiles, at):
    if at == 0:
        return tiles[0], tiles[1]
    shift = 2 * LANES - at
    first = jnp.where(lanes() < shift, pltpu.roll(tiles[1], shift, 1), pltpu.roll(tiles[2], shift, 1))
    return first, pltpu.roll(tiles[2], shift, 1)


def pack_attn_kernel(cfg, traffic, sec_ref, in_ref, gate_ref, out_ref, keep_ref, send_ref):
    heads, channels = cfg
    traffic.wait(1)
    spots = tail_spots(heads)
    tail = channels - LANES
    rows = in_ref.shape[1]
    short = jnp.zeros((rows, 3 * LANES - 2 * channels), F32)
    keep_first = sec_ref[0] == 0
    lane = lanes()
    tails = [gate_ref[...], pltpu.roll(gate_ref[...], LANES - heads, 1)]
    tails = [
        jnp.where((lane >= tail) & (lane < tail + heads), pltpu.roll(v, tail, 1), 0.0) for v in tails
    ]
    for j in range(5):
        ref = out_ref if j == 4 else in_ref.at[j]
        tiles = [ref[:, :LANES].astype(F32), ref[:, LANES : 2 * LANES].astype(F32)]
        tiles.append(jnp.concatenate([ref[:, 2 * LANES :].astype(F32), short], axis=1))
        whole = []
        for h in range(2):
            tile, rest = half_tiles(tiles, h * channels)
            whole.append(tile)
            tails[h] = tails[h] + pltpu.roll(jnp.where(lane < tail, rest, 0.0), spots[j], 1)
        cols = slice(j * LANES, (j + 1) * LANES)
        keep_ref[:, cols] = jnp.where(keep_first, whole[0], whole[1]).astype(BF16)
        send_ref[:, cols] = jnp.where(keep_first, whole[1], whole[0]).astype(BF16)
    cols = slice(5 * LANES, 6 * LANES)
    keep_ref[:, cols] = jnp.where(keep_first, tails[0], tails[1]).astype(BF16)
    send_ref[:, cols] = jnp.where(keep_first, tails[1], tails[0]).astype(BF16)


def pack_mlp_kernel(left, traffic, sec_ref, up_ref, down_ref, keep_b_ref, send_b_ref):
    keep_first = sec_ref[0] == 0
    lane = lanes()
    main = (keep_b_ref.shape[1] - LANES) // 2
    traffic.wait(1)
    at = 0
    for ref in (up_ref, down_ref):
        low, high = ref[:, :main], ref[:, main : 2 * main]
        keep_b_ref[:, at : at + main] = jnp.where(keep_first, low, high)
        send_b_ref[:, at : at + main] = jnp.where(keep_first, high, low)
        at += main
    up, down = (ref[:, 2 * main :].astype(F32) for ref in (up_ref, down_ref))
    low = jnp.where(lane < left, up, pltpu.roll(down, left, 1)).astype(BF16)
    high = jnp.where(lane < left, pltpu.roll(up, left, 1), down).astype(BF16)
    keep_b_ref[:, at:] = jnp.where(keep_first, low, high)
    send_b_ref[:, at:] = jnp.where(keep_first, high, low)


def unpack_mlp_kernel(left, sec_ref, sum0_ref, other0_ref, sum1_ref, other1_ref, up_ref, down_ref):
    in_first = sec_ref[0] == 0
    main = (sum0_ref.shape[1] - LANES) // 2
    lane = lanes()

    def both(cols):
        low = jnp.where(in_first, sum0_ref[:, cols], other1_ref[:, cols])
        return low.astype(F32), jnp.where(in_first, other0_ref[:, cols], sum1_ref[:, cols]).astype(F32)

    up_ref[:, :main], up_ref[:, main : 2 * main] = both(slice(0, main))
    down_ref[:, :main], down_ref[:, main : 2 * main] = both(slice(main, 2 * main))
    low, high = both(slice(2 * main, 2 * main + LANES))
    up_ref[:, 2 * main :] = jnp.where(lane < left, low, pltpu.roll(high, left, 1))
    down_ref[:, 2 * main :] = jnp.where(lane < left, pltpu.roll(low, LANES - left, 1), high)


def unpack_attn_kernel(
    cfg, sec_ref, sum0_ref, other0_ref, sum1_ref, other1_ref, in_ref, gate_ref, out_ref
):
    heads, channels = cfg
    spots = tail_spots(heads)
    tail = channels - LANES
    in_first = sec_ref[0] == 0
    lane = lanes()
    shift = channels - LANES

    def both(cols):
        low = jnp.where(in_first, sum0_ref[:, cols], other1_ref[:, cols])
        return low.astype(F32), jnp.where(in_first, other0_ref[:, cols], sum1_ref[:, cols]).astype(F32)

    low_tails, high_tails = both(slice(5 * LANES, 6 * LANES))
    for j in range(5):
        ref = out_ref if j == 4 else in_ref.at[j]
        low, high = both(slice(j * LANES, (j + 1) * LANES))
        ref[:, :LANES] = low
        high = pltpu.roll(high, shift, 1)
        low_tail = pltpu.roll(low_tails, (LANES - spots[j]) % LANES, 1)
        high_tail = pltpu.roll(high_tails, (LANES - spots[j] + shift) % LANES, 1)
        ref[:, LANES : 2 * LANES] = jnp.where(lane < tail, low_tail, high)
        last = jnp.where(lane < shift, high, high_tail)
        ref[:, 2 * LANES :] = last[:, : 2 * channels - 2 * LANES]
    low_gate = pltpu.roll(low_tails, LANES - tail, 1)
    high_gate = pltpu.roll(high_tails, LANES - tail + heads, 1)
    gate_ref[...] = jnp.where(lane < heads, low_gate, high_gate)[:, : 2 * heads]


def attn_forward_kernel(cfg, traffic, me_ref, *refs):
    columns_first, heads, head_width = cfg
    shards, (w_ref, gb_ref, tap_ref) = refs[:8], refs[8:11]
    n_ref, proj_ref, log_ref, attn_ref, mix_ref, other_ref = refs[11:17]
    own_refs, total_ref = refs[17:21], refs[21]
    me = me_ref[0]
    wide = 2 * LANES
    gate_lane = heads * head_width - LANES
    spots = tail_spots(heads)
    mask = scan_mask(columns_first)
    column = grid_column()
    sets = lane_sets(wide, 0, head_width, heads)
    gather_pieces(me, shards, n_ref)
    traffic.flush(0)
    traffic.wait(9)
    for m in range(n_ref.shape[0]):
        projected = mm(n_ref[m], w_ref[:, : 4 * LANES])
        tails = mm(n_ref[m], w_ref[:, 5 * LANES :])
        logits = tails + gb_ref[...]
        log_ref[m] = logits
        decays, _ = decay_parts(logits, mask, gate_lane, heads)
        query, key, value, gate = (join_tail(projected, j, tails, spots[j]) for j in range(4))
        in_head = sets[0]
        for own in sets[1:]:
            in_head = in_head | own
        query, key, value = (jnp.where(in_head, v, 0.0).astype(BF16) for v in (query, key, value))
        gate = gate.astype(BF16)
        for j, v in enumerate((query, key, value, gate)):
            proj_ref[m, :, j * wide : (j + 1) * wide] = v
        attn = None
        for h in range(heads):
            w, mass = decays[h]
            raw = mm_nt(jnp.where(sets[h], query, jnp.zeros_like(query)), key)
            scores = (raw * head_width ** (-0.5) * w).astype(BF16)
            normed = mm(scores, value) * lax.rsqrt(mass)
            attn = jnp.where(sets[h], normed, 0.0 if attn is None else attn)
        attn_ref[m] = attn
        spread = convolve(side_shifts(attn, column), lambda i: tap_ref[i : i + 1, :])
        gate = gate.astype(F32)
        mixed = spread * (gate * jax.nn.sigmoid(gate))
        mixed = jnp.where(in_head, mixed, 0.0)
        mixed = jnp.concatenate(
            [mixed[:, :LANES], pltpu.roll(mixed[:, LANES:], spots[4], 1)], axis=1
        ).astype(BF16)
        mix_ref[m] = mixed
        if m == n_ref.shape[0] - 1:
            traffic.flush(1, 2, 3, 4)
        total_ref[m] = mm_nt(mixed, w_ref[:, 4 * LANES :]).astype(BF16)
    write_pieces(me, total_ref, other_ref, own_refs)


def attn_backward_kernel(cfg, traffic, me_ref, *refs):
    columns_first, heads, head_width = cfg
    shards, (proj_ref, log_ref, attn_ref, w_ref, tap_ref) = refs[:8], refs[8:13]
    g_ref, gproj_ref, gtap_ref, other_ref = refs[13:17]
    own_refs, total_ref = refs[17:21], refs[21]
    me = me_ref[0]
    wide = 2 * LANES
    gate_lane = heads * head_width - LANES
    spots = tail_spots(heads)
    scale = head_width ** (-0.5)
    mask = scan_mask(columns_first)
    column = grid_column()
    sets = lane_sets(wide, 0, head_width, heads)
    gate_sets = lane_sets(LANES, gate_lane, 1, heads)
    sublane = lax.broadcasted_iota(jnp.int32, (LANES, 1), 0)
    in_head = sets[0]
    for own in sets[1:]:
        in_head = in_head | own
    gather_pieces(me, shards, g_ref)
    gtap_ref[...] = jnp.zeros(gtap_ref.shape, F32)
    traffic.wait(9, 10, 11, 12)
    for m in range(g_ref.shape[0]):
        g_packed = mm(g_ref[m], w_ref[:, 4 * LANES :])
        g_mixed = jnp.where(in_head, join_tail(g_packed, 0, g_packed[:, LANES:], spots[4]), 0.0)
        query, key, value, gate = (proj_ref[m, :, j * wide : (j + 1) * wide] for j in range(4))
        gate = gate.astype(F32)
        sig = jax.nn.sigmoid(gate)
        attn = attn_ref[m]
        shifted = side_shifts(attn, column)
        spread = convolve(shifted, lambda i: tap_ref[i : i + 1, :])
        g_spread = g_mixed * (gate * sig)
        g_gate = g_mixed * spread * (sig * (1.0 + gate * (1.0 - sig)))
        for i, grad in enumerate(tap_grads(shifted, g_spread)):
            gtap_ref[i : i + 1, :] = grad if m == 0 else gtap_ref[i : i + 1, :] + grad
        g_attn = convolve(side_shifts(g_spread, column), lambda i: tap_ref[8 - i : 9 - i, :])
        logits = log_ref[m]
        decays, ones = decay_parts(logits, mask, gate_lane, heads)
        g_query = g_key = g_value = 0.0
        across = jnp.zeros((PATCHES, LANES), F32)
        down = jnp.zeros((LANES, PATCHES), F32)
        for h in range(heads):
            w, mass = decays[h]
            own_query = jnp.where(sets[h], query, jnp.zeros_like(query))
            raw = mm_nt(own_query, key) * scale
            own_grad = jnp.where(sets[h], g_attn, 0.0)
            g_mass = -0.5 * jnp.sum(own_grad * attn, axis=1, keepdims=True) / mass
            g_out = (own_grad * lax.rsqrt(mass)).astype(BF16)
            g_value = g_value + mm_tn((raw * w).astype(BF16), g_out)
            g_scores = mm_nt(g_out, value)
            g_raw = (g_scores * w * scale).astype(BF16)
            g_query = jnp.where(sets[h], mm(g_raw, key), g_query)
            g_key = g_key + mm_tn(g_raw, own_query)
            g_span = (g_scores * raw + g_mass) * w
            across = jnp.where(gate_sets[h], jnp.sum(g_span, axis=1, keepdims=True), across)
            down = jnp.where(sublane == gate_lane + h, rows_sum(g_span), down)
        g_rates = add_parts(mm_tn(ones, three_parts(across - down.T)))
        g_logits = (-g_rates * jax.nn.sigmoid(logits)).astype(BF16).astype(F32)
        g_bias = rows_sum(g_logits)
        gtap_ref[9:10, :LANES] = g_bias if m == 0 else gtap_ref[9:10, :LANES] + g_bias
        tails = g_logits
        for j, v in enumerate((g_query, g_key, g_value, g_gate)):
            gproj_ref[m, :, j * LANES : (j + 1) * LANES] = v[:, :LANES].astype(BF16)
            tails = tails + pltpu.roll(v[:, LANES:], spots[j], 1)
        gproj_ref[m, :, 4 * LANES :] = tails.astype(BF16)
        total = mm_nt(gproj_ref[m, :, : 4 * LANES], w_ref[:, : 4 * LANES])
        total = total + mm_nt(gproj_ref[m, :, 4 * LANES :], w_ref[:, 5 * LANES :])
        total_ref[m] = total.astype(BF16)
    write_pieces(me, total_ref, other_ref, own_refs)


def attn_weights_kernel(traffic, n_ref, gproj_ref, g_ref, mix_ref, gw_ref):
    traffic.wait(0, 3)
    for part in range(2):
        cols = slice(part * 2 * LANES, (part + 1) * 2 * LANES)
        total = mm_tn(n_ref[0], gproj_ref[0, :, cols])
        for m in range(1, n_ref.shape[0]):
            total = total + mm_tn(n_ref[m], gproj_ref[m, :, cols])
        gw_ref[:, cols] = total.astype(BF16)
    total = mm_tn(g_ref[0], mix_ref[0])
    tails = mm_tn(n_ref[0], gproj_ref[0, :, 4 * LANES :])
    for m in range(1, n_ref.shape[0]):
        total = total + mm_tn(g_ref[m], mix_ref[m])
        tails = tails + mm_tn(n_ref[m], gproj_ref[m, :, 4 * LANES :])
    gw_ref[:, 4 * LANES : 5 * LANES] = total[:, :LANES].astype(BF16)
    gw_ref[:, 5 * LANES :] = (total[:, LANES:] + tails).astype(BF16)


def stack_shards(shards, full_ref):
    for k, shard in enumerate(each_shard(shards)):
        images, rows, width = shard.shape
        full_ref[k * images * rows : (k + 1) * images * rows, :] = shard[...].reshape(
            images * rows, width
        )


def stack_kernel(traffic, *refs):
    stack_shards(refs[:8], refs[8])


def put_shard(k, value, shape, other_ref, own_refs):
    own, other = send_order(k)
    if own is None:
        other_ref[other] = value.astype(BF16).reshape(shape)
    else:
        own_refs[own][...] = value.astype(BF16).reshape(shape)


def put_shards(total, shape, other_ref, own_refs):
    rows = total.shape[0] // 8
    for k in range(8):
        put_shard(k, total[k * rows : (k + 1) * rows], shape, other_ref, own_refs)


def mlp_forward_kernel(left, traffic, *refs):
    shards, (w_ref, ub_ref) = refs[:8], refs[8:10]
    n_ref, pre_ref, hid_ref, other_ref = refs[10:14]
    own_refs = refs[14:18]
    main = (w_ref.shape[1] - LANES) // 2
    stack_shards(shards, n_ref)
    traffic.flush(0)
    traffic.wait(8)
    n = n_ref[...]
    pre = mm(n, w_ref[:, :main]) + ub_ref[:, :main]
    pre_ref[:, :main] = pre
    hidden = gelu_terms(pre)[0].astype(BF16)
    hid_ref[:, :main] = hidden
    last = mm(n, w_ref[:, 2 * main :]) + ub_ref[:, main:]
    pre_ref[:, main:] = last
    lane = lax.broadcasted_iota(jnp.int32, (1, LANES), 1)
    tail = jnp.where(lane < left, gelu_terms(last)[0], 0.0)
    tail = pltpu.roll(tail, LANES - left, 1).astype(BF16)
    hid_ref[:, main:] = tail
    traffic.flush(1, 2)
    total = mm_nt(hidden, w_ref[:, main : 2 * main]) + mm_nt(tail, w_ref[:, 2 * main :])
    put_shards(total, shards[0].shape, other_ref, own_refs)


def mlp_backward_kernel(left, traffic, *refs):
    given, (pre_ref, w_ref) = refs[:8], refs[8:10]
    g_ref, rest = refs[10], refs[11:]
    stack_shards(given, g_ref)
    traffic.wait(8, 9)
    gpre_ref, gub_ref, other_ref = rest[:3]
    own_refs = rest[3:]
    main = (w_ref.shape[1] - LANES) // 2
    g = g_ref[...]
    g_pre = mm(g, w_ref[:, main : 2 * main]) * gelu_terms(pre_ref[:, :main])[1]
    g_pre = g_pre.astype(BF16)
    gpre_ref[:, :main] = g_pre
    gub_ref[:, :main] = rows_sum(g_pre.astype(F32))
    lane = lax.broadcasted_iota(jnp.int32, (1, LANES), 1)
    last = pltpu.roll(mm(g, w_ref[:, 2 * main :]), left, 1) * gelu_terms(pre_ref[:, main:])[1]
    last = jnp.where(lane < left, last, 0.0).astype(BF16)
    gpre_ref[:, main:] = last
    gub_ref[:, main:] = rows_sum(last.astype(F32))
    total = mm_nt(g_pre, w_ref[:, :main]) + mm_nt(last, w_ref[:, 2 * main :])
    put_shards(total, own_refs[0].shape, other_ref, own_refs)


def mlp_both_kernel(left, traffic, n_ref, raw_ref, w_ref, ub_ref, mod_ref, *refs):
    gw_ref, gub_ref, gate_ref, other_ref = refs[:4]
    own_refs, end_ref, end_refs = refs[4:8], refs[8], refs[9:13]
    g_ref = refs[13]
    images, rows = own_refs[0].shape[:2]
    main = (w_ref.shape[1] - LANES) // 2
    lane = lax.broadcasted_iota(jnp.int32, (1, LANES), 1)
    spans = [(i % images, slice(i * rows, (i + 1) * rows)) for i in range(8 * images)]
    traffic.wait(0, 1)
    for m, span in spans:
        g_ref[span] = (mod_ref[m, 5:6] * raw_ref[span].astype(F32)).astype(BF16)
    traffic.wait(2)
    n, g = n_ref[...], g_ref[...]
    value, slope = gelu_terms(mm(n, w_ref[:, :main]) + ub_ref[:, :main])
    hidden = value.astype(BF16)
    g_pre = (mm(g, w_ref[:, main : 2 * main]) * slope).astype(BF16)
    value, slope = gelu_terms(mm(n, w_ref[:, 2 * main :]) + ub_ref[:, main:])
    tail = pltpu.roll(jnp.where(lane < left, value, 0.0), LANES - left, 1).astype(BF16)
    last = pltpu.roll(mm(g, w_ref[:, 2 * main :]), left, 1) * slope
    last = jnp.where(lane < left, last, 0.0).astype(BF16)
    gw_ref[:, :main] = mm_tn(n, g_pre).astype(BF16)
    gw_ref[:, main : 2 * main] = mm_tn(g, hidden).astype(BF16)
    gw_ref[:, 2 * main :] = (mm_tn(n, last) + mm_tn(g, tail)).astype(BF16)
    traffic.flush(0)
    gub_ref[:, :main] = rows_sum(g_pre.astype(F32))
    gub_ref[:, main:] = rows_sum(last.astype(F32))
    total = mm_nt(hidden, w_ref[:, main : 2 * main]) + mm_nt(tail, w_ref[:, 2 * main :])
    put_shards(total, own_refs[0].shape, end_ref, end_refs)
    traffic.flush(8, 9, 10, 11, 12)
    gates = [0.0] * images
    for m, span in spans:
        gates[m] = gates[m] + rows_sum(raw_ref[span].astype(F32) * total[span])
    for m in range(images):
        gate_ref[m] = gates[m]
    total = mm_nt(g_pre, w_ref[:, :main]) + mm_nt(last, w_ref[:, 2 * main :])
    put_shards(total, own_refs[0].shape, other_ref, own_refs)


def mlp_weights_kernel(traffic, n_ref, gpre_ref, g_ref, hid_ref, gw_ref):
    main = gpre_ref.shape[1] - LANES
    traffic.wait(0, 3)
    gw_ref[:, :main] = mm_tn(n_ref[...], gpre_ref[:, :main]).astype(BF16)
    gw_ref[:, main : 2 * main] = mm_tn(g_ref[...], hid_ref[:, :main]).astype(BF16)
    last = mm_tn(n_ref[...], gpre_ref[:, main:]) + mm_tn(g_ref[...], hid_ref[:, main:])
    gw_ref[:, 2 * main :] = last.astype(BF16)


def swap(value, tensor_bits, section_bit):
    tensors, sections = lax.axis_size("tensor"), lax.axis_size("section")
    route = [
        (t * sections + s, (t ^ tensor_bits) * sections + (s ^ section_bit))
        for t in range(tensors)
        for s in range(sections)
    ]
    return lax.ppermute(value, PLANE, route)


def gather_plane(own):
    xy, x, y = swap(own, 2, 1), swap(own, 0, 1), swap(own, 2, 0)
    return own, x, y, xy, *(swap(v, 1, 0) for v in (own, x, y, xy))


def scatter_plane(other, own, late=False):
    received = swap(other, 1, 0)
    sums = call(
        add_late_kernel if late else add_kernel,
        (out(own[0].shape, BF16),) * 4,
        *own,
        received,
        streamed=(0, 1, 2, 3) if late else (),
    )
    return (sums[0], swap(sums[3], 2, 1), swap(sums[1], 0, 1), swap(sums[2], 2, 0))


def spread_over(value, axes):
    count = math.prod(lax.axis_size(a) for a in axes)
    copies = jnp.broadcast_to(value[None], (count,) + value.shape)
    return lax.all_to_all(copies, axes, split_axis=0, concat_axis=0, tiled=True)


def gather_all(own):
    return lax.all_gather(own, "dp", axis=0, tiled=True)


def scatter_rows(partial):
    return lax.psum_scatter(partial, "dp", scatter_dimension=0, tiled=True)


def sinusoid(time_steps, channels):
    half_width = channels // 2
    frequency = jnp.exp(
        jnp.arange(half_width, dtype=jnp.float32) * (-math.log(10000.0) / half_width)
    )
    angles = time_steps.astype(jnp.float32)[:, None] * frequency[None, :]
    return jnp.concatenate([jnp.cos(angles), jnp.sin(angles)], axis=1)


def per_device(
    section_inputs,
    condition,
    timesteps,
    ada_weight,
    ada_bias,
    in_weight,
    gate_weight,
    gate_bias,
    conv_taps,
    out_weight,
    up_weight,
    up_bias,
    down_weight,
):
    d = lax.axis_index("dp")
    t = lax.axis_index("tensor")
    s = lax.axis_index("section")
    dps, tensors, sections = (lax.axis_size(a) for a in ("dp", "tensor", "section"))
    first = s == 0
    me = (t * sections + s).astype(jnp.int32).reshape(1)
    images = condition.shape[0]
    width = condition.shape[1]
    slab = in_weight.shape[2]
    heads = gate_weight.shape[2] // sections
    channels = in_weight.shape[3] // sections
    head_width = channels // heads
    units = up_weight.shape[2] // sections
    wide = 2 * LANES
    tail = channels - LANES
    rows = section_inputs.shape[2] // sections
    main = units // LANES * LANES
    left = units - main
    spots = tail_spots(heads)

    def cut(value, axis):
        half = value.shape[axis] // 2
        return (
            lax.slice_in_dim(value, 0, half, axis=axis),
            lax.slice_in_dim(value, half, 2 * half, axis=axis),
        )

    def swap_halves(keep, send):
        received = lax.ppermute(send, "section", [(0, 1), (1, 0)])
        return jnp.where(first, keep, received), jnp.where(first, received, keep)

    def choose(pair):
        return jnp.where(first, pair[0], pair[1]), jnp.where(first, pair[1], pair[0])

    cfg = (heads, channels)
    section = s.astype(jnp.int32).reshape(1)
    shape_a, shape_b = (slab, 6 * LANES), (slab, 2 * main + LANES)
    kept_a, sent_a = call(
        functools.partial(pack_attn_kernel, cfg),
        (out(shape_a, BF16),) * 2,
        section,
        in_weight[0],
        jnp.pad(gate_weight[0].astype(F32), ((0, 0), (0, LANES - gate_weight.shape[2]))),
        out_weight[0].T,
        scalars=1,
        streamed=(1,),
    )
    sent_a, condition, down_in = lax.optimization_barrier((sent_a, condition, down_weight[0]))
    received_a = lax.ppermute(sent_a, "section", [(0, 1), (1, 0)])
    kept_b, sent_b = call(
        functools.partial(pack_mlp_kernel, left),
        (out(shape_b, BF16),) * 2,
        section,
        up_weight[0],
        down_in.T,
        scalars=1,
        streamed=(1,),
    )
    received_b = lax.ppermute(sent_b, "section", [(0, 1), (1, 0)])

    def unit_halves(value):
        rest = sections * main
        return tuple(
            (value[:, h * main : (h + 1) * main], value[:, rest + h * left : rest + (h + 1) * left])
            for h in (0, 1)
        )

    def pack_small(gate_half, taps_half, up_half):
        return jnp.concatenate([gate_half.reshape(-1), taps_half.reshape(-1), up_half.reshape(-1)])

    def pack_halves(pack, *pairs):
        return tuple(pack(*(pair[i] for pair in pairs)) for i in (0, 1))

    x_pair = cut(section_inputs[0], 1)
    x_received = lax.ppermute(
        jnp.where(first, x_pair[1], x_pair[0]), "section", [(0, 1), (1, 0)]
    )
    x0 = jnp.where(first, x_pair[0], x_received)
    g1 = jnp.where(first, x_received, x_pair[1])
    taps_count = conv_taps.shape[1]
    up_row = up_bias[0].astype(F32)[None]
    small = swap_halves(
        *choose(
            pack_halves(
                pack_small,
                cut(gate_bias[0].astype(F32), 0),
                cut(conv_taps[0].astype(F32), 1),
                tuple(jnp.concatenate(v, axis=1) for v in unit_halves(up_row)),
            )
        )
    )

    def unpack_small(packed):
        gate_row = jnp.pad(packed[:heads][None], ((0, 0), (tail, LANES - heads - tail)))
        taps = packed[heads : heads + taps_count * channels].reshape(taps_count, channels)
        taps = jnp.pad(taps, ((0, 16 - taps_count), (0, wide - channels)))
        up_row = packed[heads + taps_count * channels :][None]
        return gate_row, taps, jnp.pad(up_row, ((0, 0), (0, main + LANES - units)))

    cond_vec = condition + sinusoid(timesteps, width)
    activated = jax.nn.silu(cond_vec).astype(BF16)
    slab_active = activated.reshape(images, dps, slab).transpose(1, 0, 2)
    slab_active = lax.all_to_all(slab_active, "dp", split_axis=0, concat_axis=0, tiled=True)
    slab_active = slab_active.reshape(dps * images, slab)
    slab_active, received_a = lax.optimization_barrier((slab_active, received_a))
    mod_part = jnp.dot(slab_active, ada_weight[0], preferred_element_type=F32)
    mod_parts = lax.all_to_all(
        mod_part.reshape(dps, images, -1), "dp", split_axis=0, concat_axis=0, tiled=True
    )
    mod_share = jnp.sum(mod_parts, axis=0) + ada_bias[0].astype(F32)
    mod_all = spread_over(mod_share, ("section", "tensor"))
    received_b, mod_all = lax.optimization_barrier((received_b, mod_all))
    mod_all = mod_all.reshape(sections, tensors, images, -1).transpose(0, 2, 1, 3)
    mod_all = mod_all.reshape(sections, images, 6, width)
    mods = (mod_all[0], mod_all[1])

    shard = out((images, rows, width), BF16)
    shard_wide = out((images, rows, width), F32)
    vector = out((images, 1, width), F32)
    pieces_out = (out((4, images, rows, width), BF16),) + (shard,) * 4
    full = out((images, PATCHES, width), BF16)
    flat = out((images * PATCHES, width), BF16)
    total_rows = images * PATCHES
    kept = pltpu.VMEM((images, PATCHES, width), BF16)
    middle_flops = 2 * total_rows * PATCHES * wide * heads * 6
    attn_flops = 2 * total_rows * width * wide * 5 + middle_flops
    mlp_flops = 4 * total_rows * width * units

    def attn_forward(b, shards):
        w, _, gate_row, taps, _ = weights[b]
        body = functools.partial(attn_forward_kernel, (b == 1, heads, head_width))
        found = call(
            body,
            (
                full,
                out((images, PATCHES, 4 * wide), BF16),
                out((images, PATCHES, LANES), F32),
                out((images, PATCHES, wide), F32),
                out((images, PATCHES, wide), BF16),
                *pieces_out,
            ),
            me,
            *shards,
            w,
            gate_row,
            taps,
            scalars=1,
            flops=attn_flops,
            scratch=[kept],
            streamed=(9,),
            saved=(0, 1, 2, 3, 4),
        )
        return found[:5], scatter_plane(found[5], found[6:])

    def attn_backward(b, shards, saved, after=()):
        w, _, _, taps, _ = weights[b]
        body = functools.partial(attn_backward_kernel, (b == 1, heads, head_width))
        found = call(
            body,
            (
                full,
                out((images, PATCHES, 5 * LANES), BF16),
                out((16, wide), F32),
                *pieces_out,
            ),
            me,
            *shards,
            saved[1],
            saved[2],
            saved[3],
            w,
            taps,
            scalars=1,
            flops=2 * attn_flops,
            scratch=[kept],
            streamed=(9, 10, 11, 12),
            after=after,
        )
        terms = scatter_plane(found[3], found[4:])
        (grads,) = call(
            attn_weights_kernel,
            (out((width, 6 * LANES), BF16),),
            saved[0],
            found[1],
            found[0],
            saved[4],
            flops=2 * total_rows * width * wide * 5,
            after=terms if b else (),
            streamed=(0, 3),
            saved=(0,),
        )
        return terms, grads, found[2]

    def mlp_forward(b, normed):
        _, w, _, _, up_row = weights[b]
        found = call(
            functools.partial(mlp_forward_kernel, left),
            (
                flat,
                out((total_rows, main + LANES), F32),
                out((total_rows, main + LANES), BF16),
                *pieces_out,
            ),
            *gather_plane(normed),
            w,
            up_row,
            flops=mlp_flops,
            streamed=(8,),
            saved=(0, 1, 2),
        )
        return found[:3], scatter_plane(found[3], found[4:])

    shape_gw = out((width, 2 * main + LANES), BF16)
    shape_gub = out((1, main + LANES), F32)

    def mlp_both(b, gathered, gradient):
        _, w, _, _, up_row = weights[b]
        found = call(
            functools.partial(mlp_both_kernel, left),
            (shape_gw, shape_gub, vector, *pieces_out, *pieces_out),
            gathered,
            gradient,
            w,
            up_row,
            mods[b],
            flops=3 * mlp_flops,
            scratch=[pltpu.VMEM(flat.shape, flat.dtype)],
            streamed=(0, 1, 2),
            saved=(0, 8, 9, 10, 11, 12),
        )
        return scatter_plane(found[3], found[4:8]), found[0], found[1], found[2], found[8:]

    def mlp_backward(b, given, saved, after=()):
        _, w, _, _, _ = weights[b]
        found = call(
            functools.partial(mlp_backward_kernel, left),
            (flat, out((total_rows, main + LANES), BF16), shape_gub, *pieces_out),
            *given,
            saved[1],
            w,
            flops=mlp_flops,
            streamed=(8, 9),
            after=after,
        )
        terms = scatter_plane(found[3], found[4:])
        (grads,) = call(
            mlp_weights_kernel,
            (shape_gw,),
            saved[0],
            found[1],
            found[0],
            saved[2],
            flops=mlp_flops,
            after=terms,
            streamed=(0, 3),
            saved=(0,),
        )
        return terms, grads, found[2]

    def of_block(b, kept, received):
        return jnp.where(first == (b == 0), kept, received)

    full_a0 = gather_all(of_block(0, kept_a, received_a))
    middle = [of_block(0, kept_b, received_b), of_block(1, kept_a, received_a)]
    full_middle = gather_all(jnp.concatenate(middle, axis=1))
    full_b0 = Columns(full_middle, 0, middle[0].shape[1])
    full_a1 = Columns(full_middle, middle[0].shape[1], middle[1].shape[1])
    (g1_all,) = call(stack_kernel, (flat,), *gather_plane(g1), saved=(0,))
    (normed,) = call(start_kernel, (shard,), x0, mods[0])
    shards, g1_all, next_b = lax.optimization_barrier(
        (
            gather_plane(normed),
            g1_all,
            of_block(1, kept_b, received_b),
        )
    )
    weights = [
        (full_a0, full_b0, *unpack_small(small[0])),
        (full_a1, gather_all(next_b), *unpack_small(small[1])),
    ]

    def to_second(value):
        return lax.ppermute(value, "section", [(0, 1)])

    def to_first(value):
        return lax.ppermute(value, "section", [(1, 0)])

    attn0, terms = attn_forward(0, shards)
    att0, aft0, normed = call(
        after_attn_kernel, (shard_wide, shard_wide, shard), *terms, x0, mods[0], saved=(0, 1)
    )
    mlp0, terms = mlp_forward(0, normed)
    mlp_out0, x1, normed = call(
        between_kernel,
        (shard_wide, shard, shard),
        *terms,
        aft0,
        mods[0],
        mods[1],
        saved=(0, 1),
    )
    attn1, terms = attn_forward(1, gather_plane(normed))
    att1, aft1, normed = call(
        after_attn_kernel, (shard_wide, shard_wide, shard), *terms, x1, mods[1], saved=(0, 1)
    )

    three, six = (out((images, n, width), F32) for n in (3, 6))
    (n_all,) = call(stack_kernel, (flat,), *gather_plane(normed), saved=(0,))
    terms, mlp_grads1, g_up_bias1, g_gate_two1, end_pieces = mlp_both(1, n_all, g1_all)
    g_after, g_attn, g_some = call(
        back_mlp_rows_kernel,
        (shard_wide, shard, three),
        *terms,
        g1,
        aft1,
        att1,
        mods[1],
        saved=(0,),
    )
    sum_b1 = scatter_rows(mlp_grads1)
    terms, attn_grads1, g_taps1 = attn_backward(1, gather_plane(g_attn), attn1)
    g0, g_mlp, g_mods1, g_gate_two0 = call(
        back_between_kernel,
        (shard, shard, six, vector),
        *terms,
        g_after,
        x1,
        mods[1],
        g_some,
        g_gate_two1,
        mods[0],
        mlp_out0,
    )
    sum_a1 = scatter_rows(attn_grads1)
    terms, mlp_grads0, g_up_bias0 = mlp_backward(0, gather_plane(g_mlp), mlp0, (attn_grads1,))
    g_after, g_attn, g_some = call(
        back_mlp_rows_kernel,
        (shard_wide, shard, three),
        *terms,
        g0,
        aft0,
        att0,
        mods[0],
        after=(sum_b1,),
        saved=(0,),
    )
    terms, attn_grads0, g_taps0 = attn_backward(0, gather_plane(g_attn), attn0, (mlp_grads0,))
    g_in, g_mods0 = call(
        back_end_kernel,
        (shard, six),
        *terms,
        g_after,
        x0,
        mods[0],
        g_some,
        g_gate_two0,
        after=(attn_grads0,),
    )

    sum_b0, sum_a0 = scatter_rows(mlp_grads0), scatter_rows(attn_grads0)

    g_mod = jnp.stack([g_mods0.reshape(images, -1), g_mods1.reshape(images, -1)])
    g_mod = g_mod.reshape(sections, images, tensors, -1).transpose(0, 2, 1, 3)
    columns = g_mod.shape[3]
    g_mod = g_mod.reshape(sections, tensors, images * columns)
    taps_rows = taps_count + 1

    def small_grads(g_taps, g_up_bias):
        return jnp.concatenate([g_taps[:taps_rows].reshape(-1), g_up_bias.reshape(-1)])

    g_small = jnp.stack([small_grads(g_taps0, g_up_bias0), small_grads(g_taps1, g_up_bias1)])
    to_tensor = (jnp.arange(tensors) == t)[None, :, None]
    g_small = jnp.where(to_tensor, g_small[:, None], 0.0)
    g_sent = jnp.concatenate([g_mod, g_small], axis=2).reshape(sections * tensors, -1)
    g_parts = lax.all_to_all(
        g_sent, ("section", "tensor"), split_axis=0, concat_axis=0, tiled=True
    )
    g_parts, sum_b1, sum_a1 = lax.optimization_barrier((g_parts, sum_b1, sum_a1))
    other_b1, other_a1 = to_second(sum_b1), to_second(sum_a1)
    g_share = jnp.sum(g_parts[:, : images * columns], axis=0)
    small_parts = g_parts[:, images * columns :].reshape(sections, tensors, -1).sum(1)
    g_all = spread_over(jnp.concatenate([g_share, small_parts.reshape(-1)]), ("dp",))
    g_all, end_pieces, sum_b0 = lax.optimization_barrier((g_all, end_pieces, sum_b0))
    others = other_b1, other_a1, to_first(sum_b0)
    (block_out,) = call(
        end_kernel, (shard,), *scatter_plane(end_pieces[0], end_pieces[1:], True), aft1, mods[1]
    )
    small_own = jnp.sum(g_all[:, images * columns :], axis=0).reshape(sections, -1)
    g_all = g_all[:, : images * columns].reshape(dps * images, columns).astype(BF16)
    grad_ada_bias = jnp.sum(g_all.astype(F32), axis=0)
    act_part = jnp.einsum("me,de->md", g_all, ada_weight[0], preferred_element_type=F32)
    act_part, other_b1 = lax.optimization_barrier((act_part, others[0]))
    others = other_b1, *others[1:]
    plane = sections * tensors
    act_sent = jnp.broadcast_to(
        act_part.reshape(dps, 1, images, slab), (dps, plane, images, slab)
    )
    act_all = lax.all_to_all(
        act_sent.reshape(-1, images, slab),
        ("dp", "section", "tensor"),
        split_axis=0,
        concat_axis=0,
        tiled=True,
    )
    act_all, other_b0 = lax.optimization_barrier((act_all, others[2]))
    others = *others[:2], other_b0
    act_all = jnp.sum(act_all.reshape(dps, plane, images, slab), axis=1)
    act_grad = act_all.reshape(dps, images, slab).transpose(1, 0, 2).reshape(images, width)
    cond_grad = jax.vjp(jax.nn.silu, cond_vec)[1](act_grad)[0]

    ends_from_first = lax.ppermute(block_out, "section", [(0, 1)])
    ends_from_second = lax.ppermute(g_in, "section", [(1, 0)])
    mine = jnp.where(first, g_in, block_out)
    received = jnp.where(first, ends_from_second, ends_from_first)
    section_ends = jnp.concatenate(
        [jnp.where(first, mine, received), jnp.where(first, received, mine)], axis=1
    )
    cond_grad, section_ends, sum_a0, g_all, others = lax.optimization_barrier(
        (cond_grad, section_ends, sum_a0, g_all, others)
    )
    other_b1, other_a1, other_b0 = others
    other_a0 = to_first(sum_a0)
    grad_ada = jnp.einsum("md,me->de", slab_active, g_all, preferred_element_type=F32)

    small_taps = small_own[:, : taps_rows * wide].reshape(sections, taps_rows, wide)
    grad_gateb = small_taps[:, taps_count, tail : tail + heads].reshape(-1)
    grad_taps = small_taps[:, :taps_count, :channels].transpose(1, 0, 2)
    grad_taps = grad_taps.reshape(taps_count, sections * channels)
    up_halves = small_own[:, taps_rows * wide :]
    grad_up_bias = jnp.concatenate(
        [up_halves[:, :main].reshape(-1), up_halves[:, main : main + left].reshape(-1)]
    )

    grad_up, grad_down = call(
        functools.partial(unpack_mlp_kernel, left),
        (out(up_weight.shape[1:], F32),) * 2,
        section,
        sum_b0,
        other_b0,
        sum_b1,
        other_b1,
        scalars=1,
    )
    grad_down = grad_down.T
    grad_in, grad_gate, grad_out = call(
        functools.partial(unpack_attn_kernel, cfg),
        (
            out(in_weight.shape[1:], F32),
            out(gate_weight.shape[1:], F32),
            out((slab, out_weight.shape[1]), F32),
        ),
        section,
        sum_a0,
        other_a0,
        sum_a1,
        other_a1,
        scalars=1,
    )
    grad_out = grad_out.T

    return (
        section_ends[None],
        cond_grad,
        grad_ada[None],
        grad_ada_bias[None],
        grad_in[None],
        grad_gate[None],
        grad_gateb[None],
        grad_taps[None],
        grad_out[None],
        grad_up[None],
        grad_up_bias[None],
        grad_down[None],
    )


def solution(mesh):
    in_specs = (
        P("section", "dp", "tensor", None),
        P("dp", None),
        P("dp"),
        P("section", "dp", "tensor"),
        P("section", "tensor"),
        P("section", None, "dp", "tensor"),
        P("section", "dp", "tensor"),
        P("section", "tensor"),
        P("section", None, "tensor"),
        P("section", "tensor", "dp"),
        P("section", "dp", "tensor"),
        P("section", "tensor"),
        P("section", "tensor", "dp"),
    )
    out_specs = (
        P("section", "dp", "tensor", None),
        P("dp", None),
        P("section", "dp", "tensor"),
        P("section", "tensor"),
        P("section", None, "dp", "tensor"),
        P("section", "dp", "tensor"),
        P("section", "tensor"),
        P("section", None, "tensor"),
        P("section", "tensor", "dp"),
        P("section", "dp", "tensor"),
        P("section", "tensor"),
        P("section", "tensor", "dp"),
    )
    return jax.shard_map(
        per_device, mesh=mesh, in_specs=in_specs, out_specs=out_specs, check_vma=False
    )
```

```python
import functools
import math

import jax
import jax.numpy as jnp
from jax import lax
from jax.experimental import pallas as pl
from jax.experimental.pallas import tpu as pltpu
from jax.sharding import PartitionSpec as P

SIDE = 16
PATCHES = SIDE * SIDE
LANES = 128
F32 = jnp.float32
BF16 = jnp.bfloat16
PLANE = ("tensor", "section")


class Traffic:
    def __init__(self, arriving, leaving):
        self.arriving, self.leaving, self.left = arriving, leaving, set()

    def wait(self, *places):
        for at in places:
            self.arriving[at].wait()

    def flush(self, *places):
        for at in places:
            self.leaving[at].start()
            self.left.add(at)


class Columns:
    def __init__(self, array, start, width):
        self.array, self.start = array, start
        self.shape, self.dtype = (array.shape[0], width), array.dtype
        self.size = array.shape[0] * width

    def source(self, ref):
        return ref.at[:, self.start : self.start + self.shape[1]]


def call(body, outs, *args, scalars=0, flops=0, scratch=(), after=(), streamed=(), saved=()):
    count, waits, many = len(args), len(after), len(outs)
    given = args
    moving = bool(streamed or saved)

    def kernel(*refs):
        ins, out_refs = list(refs[:count]), list(refs[count + waits : count + waits + many])
        rest = refs[count + waits + many :]
        own, held = rest[: len(scratch)], rest[len(scratch) :]
        arriving, leaving = {}, {}
        for i, at in enumerate(streamed):
            source = given[at].source(ins[at]) if isinstance(given[at], Columns) else ins[at]
            arriving[at] = pltpu.make_async_copy(source, held[i], held[-1].at[i])
            ins[at] = held[i]
        for i, at in enumerate(saved, len(streamed)):
            leaving[at] = pltpu.make_async_copy(held[i], out_refs[at], held[-1].at[i])
            out_refs[at] = held[i]
        traffic = Traffic(arriving, leaving)
        for copy in arriving.values():
            copy.start()
        if moving:
            body(traffic, *ins, *out_refs, *own)
        else:
            body(*ins, *out_refs, *own)
        traffic.flush(*[at for at in saved if at not in traffic.left])
        for copy in leaving.values():
            copy.wait()

    moved = sum(a.size * a.dtype.itemsize for a in args)
    moved += sum(math.prod(o.shape) * o.dtype.itemsize for o in outs)
    specs = [pl.BlockSpec(memory_space=pltpu.SMEM)] * scalars
    specs += [
        pl.BlockSpec(memory_space=pltpu.HBM if i in streamed else pltpu.VMEM)
        for i in range(scalars, count)
    ]
    large = [a.size > 2**17 for a in after]
    specs += [pl.BlockSpec(memory_space=pltpu.HBM if v else pl.ANY) for v in large]
    after = [
        pltpu.with_memory_space_constraint(a, pltpu.HBM) if v else a for a, v in zip(after, large)
    ]
    spaces = [pltpu.HBM if i in saved else pltpu.VMEM for i in range(many)]
    shapes = [
        pltpu.HBM(o.shape, o.dtype) if i in saved else o for i, o in enumerate(outs)
    ]
    args = [a.array if isinstance(a, Columns) else a for a in args]
    args = [
        pltpu.with_memory_space_constraint(a, pltpu.HBM) if i in streamed else a
        for i, a in enumerate(args)
    ]
    hold = [pltpu.VMEM(given[i].shape, given[i].dtype) for i in streamed]
    hold += [pltpu.VMEM(outs[i].shape, outs[i].dtype) for i in saved]
    if moving:
        hold.append(pltpu.SemaphoreType.DMA((len(hold),)))
    return pl.pallas_call(
        kernel,
        out_shape=tuple(shapes),
        in_specs=specs,
        out_specs=tuple(pl.BlockSpec(memory_space=space) for space in spaces),
        scratch_shapes=[*scratch, *hold],
        compiler_params=pltpu.CompilerParams(vmem_limit_bytes=6 * 2**20 + moved * 3 // 2),
        cost_estimate=pl.CostEstimate(flops=flops, bytes_accessed=moved, transcendentals=0),
    )(*args, *after)


def out(shape, dtype):
    return jax.ShapeDtypeStruct(shape, dtype)


def mm(a, b):
    return lax.dot_general(a, b, (((1,), (0,)), ((), ())), preferred_element_type=F32)


def mm_nt(a, b):
    return lax.dot_general(a, b, (((1,), (1,)), ((), ())), preferred_element_type=F32)


def mm_tn(a, b):
    return lax.dot_general(a, b, (((0,), (0,)), ((), ())), preferred_element_type=F32)


def normalize(v):
    centered = v - jnp.mean(v, axis=-1, keepdims=True)
    scale = lax.rsqrt(jnp.mean(centered * centered, axis=-1, keepdims=True) + 1e-06)
    return centered * scale, scale


def norm_grad(hat, rstd, grad):
    inner = jnp.mean(grad * hat, axis=-1, keepdims=True)
    return rstd * (grad - jnp.mean(grad, axis=-1, keepdims=True) - hat * inner)


def gather_total(pieces):
    total = pieces[0][...].astype(F32)
    for piece in pieces[1:]:
        total = total + piece[...].astype(F32)
    return total


def rows_sum(v):
    return jnp.sum(v, axis=0, keepdims=True)


def gelu_terms(x):
    k = math.sqrt(2.0 / math.pi)
    th = jnp.tanh(k * (x + 0.044715 * x * x * x))
    value = 0.5 * x * (1.0 + th)
    slope = 0.5 * (1.0 + th) + 0.5 * x * (1.0 - th * th) * k * (1.0 + 3 * 0.044715 * x * x)
    return value, slope


def start_kernel(x_ref, mod_ref, n_ref):
    for m in range(x_ref.shape[0]):
        hat, _ = normalize(x_ref[m].astype(F32))
        n_ref[m] = (hat * (1.0 + mod_ref[m, 1:2]) + mod_ref[m, 0:1]).astype(BF16)


def add_kernel(a, b, c, d, recv, *outs):
    for j, own in enumerate((a, b, c, d)):
        outs[j][...] = (own[...].astype(F32) + recv[j].astype(F32)).astype(BF16)


def add_late_kernel(traffic, a, b, c, d, recv, *outs):
    traffic.wait(0, 1, 2, 3)
    add_kernel(a, b, c, d, recv, *outs)


def after_attn_kernel(traffic, p0, p1, p2, p3, x_ref, mod_ref, att_ref, aft_ref, n_ref):
    for m in range(x_ref.shape[0]):
        att = gather_total([p.at[m] for p in (p0, p1, p2, p3)])
        aft = x_ref[m].astype(F32) + mod_ref[m, 2:3] * att
        hat, _ = normalize(aft)
        att_ref[m] = att
        aft_ref[m] = aft
        n_ref[m] = (hat * (1.0 + mod_ref[m, 4:5]) + mod_ref[m, 3:4]).astype(BF16)


def between_kernel(traffic, p0, p1, p2, p3, aft_ref, mod_ref, next_ref, mlp_ref, x_ref, n_ref):
    for m in range(aft_ref.shape[0]):
        mlp = gather_total([p.at[m] for p in (p0, p1, p2, p3)])
        x = (aft_ref[m] + mod_ref[m, 5:6] * mlp).astype(BF16)
        hat, _ = normalize(x.astype(F32))
        mlp_ref[m] = mlp
        x_ref[m] = x
        n_ref[m] = (hat * (1.0 + next_ref[m, 1:2]) + next_ref[m, 0:1]).astype(BF16)


def end_kernel(p0, p1, p2, p3, aft_ref, mod_ref, x_ref):
    for m in range(aft_ref.shape[0]):
        mlp = gather_total([p.at[m] for p in (p0, p1, p2, p3)])
        x_ref[m] = (aft_ref[m] + mod_ref[m, 5:6] * mlp).astype(BF16)


def back_mlp_rows_kernel(traffic, p0, p1, p2, p3, g_ref, aft_ref, att_ref, mod_ref, ga_ref, gt_ref, gm_ref):
    for m in range(aft_ref.shape[0]):
        gn = gather_total([p.at[m] for p in (p0, p1, p2, p3)])
        hat, rstd = normalize(aft_ref[m])
        grad = g_ref[m].astype(F32) + norm_grad(hat, rstd, gn * (1.0 + mod_ref[m, 4:5]))
        ga_ref[m] = grad
        gt_ref[m] = (mod_ref[m, 2:3] * grad).astype(BF16)
        gm_ref[m, 0:1] = rows_sum(grad * att_ref[m])
        gm_ref[m, 1:2] = rows_sum(gn)
        gm_ref[m, 2:3] = rows_sum(gn * hat)


def back_attn_rows(pieces, ga_ref, x_ref, mod_ref, some_ref, gate_ref, gm_ref, m):
    gn = gather_total([p.at[m] for p in pieces])
    hat, rstd = normalize(x_ref[m].astype(F32))
    grad = ga_ref[m] + norm_grad(hat, rstd, gn * (1.0 + mod_ref[m, 1:2]))
    gm_ref[m, 0:1] = rows_sum(gn)
    gm_ref[m, 1:2] = rows_sum(gn * hat)
    gm_ref[m, 2:5] = some_ref[m]
    gm_ref[m, 5:6] = gate_ref[m]
    return grad.astype(BF16)


def back_between_kernel(p0, p1, p2, p3, ga_ref, x_ref, mod_ref, some_ref, gate_ref, prev_ref, mlp_ref, *outs):
    g_ref, gmlp_ref, gm_ref, next_ref = outs
    for m in range(x_ref.shape[0]):
        grad = back_attn_rows((p0, p1, p2, p3), ga_ref, x_ref, mod_ref, some_ref, gate_ref, gm_ref, m)
        g_ref[m] = grad
        wide = grad.astype(F32)
        gmlp_ref[m] = (prev_ref[m, 5:6] * wide).astype(BF16)
        next_ref[m] = rows_sum(wide * mlp_ref[m])


def back_end_kernel(p0, p1, p2, p3, ga_ref, x_ref, mod_ref, some_ref, gate_ref, g_ref, gm_ref):
    for m in range(x_ref.shape[0]):
        g_ref[m] = back_attn_rows((p0, p1, p2, p3), ga_ref, x_ref, mod_ref, some_ref, gate_ref, gm_ref, m)


def scan_mask(columns_first):
    def place(number):
        if columns_first:
            return (number % SIDE) * SIDE + number // SIDE
        return number

    shape = (PATCHES, PATCHES)
    later = place(lax.broadcasted_iota(jnp.int32, shape, 0))
    return later >= place(lax.broadcasted_iota(jnp.int32, shape, 1))


def grid_column():
    return lax.broadcasted_iota(jnp.int32, (PATCHES, 1), 0) % SIDE


def side_shifts(a, column):
    left = jnp.where(column == 0, 0.0, pltpu.roll(a, 1, 0))
    right = jnp.where(column == SIDE - 1, 0.0, pltpu.roll(a, PATCHES - 1, 0))
    return left, a, right


def convolve(shifted, tap):
    sums = []
    for row in range(3):
        terms = [shifted[col] * tap(3 * row + col) for col in range(3)]
        sums.append(terms[0] + terms[1] + terms[2])
    zeros = jnp.zeros((SIDE, sums[0].shape[1]), F32)
    above = jnp.concatenate([zeros, sums[0][:-SIDE]], axis=0)
    below = jnp.concatenate([sums[2][SIDE:], zeros], axis=0)
    return shifted[1] + sums[1] + above + below


def tap_grads(shifted, grad):
    found = []
    for row in range(3):
        for col in range(3):
            if row == 0:
                product = shifted[col][:-SIDE] * grad[SIDE:]
            elif row == 1:
                product = shifted[col] * grad
            else:
                product = shifted[col][SIDE:] * grad[:-SIDE]
            found.append(rows_sum(product))
    return found


def lane_sets(width, first, head_width, heads):
    lane = lax.broadcasted_iota(jnp.int32, (1, width), 1)
    return [
        (lane >= first + h * head_width) & (lane < first + (h + 1) * head_width)
        for h in range(heads)
    ]


def three_parts(v):
    parts = []
    for _ in range(3):
        parts.append(v.astype(BF16))
        v = v - parts[-1].astype(F32)
    return jnp.concatenate(parts, axis=1)


def add_parts(v):
    return v[:, :LANES] + v[:, LANES : 2 * LANES] + v[:, 2 * LANES :]


def decay_parts(logits, mask, gate_lane, heads):
    rates = -(jnp.maximum(logits, 0.0) + jnp.log1p(jnp.exp(-jnp.abs(logits))))
    ones = jnp.where(mask, 1.0, 0.0).astype(BF16)
    totals = add_parts(mm(ones, three_parts(rates)))
    turned = totals.T
    decays = []
    for h in range(heads):
        at = gate_lane + h
        spans = jnp.where(mask, totals[:, at : at + 1] - turned[at : at + 1, :], -1e30)
        w = jnp.exp(spans)
        decays.append((w, jnp.sum(w, axis=1, keepdims=True)))
    return decays, ones


def send_order(k):
    return (0, 1, None, None, 2, 3, None, None)[k], (None, None, 0, 1, None, None, 2, 3)[k]


def write_pieces(me, total_ref, other_ref, own_refs):
    rows = total_ref.shape[1] // 8
    for k in range(8):
        spot = pl.ds(pl.multiple_of(jnp.bitwise_xor(me, k) * rows, rows), rows)
        own, other = send_order(k)
        if own is None:
            other_ref[other] = total_ref[:, spot, :]
        else:
            own_refs[own][...] = total_ref[:, spot, :]


def each_shard(refs):
    own, x, y, xy, core, core_x, core_y, core_xy = refs
    return own, x, core, core_x, y, xy, core_y, core_xy


def gather_pieces(me, shard_refs, full_ref):
    rows = full_ref.shape[1] // 8
    for k, shard in enumerate(each_shard(shard_refs)):
        spot = pl.ds(pl.multiple_of(jnp.bitwise_xor(me, k) * rows, rows), rows)
        full_ref[:, spot, :] = shard[...]


def tail_spots(heads):
    return (0, 32, 48, 64, 80)


def join_tail(packed, piece, tails, lane):
    tile = packed[:, piece * LANES : (piece + 1) * LANES]
    return jnp.concatenate([tile, pltpu.roll(tails, (LANES - lane) % LANES, 1)], axis=1)


def lanes():
    return lax.broadcasted_iota(jnp.int32, (1, LANES), 1)


def half_tiles(tiles, at):
    if at == 0:
        return tiles[0], tiles[1]
    shift = 2 * LANES - at
    first = jnp.where(lanes() < shift, pltpu.roll(tiles[1], shift, 1), pltpu.roll(tiles[2], shift, 1))
    return first, pltpu.roll(tiles[2], shift, 1)


def pack_attn_kernel(cfg, traffic, sec_ref, in_ref, gate_ref, out_ref, keep_ref, send_ref):
    heads, channels = cfg
    traffic.wait(1)
    spots = tail_spots(heads)
    tail = channels - LANES
    rows = in_ref.shape[1]
    short = jnp.zeros((rows, 3 * LANES - 2 * channels), F32)
    keep_first = sec_ref[0] == 0
    lane = lanes()
    tails = [gate_ref[...], pltpu.roll(gate_ref[...], LANES - heads, 1)]
    tails = [
        jnp.where((lane >= tail) & (lane < tail + heads), pltpu.roll(v, tail, 1), 0.0) for v in tails
    ]
    for j in range(5):
        ref = out_ref if j == 4 else in_ref.at[j]
        tiles = [ref[:, :LANES].astype(F32), ref[:, LANES : 2 * LANES].astype(F32)]
        tiles.append(jnp.concatenate([ref[:, 2 * LANES :].astype(F32), short], axis=1))
        whole = []
        for h in range(2):
            tile, rest = half_tiles(tiles, h * channels)
            whole.append(tile)
            tails[h] = tails[h] + pltpu.roll(jnp.where(lane < tail, rest, 0.0), spots[j], 1)
        cols = slice(j * LANES, (j + 1) * LANES)
        keep_ref[:, cols] = jnp.where(keep_first, whole[0], whole[1]).astype(BF16)
        send_ref[:, cols] = jnp.where(keep_first, whole[1], whole[0]).astype(BF16)
    cols = slice(5 * LANES, 6 * LANES)
    keep_ref[:, cols] = jnp.where(keep_first, tails[0], tails[1]).astype(BF16)
    send_ref[:, cols] = jnp.where(keep_first, tails[1], tails[0]).astype(BF16)


def pack_mlp_kernel(left, traffic, sec_ref, up_ref, down_ref, keep_b_ref, send_b_ref):
    keep_first = sec_ref[0] == 0
    lane = lanes()
    main = (keep_b_ref.shape[1] - LANES) // 2
    traffic.wait(1)
    at = 0
    for ref in (up_ref, down_ref):
        low, high = ref[:, :main], ref[:, main : 2 * main]
        keep_b_ref[:, at : at + main] = jnp.where(keep_first, low, high)
        send_b_ref[:, at : at + main] = jnp.where(keep_first, high, low)
        at += main
    up, down = (ref[:, 2 * main :].astype(F32) for ref in (up_ref, down_ref))
    low = jnp.where(lane < left, up, pltpu.roll(down, left, 1)).astype(BF16)
    high = jnp.where(lane < left, pltpu.roll(up, left, 1), down).astype(BF16)
    keep_b_ref[:, at:] = jnp.where(keep_first, low, high)
    send_b_ref[:, at:] = jnp.where(keep_first, high, low)


def unpack_mlp_kernel(left, sec_ref, sum0_ref, other0_ref, sum1_ref, other1_ref, up_ref, down_ref):
    in_first = sec_ref[0] == 0
    main = (sum0_ref.shape[1] - LANES) // 2
    lane = lanes()

    def both(cols):
        low = jnp.where(in_first, sum0_ref[:, cols], other1_ref[:, cols])
        return low.astype(F32), jnp.where(in_first, other0_ref[:, cols], sum1_ref[:, cols]).astype(F32)

    up_ref[:, :main], up_ref[:, main : 2 * main] = both(slice(0, main))
    down_ref[:, :main], down_ref[:, main : 2 * main] = both(slice(main, 2 * main))
    low, high = both(slice(2 * main, 2 * main + LANES))
    up_ref[:, 2 * main :] = jnp.where(lane < left, low, pltpu.roll(high, left, 1))
    down_ref[:, 2 * main :] = jnp.where(lane < left, pltpu.roll(low, LANES - left, 1), high)


def unpack_attn_kernel(
    cfg, sec_ref, sum0_ref, other0_ref, sum1_ref, other1_ref, in_ref, gate_ref, out_ref
):
    heads, channels = cfg
    spots = tail_spots(heads)
    tail = channels - LANES
    in_first = sec_ref[0] == 0
    lane = lanes()
    shift = channels - LANES

    def both(cols):
        low = jnp.where(in_first, sum0_ref[:, cols], other1_ref[:, cols])
        return low.astype(F32), jnp.where(in_first, other0_ref[:, cols], sum1_ref[:, cols]).astype(F32)

    low_tails, high_tails = both(slice(5 * LANES, 6 * LANES))
    for j in range(5):
        ref = out_ref if j == 4 else in_ref.at[j]
        low, high = both(slice(j * LANES, (j + 1) * LANES))
        ref[:, :LANES] = low
        high = pltpu.roll(high, shift, 1)
        low_tail = pltpu.roll(low_tails, (LANES - spots[j]) % LANES, 1)
        high_tail = pltpu.roll(high_tails, (LANES - spots[j] + shift) % LANES, 1)
        ref[:, LANES : 2 * LANES] = jnp.where(lane < tail, low_tail, high)
        last = jnp.where(lane < shift, high, high_tail)
        ref[:, 2 * LANES :] = last[:, : 2 * channels - 2 * LANES]
    low_gate = pltpu.roll(low_tails, LANES - tail, 1)
    high_gate = pltpu.roll(high_tails, LANES - tail + heads, 1)
    gate_ref[...] = jnp.where(lane < heads, low_gate, high_gate)[:, : 2 * heads]


def attn_forward_kernel(cfg, traffic, me_ref, *refs):
    columns_first, heads, head_width = cfg
    shards, (w_ref, gb_ref, tap_ref) = refs[:8], refs[8:11]
    n_ref, proj_ref, log_ref, attn_ref, mix_ref, other_ref = refs[11:17]
    own_refs, total_ref = refs[17:21], refs[21]
    me = me_ref[0]
    wide = 2 * LANES
    gate_lane = heads * head_width - LANES
    spots = tail_spots(heads)
    mask = scan_mask(columns_first)
    column = grid_column()
    sets = lane_sets(wide, 0, head_width, heads)
    gather_pieces(me, shards, n_ref)
    traffic.flush(0)
    traffic.wait(9)
    for m in range(n_ref.shape[0]):
        projected = mm(n_ref[m], w_ref[:, : 4 * LANES])
        tails = mm(n_ref[m], w_ref[:, 5 * LANES :])
        logits = tails + gb_ref[...]
        log_ref[m] = logits
        decays, _ = decay_parts(logits, mask, gate_lane, heads)
        query, key, value, gate = (join_tail(projected, j, tails, spots[j]) for j in range(4))
        in_head = sets[0]
        for own in sets[1:]:
            in_head = in_head | own
        query, key, value = (jnp.where(in_head, v, 0.0).astype(BF16) for v in (query, key, value))
        gate = gate.astype(BF16)
        for j, v in enumerate((query, key, value, gate)):
            proj_ref[m, :, j * wide : (j + 1) * wide] = v
        attn = None
        for h in range(heads):
            w, mass = decays[h]
            raw = mm_nt(jnp.where(sets[h], query, jnp.zeros_like(query)), key)
            scores = (raw * head_width ** (-0.5) * w).astype(BF16)
            normed = mm(scores, value) * lax.rsqrt(mass)
            attn = jnp.where(sets[h], normed, 0.0 if attn is None else attn)
        attn_ref[m] = attn
        spread = convolve(side_shifts(attn, column), lambda i: tap_ref[i : i + 1, :])
        gate = gate.astype(F32)
        mixed = spread * (gate * jax.nn.sigmoid(gate))
        mixed = jnp.where(in_head, mixed, 0.0)
        mixed = jnp.concatenate(
            [mixed[:, :LANES], pltpu.roll(mixed[:, LANES:], spots[4], 1)], axis=1
        ).astype(BF16)
        mix_ref[m] = mixed
        if m == n_ref.shape[0] - 1:
            traffic.flush(1, 2, 3, 4)
        total_ref[m] = mm_nt(mixed, w_ref[:, 4 * LANES :]).astype(BF16)
    write_pieces(me, total_ref, other_ref, own_refs)


def attn_backward_kernel(cfg, traffic, me_ref, *refs):
    columns_first, heads, head_width = cfg
    shards, (proj_ref, log_ref, attn_ref, w_ref, tap_ref) = refs[:8], refs[8:13]
    g_ref, gproj_ref, gtap_ref, other_ref = refs[13:17]
    own_refs, total_ref = refs[17:21], refs[21]
    me = me_ref[0]
    wide = 2 * LANES
    gate_lane = heads * head_width - LANES
    spots = tail_spots(heads)
    scale = head_width ** (-0.5)
    mask = scan_mask(columns_first)
    column = grid_column()
    sets = lane_sets(wide, 0, head_width, heads)
    gate_sets = lane_sets(LANES, gate_lane, 1, heads)
    sublane = lax.broadcasted_iota(jnp.int32, (LANES, 1), 0)
    in_head = sets[0]
    for own in sets[1:]:
        in_head = in_head | own
    gather_pieces(me, shards, g_ref)
    gtap_ref[...] = jnp.zeros(gtap_ref.shape, F32)
    traffic.wait(9, 10, 11, 12)
    for m in range(g_ref.shape[0]):
        g_packed = mm(g_ref[m], w_ref[:, 4 * LANES :])
        g_mixed = jnp.where(in_head, join_tail(g_packed, 0, g_packed[:, LANES:], spots[4]), 0.0)
        query, key, value, gate = (proj_ref[m, :, j * wide : (j + 1) * wide] for j in range(4))
        gate = gate.astype(F32)
        sig = jax.nn.sigmoid(gate)
        attn = attn_ref[m]
        shifted = side_shifts(attn, column)
        spread = convolve(shifted, lambda i: tap_ref[i : i + 1, :])
        g_spread = g_mixed * (gate * sig)
        g_gate = g_mixed * spread * (sig * (1.0 + gate * (1.0 - sig)))
        for i, grad in enumerate(tap_grads(shifted, g_spread)):
            gtap_ref[i : i + 1, :] = grad if m == 0 else gtap_ref[i : i + 1, :] + grad
        g_attn = convolve(side_shifts(g_spread, column), lambda i: tap_ref[8 - i : 9 - i, :])
        logits = log_ref[m]
        decays, ones = decay_parts(logits, mask, gate_lane, heads)
        g_query = g_key = g_value = 0.0
        across = jnp.zeros((PATCHES, LANES), F32)
        down = jnp.zeros((LANES, PATCHES), F32)
        for h in range(heads):
            w, mass = decays[h]
            own_query = jnp.where(sets[h], query, jnp.zeros_like(query))
            raw = mm_nt(own_query, key) * scale
            own_grad = jnp.where(sets[h], g_attn, 0.0)
            g_mass = -0.5 * jnp.sum(own_grad * attn, axis=1, keepdims=True) / mass
            g_out = (own_grad * lax.rsqrt(mass)).astype(BF16)
            g_value = g_value + mm_tn((raw * w).astype(BF16), g_out)
            g_scores = mm_nt(g_out, value)
            g_raw = (g_scores * w * scale).astype(BF16)
            g_query = jnp.where(sets[h], mm(g_raw, key), g_query)
            g_key = g_key + mm_tn(g_raw, own_query)
            g_span = (g_scores * raw + g_mass) * w
            across = jnp.where(gate_sets[h], jnp.sum(g_span, axis=1, keepdims=True), across)
            down = jnp.where(sublane == gate_lane + h, rows_sum(g_span), down)
        g_rates = add_parts(mm_tn(ones, three_parts(across - down.T)))
        g_logits = (-g_rates * jax.nn.sigmoid(logits)).astype(BF16).astype(F32)
        g_bias = rows_sum(g_logits)
        gtap_ref[9:10, :LANES] = g_bias if m == 0 else gtap_ref[9:10, :LANES] + g_bias
        tails = g_logits
        for j, v in enumerate((g_query, g_key, g_value, g_gate)):
            gproj_ref[m, :, j * LANES : (j + 1) * LANES] = v[:, :LANES].astype(BF16)
            tails = tails + pltpu.roll(v[:, LANES:], spots[j], 1)
        gproj_ref[m, :, 4 * LANES :] = tails.astype(BF16)
        total = mm_nt(gproj_ref[m, :, : 4 * LANES], w_ref[:, : 4 * LANES])
        total = total + mm_nt(gproj_ref[m, :, 4 * LANES :], w_ref[:, 5 * LANES :])
        total_ref[m] = total.astype(BF16)
    write_pieces(me, total_ref, other_ref, own_refs)


def attn_weights_kernel(traffic, n_ref, gproj_ref, g_ref, mix_ref, gw_ref):
    traffic.wait(0, 3)
    for part in range(2):
        cols = slice(part * 2 * LANES, (part + 1) * 2 * LANES)
        total = mm_tn(n_ref[0], gproj_ref[0, :, cols])
        for m in range(1, n_ref.shape[0]):
            total = total + mm_tn(n_ref[m], gproj_ref[m, :, cols])
        gw_ref[:, cols] = total.astype(BF16)
    total = mm_tn(g_ref[0], mix_ref[0])
    tails = mm_tn(n_ref[0], gproj_ref[0, :, 4 * LANES :])
    for m in range(1, n_ref.shape[0]):
        total = total + mm_tn(g_ref[m], mix_ref[m])
        tails = tails + mm_tn(n_ref[m], gproj_ref[m, :, 4 * LANES :])
    gw_ref[:, 4 * LANES : 5 * LANES] = total[:, :LANES].astype(BF16)
    gw_ref[:, 5 * LANES :] = (total[:, LANES:] + tails).astype(BF16)


def stack_shards(shards, full_ref):
    for k, shard in enumerate(each_shard(shards)):
        images, rows, width = shard.shape
        full_ref[k * images * rows : (k + 1) * images * rows, :] = shard[...].reshape(
            images * rows, width
        )


def stack_kernel(traffic, *refs):
    stack_shards(refs[:8], refs[8])


def put_shard(k, value, shape, other_ref, own_refs):
    own, other = send_order(k)
    if own is None:
        other_ref[other] = value.astype(BF16).reshape(shape)
    else:
        own_refs[own][...] = value.astype(BF16).reshape(shape)


def put_shards(total, shape, other_ref, own_refs):
    rows = total.shape[0] // 8
    for k in range(8):
        put_shard(k, total[k * rows : (k + 1) * rows], shape, other_ref, own_refs)


def mlp_forward_kernel(left, traffic, *refs):
    shards, (w_ref, ub_ref) = refs[:8], refs[8:10]
    n_ref, pre_ref, hid_ref, other_ref = refs[10:14]
    own_refs = refs[14:18]
    main = (w_ref.shape[1] - LANES) // 2
    stack_shards(shards, n_ref)
    traffic.flush(0)
    traffic.wait(8)
    n = n_ref[...]
    pre = mm(n, w_ref[:, :main]) + ub_ref[:, :main]
    pre_ref[:, :main] = pre
    hidden = gelu_terms(pre)[0].astype(BF16)
    hid_ref[:, :main] = hidden
    last = mm(n, w_ref[:, 2 * main :]) + ub_ref[:, main:]
    pre_ref[:, main:] = last
    lane = lax.broadcasted_iota(jnp.int32, (1, LANES), 1)
    tail = jnp.where(lane < left, gelu_terms(last)[0], 0.0)
    tail = pltpu.roll(tail, LANES - left, 1).astype(BF16)
    hid_ref[:, main:] = tail
    traffic.flush(1, 2)
    total = mm_nt(hidden, w_ref[:, main : 2 * main]) + mm_nt(tail, w_ref[:, 2 * main :])
    put_shards(total, shards[0].shape, other_ref, own_refs)


def mlp_backward_kernel(left, traffic, *refs):
    given, (pre_ref, w_ref) = refs[:8], refs[8:10]
    g_ref, rest = refs[10], refs[11:]
    stack_shards(given, g_ref)
    traffic.wait(8, 9)
    gpre_ref, gub_ref, other_ref = rest[:3]
    own_refs = rest[3:]
    main = (w_ref.shape[1] - LANES) // 2
    g = g_ref[...]
    g_pre = mm(g, w_ref[:, main : 2 * main]) * gelu_terms(pre_ref[:, :main])[1]
    g_pre = g_pre.astype(BF16)
    gpre_ref[:, :main] = g_pre
    gub_ref[:, :main] = rows_sum(g_pre.astype(F32))
    lane = lax.broadcasted_iota(jnp.int32, (1, LANES), 1)
    last = pltpu.roll(mm(g, w_ref[:, 2 * main :]), left, 1) * gelu_terms(pre_ref[:, main:])[1]
    last = jnp.where(lane < left, last, 0.0).astype(BF16)
    gpre_ref[:, main:] = last
    gub_ref[:, main:] = rows_sum(last.astype(F32))
    total = mm_nt(g_pre, w_ref[:, :main]) + mm_nt(last, w_ref[:, 2 * main :])
    put_shards(total, own_refs[0].shape, other_ref, own_refs)


def mlp_both_kernel(left, traffic, *refs):
    shards, (raw_ref, w_ref, ub_ref, mod_ref), refs = refs[:8], refs[8:12], refs[12:]
    gw_ref, gub_ref, gate_ref, other_ref = refs[:4]
    own_refs, end_ref, end_refs = refs[4:8], refs[8], refs[9:13]
    g_ref, n_ref = refs[13:15]
    images, rows = own_refs[0].shape[:2]
    main = (w_ref.shape[1] - LANES) // 2
    lane = lax.broadcasted_iota(jnp.int32, (1, LANES), 1)
    spans = [(i % images, slice(i * rows, (i + 1) * rows)) for i in range(8 * images)]
    stack_shards(shards, n_ref)
    traffic.wait(8)
    for m, span in spans:
        g_ref[span] = (mod_ref[m, 5:6] * raw_ref[span].astype(F32)).astype(BF16)
    traffic.wait(9)
    n, g = n_ref[...], g_ref[...]
    value, slope = gelu_terms(mm(n, w_ref[:, :main]) + ub_ref[:, :main])
    hidden = value.astype(BF16)
    g_pre = (mm(g, w_ref[:, main : 2 * main]) * slope).astype(BF16)
    value, slope = gelu_terms(mm(n, w_ref[:, 2 * main :]) + ub_ref[:, main:])
    tail = pltpu.roll(jnp.where(lane < left, value, 0.0), LANES - left, 1).astype(BF16)
    last = pltpu.roll(mm(g, w_ref[:, 2 * main :]), left, 1) * slope
    last = jnp.where(lane < left, last, 0.0).astype(BF16)
    gw_ref[:, :main] = mm_tn(n, g_pre).astype(BF16)
    gw_ref[:, main : 2 * main] = mm_tn(g, hidden).astype(BF16)
    gw_ref[:, 2 * main :] = (mm_tn(n, last) + mm_tn(g, tail)).astype(BF16)
    traffic.flush(0)
    gub_ref[:, :main] = rows_sum(g_pre.astype(F32))
    gub_ref[:, main:] = rows_sum(last.astype(F32))
    total = mm_nt(hidden, w_ref[:, main : 2 * main]) + mm_nt(tail, w_ref[:, 2 * main :])
    put_shards(total, own_refs[0].shape, end_ref, end_refs)
    traffic.flush(8, 9, 10, 11, 12)
    gates = [0.0] * images
    for m, span in spans:
        gates[m] = gates[m] + rows_sum(raw_ref[span].astype(F32) * total[span])
    for m in range(images):
        gate_ref[m] = gates[m]
    total = mm_nt(g_pre, w_ref[:, :main]) + mm_nt(last, w_ref[:, 2 * main :])
    put_shards(total, own_refs[0].shape, other_ref, own_refs)


def mlp_weights_kernel(traffic, n_ref, gpre_ref, g_ref, hid_ref, gw_ref):
    main = gpre_ref.shape[1] - LANES
    traffic.wait(0, 3)
    gw_ref[:, :main] = mm_tn(n_ref[...], gpre_ref[:, :main]).astype(BF16)
    gw_ref[:, main : 2 * main] = mm_tn(g_ref[...], hid_ref[:, :main]).astype(BF16)
    last = mm_tn(n_ref[...], gpre_ref[:, main:]) + mm_tn(g_ref[...], hid_ref[:, main:])
    gw_ref[:, 2 * main :] = last.astype(BF16)


def swap(value, tensor_bits, section_bit):
    tensors, sections = lax.axis_size("tensor"), lax.axis_size("section")
    route = [
        (t * sections + s, (t ^ tensor_bits) * sections + (s ^ section_bit))
        for t in range(tensors)
        for s in range(sections)
    ]
    return lax.ppermute(value, PLANE, route)


def gather_plane(own):
    xy, x, y = swap(own, 2, 1), swap(own, 0, 1), swap(own, 2, 0)
    return own, x, y, xy, *(swap(v, 1, 0) for v in (own, x, y, xy))


def scatter_plane(other, own, late=False):
    received = swap(other, 1, 0)
    sums = call(
        add_late_kernel if late else add_kernel,
        (out(own[0].shape, BF16),) * 4,
        *own,
        received,
        streamed=(0, 1, 2, 3) if late else (),
    )
    return (sums[0], swap(sums[3], 2, 1), swap(sums[1], 0, 1), swap(sums[2], 2, 0))


def spread_over(value, axes):
    count = math.prod(lax.axis_size(a) for a in axes)
    copies = jnp.broadcast_to(value[None], (count,) + value.shape)
    return lax.all_to_all(copies, axes, split_axis=0, concat_axis=0, tiled=True)


def gather_all(own):
    return lax.all_gather(own, "dp", axis=0, tiled=True)


def scatter_rows(partial):
    return lax.psum_scatter(partial, "dp", scatter_dimension=0, tiled=True)


def sinusoid(time_steps, channels):
    half_width = channels // 2
    frequency = jnp.exp(
        jnp.arange(half_width, dtype=jnp.float32) * (-math.log(10000.0) / half_width)
    )
    angles = time_steps.astype(jnp.float32)[:, None] * frequency[None, :]
    return jnp.concatenate([jnp.cos(angles), jnp.sin(angles)], axis=1)


def per_device(
    section_inputs,
    condition,
    timesteps,
    ada_weight,
    ada_bias,
    in_weight,
    gate_weight,
    gate_bias,
    conv_taps,
    out_weight,
    up_weight,
    up_bias,
    down_weight,
):
    d = lax.axis_index("dp")
    t = lax.axis_index("tensor")
    s = lax.axis_index("section")
    dps, tensors, sections = (lax.axis_size(a) for a in ("dp", "tensor", "section"))
    first = s == 0
    me = (t * sections + s).astype(jnp.int32).reshape(1)
    images = condition.shape[0]
    width = condition.shape[1]
    slab = in_weight.shape[2]
    heads = gate_weight.shape[2] // sections
    channels = in_weight.shape[3] // sections
    head_width = channels // heads
    units = up_weight.shape[2] // sections
    wide = 2 * LANES
    tail = channels - LANES
    rows = section_inputs.shape[2] // sections
    main = units // LANES * LANES
    left = units - main
    spots = tail_spots(heads)

    def cut(value, axis):
        half = value.shape[axis] // 2
        return (
            lax.slice_in_dim(value, 0, half, axis=axis),
            lax.slice_in_dim(value, half, 2 * half, axis=axis),
        )

    def swap_halves(keep, send):
        received = lax.ppermute(send, "section", [(0, 1), (1, 0)])
        return jnp.where(first, keep, received), jnp.where(first, received, keep)

    def choose(pair):
        return jnp.where(first, pair[0], pair[1]), jnp.where(first, pair[1], pair[0])

    cfg = (heads, channels)
    section = s.astype(jnp.int32).reshape(1)
    shape_a, shape_b = (slab, 6 * LANES), (slab, 2 * main + LANES)
    kept_a, sent_a = call(
        functools.partial(pack_attn_kernel, cfg),
        (out(shape_a, BF16),) * 2,
        section,
        in_weight[0],
        jnp.pad(gate_weight[0].astype(F32), ((0, 0), (0, LANES - gate_weight.shape[2]))),
        out_weight[0].T,
        scalars=1,
        streamed=(1,),
    )
    sent_a, condition, down_in = lax.optimization_barrier((sent_a, condition, down_weight[0]))
    received_a = lax.ppermute(sent_a, "section", [(0, 1), (1, 0)])
    kept_b, sent_b = call(
        functools.partial(pack_mlp_kernel, left),
        (out(shape_b, BF16),) * 2,
        section,
        up_weight[0],
        down_in.T,
        scalars=1,
        streamed=(1,),
    )
    received_b = lax.ppermute(sent_b, "section", [(0, 1), (1, 0)])

    def unit_halves(value):
        rest = sections * main
        return tuple(
            (value[:, h * main : (h + 1) * main], value[:, rest + h * left : rest + (h + 1) * left])
            for h in (0, 1)
        )

    def pack_small(gate_half, taps_half, up_half):
        return jnp.concatenate([gate_half.reshape(-1), taps_half.reshape(-1), up_half.reshape(-1)])

    def pack_halves(pack, *pairs):
        return tuple(pack(*(pair[i] for pair in pairs)) for i in (0, 1))

    x_pair = cut(section_inputs[0], 1)
    x_received = lax.ppermute(
        jnp.where(first, x_pair[1], x_pair[0]), "section", [(0, 1), (1, 0)]
    )
    x0 = jnp.where(first, x_pair[0], x_received)
    g1 = jnp.where(first, x_received, x_pair[1])
    taps_count = conv_taps.shape[1]
    up_row = up_bias[0].astype(F32)[None]
    small = swap_halves(
        *choose(
            pack_halves(
                pack_small,
                cut(gate_bias[0].astype(F32), 0),
                cut(conv_taps[0].astype(F32), 1),
                tuple(jnp.concatenate(v, axis=1) for v in unit_halves(up_row)),
            )
        )
    )

    def unpack_small(packed):
        gate_row = jnp.pad(packed[:heads][None], ((0, 0), (tail, LANES - heads - tail)))
        taps = packed[heads : heads + taps_count * channels].reshape(taps_count, channels)
        taps = jnp.pad(taps, ((0, 16 - taps_count), (0, wide - channels)))
        up_row = packed[heads + taps_count * channels :][None]
        return gate_row, taps, jnp.pad(up_row, ((0, 0), (0, main + LANES - units)))

    cond_vec = condition + sinusoid(timesteps, width)
    activated = jax.nn.silu(cond_vec).astype(BF16)
    slab_active = activated.reshape(images, dps, slab).transpose(1, 0, 2)
    slab_active = lax.all_to_all(slab_active, "dp", split_axis=0, concat_axis=0, tiled=True)
    slab_active = slab_active.reshape(dps * images, slab)
    slab_active, received_a = lax.optimization_barrier((slab_active, received_a))
    mod_part = jnp.dot(slab_active, ada_weight[0], preferred_element_type=F32)
    mod_parts = lax.all_to_all(
        mod_part.reshape(dps, images, -1), "dp", split_axis=0, concat_axis=0, tiled=True
    )
    mod_share = jnp.sum(mod_parts, axis=0) + ada_bias[0].astype(F32)
    mod_all = spread_over(mod_share, ("section", "tensor"))
    received_b, mod_all = lax.optimization_barrier((received_b, mod_all))
    mod_all = mod_all.reshape(sections, tensors, images, -1).transpose(0, 2, 1, 3)
    mod_all = mod_all.reshape(sections, images, 6, width)
    mods = (mod_all[0], mod_all[1])

    shard = out((images, rows, width), BF16)
    shard_wide = out((images, rows, width), F32)
    vector = out((images, 1, width), F32)
    pieces_out = (out((4, images, rows, width), BF16),) + (shard,) * 4
    full = out((images, PATCHES, width), BF16)
    flat = out((images * PATCHES, width), BF16)
    total_rows = images * PATCHES
    kept = pltpu.VMEM((images, PATCHES, width), BF16)
    middle_flops = 2 * total_rows * PATCHES * wide * heads * 6
    attn_flops = 2 * total_rows * width * wide * 5 + middle_flops
    mlp_flops = 4 * total_rows * width * units

    def attn_forward(b, shards):
        w, _, gate_row, taps, _ = weights[b]
        body = functools.partial(attn_forward_kernel, (b == 1, heads, head_width))
        found = call(
            body,
            (
                full,
                out((images, PATCHES, 4 * wide), BF16),
                out((images, PATCHES, LANES), F32),
                out((images, PATCHES, wide), F32),
                out((images, PATCHES, wide), BF16),
                *pieces_out,
            ),
            me,
            *shards,
            w,
            gate_row,
            taps,
            scalars=1,
            flops=attn_flops,
            scratch=[kept],
            streamed=(9,),
            saved=(0, 1, 2, 3, 4),
        )
        return found[:5], scatter_plane(found[5], found[6:])

    def attn_backward(b, shards, saved, after=()):
        w, _, _, taps, _ = weights[b]
        body = functools.partial(attn_backward_kernel, (b == 1, heads, head_width))
        found = call(
            body,
            (
                full,
                out((images, PATCHES, 5 * LANES), BF16),
                out((16, wide), F32),
                *pieces_out,
            ),
            me,
            *shards,
            saved[1],
            saved[2],
            saved[3],
            w,
            taps,
            scalars=1,
            flops=2 * attn_flops,
            scratch=[kept],
            streamed=(9, 10, 11, 12),
            after=after,
        )
        terms = scatter_plane(found[3], found[4:])
        (grads,) = call(
            attn_weights_kernel,
            (out((width, 6 * LANES), BF16),),
            saved[0],
            found[1],
            found[0],
            saved[4],
            flops=2 * total_rows * width * wide * 5,
            after=terms if b else (),
            streamed=(0, 3),
            saved=(0,),
        )
        return terms, grads, found[2]

    def mlp_forward(b, normed):
        _, w, _, _, up_row = weights[b]
        found = call(
            functools.partial(mlp_forward_kernel, left),
            (
                flat,
                out((total_rows, main + LANES), F32),
                out((total_rows, main + LANES), BF16),
                *pieces_out,
            ),
            *gather_plane(normed),
            w,
            up_row,
            flops=mlp_flops,
            streamed=(8,),
            saved=(0, 1, 2),
        )
        return found[:3], scatter_plane(found[3], found[4:])

    shape_gw = out((width, 2 * main + LANES), BF16)
    shape_gub = out((1, main + LANES), F32)

    def mlp_both(b, shards, gradient):
        _, w, _, _, up_row = weights[b]
        found = call(
            functools.partial(mlp_both_kernel, left),
            (shape_gw, shape_gub, vector, *pieces_out, *pieces_out),
            *shards,
            gradient,
            w,
            up_row,
            mods[b],
            flops=3 * mlp_flops,
            scratch=[pltpu.VMEM(flat.shape, flat.dtype)] * 2,
            streamed=(8, 9),
            saved=(0, 8, 9, 10, 11, 12),
        )
        return scatter_plane(found[3], found[4:8]), found[0], found[1], found[2], found[8:]

    def mlp_backward(b, given, saved, after=()):
        _, w, _, _, _ = weights[b]
        found = call(
            functools.partial(mlp_backward_kernel, left),
            (flat, out((total_rows, main + LANES), BF16), shape_gub, *pieces_out),
            *given,
            saved[1],
            w,
            flops=mlp_flops,
            streamed=(8, 9),
            after=after,
        )
        terms = scatter_plane(found[3], found[4:])
        (grads,) = call(
            mlp_weights_kernel,
            (shape_gw,),
            saved[0],
            found[1],
            found[0],
            saved[2],
            flops=mlp_flops,
            after=terms,
            streamed=(0, 3),
            saved=(0,),
        )
        return terms, grads, found[2]

    def of_block(b, kept, received):
        return jnp.where(first == (b == 0), kept, received)

    full_a0 = gather_all(of_block(0, kept_a, received_a))
    middle = [of_block(0, kept_b, received_b), of_block(1, kept_a, received_a)]
    full_middle = gather_all(jnp.concatenate(middle, axis=1))
    full_b0 = Columns(full_middle, 0, middle[0].shape[1])
    full_a1 = Columns(full_middle, middle[0].shape[1], middle[1].shape[1])
    (g1_all,) = call(stack_kernel, (flat,), *gather_plane(g1), saved=(0,))
    (normed,) = call(start_kernel, (shard,), x0, mods[0])
    shards, g1_all, next_b = lax.optimization_barrier(
        (
            gather_plane(normed),
            g1_all,
            of_block(1, kept_b, received_b),
        )
    )
    weights = [
        (full_a0, full_b0, *unpack_small(small[0])),
        (full_a1, gather_all(next_b), *unpack_small(small[1])),
    ]

    def to_second(value):
        return lax.ppermute(value, "section", [(0, 1)])

    def to_first(value):
        return lax.ppermute(value, "section", [(1, 0)])

    attn0, terms = attn_forward(0, shards)
    att0, aft0, normed = call(
        after_attn_kernel, (shard_wide, shard_wide, shard), *terms, x0, mods[0], saved=(0, 1)
    )
    mlp0, terms = mlp_forward(0, normed)
    mlp_out0, x1, normed = call(
        between_kernel,
        (shard_wide, shard, shard),
        *terms,
        aft0,
        mods[0],
        mods[1],
        saved=(0, 1),
    )
    attn1, terms = attn_forward(1, gather_plane(normed))
    att1, aft1, normed = call(
        after_attn_kernel, (shard_wide, shard_wide, shard), *terms, x1, mods[1], saved=(0, 1)
    )

    three, six = (out((images, n, width), F32) for n in (3, 6))
    terms, mlp_grads1, g_up_bias1, g_gate_two1, end_pieces = mlp_both(1, gather_plane(normed), g1_all)
    g_after, g_attn, g_some = call(
        back_mlp_rows_kernel,
        (shard_wide, shard, three),
        *terms,
        g1,
        aft1,
        att1,
        mods[1],
        saved=(0,),
    )
    sum_b1 = scatter_rows(mlp_grads1)
    terms, attn_grads1, g_taps1 = attn_backward(1, gather_plane(g_attn), attn1)
    g0, g_mlp, g_mods1, g_gate_two0 = call(
        back_between_kernel,
        (shard, shard, six, vector),
        *terms,
        g_after,
        x1,
        mods[1],
        g_some,
        g_gate_two1,
        mods[0],
        mlp_out0,
    )
    sum_a1 = scatter_rows(attn_grads1)
    terms, mlp_grads0, g_up_bias0 = mlp_backward(0, gather_plane(g_mlp), mlp0, (attn_grads1,))
    g_after, g_attn, g_some = call(
        back_mlp_rows_kernel,
        (shard_wide, shard, three),
        *terms,
        g0,
        aft0,
        att0,
        mods[0],
        after=(sum_b1,),
        saved=(0,),
    )
    terms, attn_grads0, g_taps0 = attn_backward(0, gather_plane(g_attn), attn0, (mlp_grads0,))
    g_in, g_mods0 = call(
        back_end_kernel,
        (shard, six),
        *terms,
        g_after,
        x0,
        mods[0],
        g_some,
        g_gate_two0,
        after=(attn_grads0,),
    )

    sum_b0, sum_a0 = scatter_rows(mlp_grads0), scatter_rows(attn_grads0)

    g_mod = jnp.stack([g_mods0.reshape(images, -1), g_mods1.reshape(images, -1)])
    g_mod = g_mod.reshape(sections, images, tensors, -1).transpose(0, 2, 1, 3)
    columns = g_mod.shape[3]
    g_mod = g_mod.reshape(sections, tensors, images * columns)
    taps_rows = taps_count + 1

    def small_grads(g_taps, g_up_bias):
        return jnp.concatenate([g_taps[:taps_rows].reshape(-1), g_up_bias.reshape(-1)])

    g_small = jnp.stack([small_grads(g_taps0, g_up_bias0), small_grads(g_taps1, g_up_bias1)])
    to_tensor = (jnp.arange(tensors) == t)[None, :, None]
    g_small = jnp.where(to_tensor, g_small[:, None], 0.0)
    g_sent = jnp.concatenate([g_mod, g_small], axis=2).reshape(sections * tensors, -1)
    g_parts = lax.all_to_all(
        g_sent, ("section", "tensor"), split_axis=0, concat_axis=0, tiled=True
    )
    g_parts, sum_b1, sum_a1 = lax.optimization_barrier((g_parts, sum_b1, sum_a1))
    other_b1, other_a1 = to_second(sum_b1), to_second(sum_a1)
    g_share = jnp.sum(g_parts[:, : images * columns], axis=0)
    small_parts = g_parts[:, images * columns :].reshape(sections, tensors, -1).sum(1)
    g_all = spread_over(jnp.concatenate([g_share, small_parts.reshape(-1)]), ("dp",))
    g_all, end_pieces, sum_b0 = lax.optimization_barrier((g_all, end_pieces, sum_b0))
    others = other_b1, other_a1, to_first(sum_b0)
    (block_out,) = call(
        end_kernel, (shard,), *scatter_plane(end_pieces[0], end_pieces[1:], True), aft1, mods[1]
    )
    small_own = jnp.sum(g_all[:, images * columns :], axis=0).reshape(sections, -1)
    g_all = g_all[:, : images * columns].reshape(dps * images, columns).astype(BF16)
    grad_ada_bias = jnp.sum(g_all.astype(F32), axis=0)
    act_part = jnp.einsum("me,de->md", g_all, ada_weight[0], preferred_element_type=F32)
    act_part, other_b1 = lax.optimization_barrier((act_part, others[0]))
    others = other_b1, *others[1:]
    plane = sections * tensors
    act_sent = jnp.broadcast_to(
        act_part.reshape(dps, 1, images, slab), (dps, plane, images, slab)
    )
    act_all = lax.all_to_all(
        act_sent.reshape(-1, images, slab),
        ("dp", "section", "tensor"),
        split_axis=0,
        concat_axis=0,
        tiled=True,
    )
    act_all, other_b0 = lax.optimization_barrier((act_all, others[2]))
    others = *others[:2], other_b0
    act_all = jnp.sum(act_all.reshape(dps, plane, images, slab), axis=1)
    act_grad = act_all.reshape(dps, images, slab).transpose(1, 0, 2).reshape(images, width)
    cond_grad = jax.vjp(jax.nn.silu, cond_vec)[1](act_grad)[0]

    ends_from_first = lax.ppermute(block_out, "section", [(0, 1)])
    ends_from_second = lax.ppermute(g_in, "section", [(1, 0)])
    mine = jnp.where(first, g_in, block_out)
    received = jnp.where(first, ends_from_second, ends_from_first)
    section_ends = jnp.concatenate(
        [jnp.where(first, mine, received), jnp.where(first, received, mine)], axis=1
    )
    cond_grad, section_ends, sum_a0, g_all, others = lax.optimization_barrier(
        (cond_grad, section_ends, sum_a0, g_all, others)
    )
    other_b1, other_a1, other_b0 = others
    other_a0 = to_first(sum_a0)
    grad_ada = jnp.einsum("md,me->de", slab_active, g_all, preferred_element_type=F32)

    small_taps = small_own[:, : taps_rows * wide].reshape(sections, taps_rows, wide)
    grad_gateb = small_taps[:, taps_count, tail : tail + heads].reshape(-1)
    grad_taps = small_taps[:, :taps_count, :channels].transpose(1, 0, 2)
    grad_taps = grad_taps.reshape(taps_count, sections * channels)
    up_halves = small_own[:, taps_rows * wide :]
    grad_up_bias = jnp.concatenate(
        [up_halves[:, :main].reshape(-1), up_halves[:, main : main + left].reshape(-1)]
    )

    grad_up, grad_down = call(
        functools.partial(unpack_mlp_kernel, left),
        (out(up_weight.shape[1:], F32),) * 2,
        section,
        sum_b0,
        other_b0,
        sum_b1,
        other_b1,
        scalars=1,
    )
    grad_down = grad_down.T
    grad_in, grad_gate, grad_out = call(
        functools.partial(unpack_attn_kernel, cfg),
        (
            out(in_weight.shape[1:], F32),
            out(gate_weight.shape[1:], F32),
            out((slab, out_weight.shape[1]), F32),
        ),
        section,
        sum_a0,
        other_a0,
        sum_a1,
        other_a1,
        scalars=1,
    )
    grad_out = grad_out.T

    return (
        section_ends[None],
        cond_grad,
        grad_ada[None],
        grad_ada_bias[None],
        grad_in[None],
        grad_gate[None],
        grad_gateb[None],
        grad_taps[None],
        grad_out[None],
        grad_up[None],
        grad_up_bias[None],
        grad_down[None],
    )


def solution(mesh):
    in_specs = (
        P("section", "dp", "tensor", None),
        P("dp", None),
        P("dp"),
        P("section", "dp", "tensor"),
        P("section", "tensor"),
        P("section", None, "dp", "tensor"),
        P("section", "dp", "tensor"),
        P("section", "tensor"),
        P("section", None, "tensor"),
        P("section", "tensor", "dp"),
        P("section", "dp", "tensor"),
        P("section", "tensor"),
        P("section", "tensor", "dp"),
    )
    out_specs = (
        P("section", "dp", "tensor", None),
        P("dp", None),
        P("section", "dp", "tensor"),
        P("section", "tensor"),
        P("section", None, "dp", "tensor"),
        P("section", "dp", "tensor"),
        P("section", "tensor"),
        P("section", None, "tensor"),
        P("section", "tensor", "dp"),
        P("section", "dp", "tensor"),
        P("section", "tensor"),
        P("section", "tensor", "dp"),
    )
    return jax.shard_map(
        per_device, mesh=mesh, in_specs=in_specs, out_specs=out_specs, check_vma=False
    )
```
